128 devices in a mesh: dp: 8 (over y, core), fsdp: 16 (over z, x).
Axes of the slice: x: 4, y: 4, z: 4, core: 2. Of those that a mesh axis runs over, the one named last changes fastest.
Arguments:
- tokens: bfloat16 [100352, 768], P(('dp', 'fsdp')), may hold values from -6 to 6
- keep_mask: int32 [512, 196], P(('dp', 'fsdp')), may hold values from 0 to 1, as said below
- pairing: int32 [512], replicated, may hold values from 0 to 511, each once
- text_vectors: float32 [512, 512], P(('dp', 'fsdp')), may hold values from -6 to 6
- logit_scale: float32 [1], replicated, may hold values from 3 to 3.8
- w_qkv: float32 [768, 2304], P(('dp', 'fsdp')), may hold values from -0.21875 to 0.21875
- w_out: float32 [768, 768], P(('dp', 'fsdp')), may hold values from -1.75 to 1.75
- w_up: float32 [768, 3072], P(('dp', 'fsdp')), may hold values from -0.21875 to 0.21875
- w_down: float32 [3072, 768], P(('dp', 'fsdp')), may hold values from -0.109375 to 0.109375
- w_proj: float32 [768, 512], P(('dp', 'fsdp')), may hold values from -0.21875 to 0.21875
- gain_one: float32 [768], P(('dp', 'fsdp')), may hold values from 0.25 to 1.75
- shift_one: float32 [768], P(('dp', 'fsdp')), may hold values from -1.5 to 1.5
- gain_two: float32 [768], P(('dp', 'fsdp')), may hold values from 0.25 to 1.75
- shift_two: float32 [768], P(('dp', 'fsdp')), may hold values from -1.5 to 1.5
- gain_post: float32 [768], P(('dp', 'fsdp')), may hold values from 0.25 to 1.75
- shift_post: float32 [768], P(('dp', 'fsdp')), may hold values from -1.5 to 1.5
- pool_query: float32 [768], P(('dp', 'fsdp')), may hold values from -10 to 10
Outputs:
- loss_value: float32 [1], replicated
- grad_tokens: float32 [100352, 768], P(('dp', 'fsdp'))
- grad_text: float32 [512, 512], P(('dp', 'fsdp'))
- grad_qkv: float32 [768, 2304], P(('dp', 'fsdp'))
- grad_out: float32 [768, 768], P(('dp', 'fsdp'))
- grad_up: float32 [768, 3072], P(('dp', 'fsdp'))
- grad_down: float32 [3072, 768], P(('dp', 'fsdp'))
- grad_proj: float32 [768, 512], P(('dp', 'fsdp'))
- grad_gain_one: float32 [768], P(('dp', 'fsdp'))
- grad_shift_one: float32 [768], P(('dp', 'fsdp'))
- grad_gain_two: float32 [768], P(('dp', 'fsdp'))
- grad_shift_two: float32 [768], P(('dp', 'fsdp'))
- grad_gain_post: float32 [768], P(('dp', 'fsdp'))
- grad_shift_post: float32 [768], P(('dp', 'fsdp'))
- grad_query: float32 [768], P(('dp', 'fsdp'))
- grad_scale: float32 [1], replicated
The draws below stay inside these ranges and needn't reach their ends.
Inputs may be any that keep to these rules, and one draw needn't show every extreme that they name: `keep_mask`: each image keeps between 32 and 196 patches; some image keeps all 196 and some exactly 32. `pairing`: each text row belongs to exactly one image.
All inputs are finite; a program needn't handle non-finite values.
Results may differ from the reference program's by a relative error of at most 0.022.
Values may be sent and summed in bfloat16 or wider, within the bound.
A program may use at most 192 MiB of HBM per device.

```python
import math
import jax
import jax.numpy as jnp
from jax import lax

D = 768
HEADS = 12
HDIM = 64
FF = 3072
E = 512
PATCH = 196
KEEP_MIN = 32
IMAGES = 512
TOKENS = 100352


def draw_keep_mask(key, part):
    key = jax.random.fold_in(key, 5)
    count_key, order_key = jax.random.split(key)
    counts = jax.random.randint(count_key, (IMAGES,), KEEP_MIN, PATCH + 1)
    counts = counts.at[0].set(PATCH).at[IMAGES - 1].set(KEEP_MIN)
    order_keys = jax.random.split(order_key, IMAGES)
    ranks = jax.vmap(jax.random.permutation, in_axes=(0, None))(order_keys, PATCH)
    return (ranks < counts[:, None]).astype(jnp.int32)


def block_levels(stream_key, extent, cuts, smallest, high):
    loudness = 1.0
    for axis_at, shards_of in cuts:
        draws = jax.random.uniform(jax.random.fold_in(jax.random.fold_in(stream_key, 6), axis_at), (shards_of,), jnp.float32, smallest / len(cuts), high / len(cuts))
        loudness = loudness * jnp.repeat(jnp.exp(draws), extent[axis_at] // shards_of).reshape((-1,) + (1,) * (len(extent) - 1 - axis_at))
    return loudness


def gaussian(stream_key, dims, scale, reach, shards=(), kind=jnp.bfloat16):
    drawn = jax.random.normal(stream_key, dims, jnp.float32) * scale
    if len(shards) > 0:
        drawn = block_levels(stream_key, dims, shards, -0.22, 0.18) * drawn
    return jnp.clip(drawn, min=-reach, max=reach).astype(kind)


def setup_inputs(seed: int = 0) -> dict:
    keys = jax.random.split(jax.random.key(seed), 18)
    return {
        "tokens": gaussian(keys[0], (TOKENS, D), 1.0, 6.0, ((0, 128),)),
        "keep_mask": draw_keep_mask(jax.random.fold_in(keys[17], 71), 0),
        "pairing": jax.random.permutation(keys[2], IMAGES).astype(jnp.int32),
        "text_vectors": gaussian(keys[3], (IMAGES, E), 1.0, 6.0, ((0, 128),), jnp.float32),
        "logit_scale": jnp.clip(jax.random.uniform(keys[4], (1,), jnp.float32, 3.0, 3.8), 3.0, 3.8),
        "w_qkv": gaussian(keys[5], (D, 3 * D), D ** -0.5, 0.21875, ((0, 128),), jnp.float32),
        "w_out": gaussian(keys[6], (D, D), (D // 64) ** -0.5, 1.75, ((0, 128),), jnp.float32),
        "w_up": gaussian(keys[7], (D, FF), D ** -0.5, 0.21875, ((0, 128),), jnp.float32),
        "w_down": gaussian(keys[8], (FF, D), FF ** -0.5, 0.109375, ((0, 128),), jnp.float32),
        "w_proj": gaussian(keys[9], (D, E), D ** -0.5, 0.21875, ((0, 128),), jnp.float32),
        "gain_one": jnp.clip(1.0 + 0.15 * jax.random.normal(keys[10], (D,), jnp.float32), 0.25, 1.75),
        "shift_one": gaussian(keys[11], (D,), 0.3, 1.5, ((0, 128),), jnp.float32),
        "gain_two": jnp.clip(1.0 + 0.15 * jax.random.normal(keys[12], (D,), jnp.float32), 0.25, 1.75),
        "shift_two": gaussian(keys[13], (D,), 0.3, 1.5, ((0, 128),), jnp.float32),
        "gain_post": jnp.clip(1.0 + 0.15 * jax.random.normal(keys[14], (D,), jnp.float32), 0.25, 1.75),
        "shift_post": gaussian(keys[15], (D,), 0.3, 1.5, ((0, 128),), jnp.float32),
        "pool_query": gaussian(keys[16], (D,), 2.0, 10.0, ((0, 128),), jnp.float32),
    }


@jax.custom_vjp
def low(v):
    return lax.optimization_barrier(v.astype(jnp.bfloat16)).astype(jnp.float32)

@jax.custom_vjp
def low_back(v):
    return v

def low_keep(v):
    return (low(v), None)

def low_pass(kept, grad):
    return (grad,)

def back_keep(v):
    return (v, None)

def back_low(kept, grad):
    return (low(grad),)
low.defvjp(low_keep, low_pass)
low_back.defvjp(back_keep, back_low)

def norm_rows(values, norm_gain, norm_shift):
    center = lax.optimization_barrier(jnp.mean(values, axis=-1, keepdims=True))
    centred = values - center
    spread = lax.optimization_barrier(jnp.mean(centred * centred, axis=-1, keepdims=True))
    return centred * lax.rsqrt(spread + 1e-05) * norm_gain + norm_shift

def unit_rows(values):
    row_total = lax.optimization_barrier(jnp.sum(values * values, axis=-1, keepdims=True)) + 1e-06
    return values * lax.rsqrt(row_total)

def pooled_rows(residual_two, norm_gain, norm_shift, query_vec, kept_mask):
    images_here, patches = kept_mask.shape
    final = norm_rows(residual_two, norm_gain, norm_shift).reshape(images_here, patches, -1)
    pool_logits = lax.optimization_barrier(jnp.sum(final * query_vec, axis=-1)) / math.sqrt(final.shape[-1])
    pool_logits = jnp.where(kept_mask > 0, pool_logits, -1e+30)
    shares = jax.nn.softmax(pool_logits, axis=-1)
    return lax.optimization_barrier(jnp.sum(shares[:, :, None] * final, axis=1))

def head_loss(image_rows, text_rows, scale_log, pairing):
    total_rows = image_rows.shape[0]
    logits = jnp.exp(scale_log[0]) * jnp.dot(image_rows, text_rows.T, precision=lax.Precision.HIGHEST)
    target = (pairing[:, None] == jnp.arange(total_rows, dtype=jnp.int32)[None, :]).astype(logits.dtype)
    row_totals = jax.nn.logsumexp(logits, axis=1)
    col_totals = jax.nn.logsumexp(logits, axis=0)
    matched = jnp.sum(logits * target)
    return (jnp.sum(row_totals) + jnp.sum(col_totals) - 2.0 * matched) / (2.0 * total_rows)

def encode_group(tokens_block, kept_mask, params):
    w_qkv, w_out, w_up, w_down, w_proj, gain_one, shift_one, gain_two, shift_two, gain_post, shift_post, pool_query = params
    images_here, patches = kept_mask.shape
    exact_mode = lax.Precision.HIGHEST
    normed = low(norm_rows(tokens_block, gain_one, shift_one))
    mixed = low(low_back(jnp.dot(normed, w_qkv, precision=exact_mode)))
    mixed = mixed.reshape(images_here, patches, 3, HEADS, HDIM)
    queries = mixed[:, :, 0]
    key_rows = mixed[:, :, 1]
    values = mixed[:, :, 2]
    scores = low_back(jnp.einsum('bqhd,bkhd->bhqk', queries, key_rows, precision=exact_mode) * HDIM ** (-0.5))
    scores = jnp.where((kept_mask > 0)[:, None, None, :], scores, -1e+30)
    softmaxed = low(jax.nn.softmax(scores, axis=-1))
    attended = low(low_back(jnp.einsum('bhqk,bkhd->bqhd', softmaxed, values, precision=exact_mode)))
    attended = attended.reshape(images_here * patches, HEADS * HDIM)
    residual_one = tokens_block + low_back(jnp.dot(attended, w_out, precision=exact_mode))
    normed_two = low(norm_rows(residual_one, gain_two, shift_two))
    upward = low_back(jnp.dot(normed_two, w_up, precision=exact_mode))
    active = low(jax.nn.gelu(upward, approximate=False))
    residual_two = residual_one + low_back(jnp.dot(active, w_down, precision=exact_mode))
    pooled = low(pooled_rows(residual_two, gain_post, shift_post, pool_query, kept_mask))
    embedded = low_back(jnp.dot(pooled, w_proj, precision=exact_mode))
    return low(unit_rows(embedded))

def total_loss(inputs, masters, text_rows, scale_log, keep_mask, pairing):
    params = tuple((low(master) for master in masters))
    images = keep_mask.shape[0]
    group_size = 16 if images % 16 == 0 else 1

    def encode_block(pair_block):
        return encode_group(pair_block[0], pair_block[1], params)
    blocks = (inputs.reshape(images // group_size, group_size * PATCH, D), keep_mask.reshape(images // group_size, group_size, PATCH))
    unit_image = lax.map(jax.checkpoint(encode_block), blocks).reshape(images, E)
    unit_text = low(unit_rows(text_rows))
    return head_loss(unit_image, unit_text, scale_log, pairing)

def reference(tokens, keep_mask, pairing, text_vectors, logit_scale, w_qkv, w_out, w_up, w_down, w_proj, gain_one, shift_one, gain_two, shift_two, gain_post, shift_post, pool_query):
    masters = (w_qkv, w_out, w_up, w_down, w_proj, gain_one, shift_one, gain_two, shift_two, gain_post, shift_post, pool_query)

    def objective(inputs, master_set, text_rows, scale_log):
        return total_loss(inputs, master_set, text_rows, scale_log, keep_mask, pairing)
    loss_value, pull_back = jax.vjp(objective, tokens.astype(jnp.float32), masters, text_vectors, logit_scale)
    grad_tokens, grad_masters, grad_text, grad_scale = pull_back(jnp.ones_like(loss_value))
    return (loss_value.reshape(1), grad_tokens, grad_text, grad_masters[0], grad_masters[1], grad_masters[2], grad_masters[3], grad_masters[4], grad_masters[5], grad_masters[6], grad_masters[7], grad_masters[8], grad_masters[9], grad_masters[10], grad_masters[11], grad_scale)
```

```python
from functools import partial
import math

import jax
import jax.numpy as jnp
from jax import lax
from jax.experimental import pallas as pl
from jax.experimental.pallas import tpu as pltpu
from jax.sharding import PartitionSpec as P

MESH = pl.DeviceIdType.MESH
BF = jnp.bfloat16
F32 = jnp.float32


class Place:
    def __init__(self):
        dp = lax.axis_index("dp")
        fs = lax.axis_index("fsdp")
        self.y, self.core = dp // 2, dp % 2
        self.z, self.x = fs // 4, fs % 4
        self.dp, self.fs = dp, fs

    def dev(self, **moved):
        at = dict(x=self.x, y=self.y, z=self.z, core=self.core)
        at.update(moved)
        return (at["y"] * 2 + at["core"], at["z"] * 4 + at["x"])

    def hop(self, dim, step):
        return self.dev(**{dim: (getattr(self, dim) + step + 4) % 4})

    def sibling(self):
        return self.dev(core=1 - self.core)


class Link:
    def __init__(self, send, recv, local=None):
        self.send, self.recv, self.n = send, recv, 0
        self.open = []

    def copy(self, src, dst, dev):
        k = self.n
        self.n += 1
        c = pltpu.make_async_remote_copy(
            src_ref=src,
            dst_ref=dst,
            send_sem=self.send.at[k],
            recv_sem=self.recv.at[k],
            device_id=dev,
            device_id_type=MESH,
        )
        c.start()
        self.open.append(c)
        return c

    def drain(self):
        for c in self.open:
            c.wait_send()
        self.open = []


ORDERS = (("x", "y", "z"), ("y", "z", "x"), ("z", "x", "y"))


def enter(me):
    sem = pltpu.get_barrier_semaphore()
    peers = []
    s = (me.z % 2) * 4 + me.x
    for k in range(1, 8):
        t = (s + k) % 8
        peers.append(me.dev(z=(me.z // 2) * 2 + t // 4, x=t % 4))
    v = me.dp * 2 + me.z // 2
    for k in range(1, 16):
        t = (v + k) % 16
        peers.append((t // 2, ((t % 2) * 2 + me.z % 2) * 4 + me.x))
    other = jnp.where(me.z % 2 == 0, (me.z + 3) % 4, (me.z + 1) % 4)
    peers.append(me.dev(z=other))
    for p in peers:
        pl.semaphore_signal(sem, inc=1, device_id=p, device_id_type=MESH)
    pl.semaphore_wait(sem, len(peers))


def half(ref, rows, which):
    if rows is None:
        return ref.at[pl.ds(2 * which, 2)]
    cut = rows // 32 * 16 if rows % 32 == 0 else rows // 32 * 32
    return ref.at[pl.ds(0, cut)] if which == 0 else ref.at[pl.ds(cut, rows - cut)]


def gather_steps(me, link, buf, order, rows):
    mine = buf.at[me.core]
    at = [getattr(me, d) for d in order]
    for stage in range(3):
        i, d = at[stage], order[stage]

        def block(b, stage=stage):
            if stage == 0:
                return mine.at[at[2], at[1], b]
            if stage == 1:
                return mine.at[at[2], b]
            return mine.at[b]

        r = rows if stage == 0 else None
        lo, hi, far = (i + 3) % 4, (i + 1) % 4, (i + 2) % 4
        right, left = me.hop(d, 1), me.hop(d, -1)
        cr = link.copy(block(i), block(i), right)
        cl = link.copy(block(i), block(i), left)
        sib = []
        if stage == 2:
            sib.append(link.copy(block(i), block(i), me.sibling()))
        yield
        cr.wait_recv()
        fr = link.copy(half(block(lo), r, 0), half(block(lo), r, 0), right)
        if stage == 2:
            sib.append(link.copy(block(lo), block(lo), me.sibling()))
        cl.wait_recv()
        fl = link.copy(half(block(hi), r, 1), half(block(hi), r, 1), left)
        if stage == 2:
            sib.append(link.copy(block(hi), block(hi), me.sibling()))
        yield
        fr.wait_recv()
        fl.wait_recv()
        if stage == 2:
            sib.append(link.copy(block(far), block(far), me.sibling()))
    yield
    for c in sib:
        c.wait_recv()


def add_into(dst, *srcs):
    total = dst[...].astype(F32)
    for s in srcs:
        total = total + s[...].astype(F32)
    dst[...] = total.astype(dst.dtype)


def add_blocks(dst, srcs, lead):
    if lead == 0:
        add_into(dst, *srcs)
        return
    n = dst.shape[0]
    if lead == 1:
        for a in range(n):
            add_into(dst.at[a], *[s.at[a] for s in srcs])
        return

    def body(k, _):
        a, b = k // dst.shape[1], k % dst.shape[1]
        add_into(dst.at[a, b], *[s.at[a, b] for s in srcs])
        return 0

    lax.fori_loop(0, n * dst.shape[1], body, 0)


def scatter_steps(me, link, buf, rx, order, rows, finish):
    rx_core, rx3, rx2, rx1 = rx
    mine, theirs = buf.at[me.core], buf.at[1 - me.core]
    at = [getattr(me, d) for d in order]
    i = at[2]
    lo, hi, far = (i + 3) % 4, (i + 1) % 4, (i + 2) % 4
    cores = {}
    for name, b in (("far", far), ("hi", hi), ("lo", lo), ("i", i)):
        cores[name] = link.copy(theirs.at[b], rx_core.at[b], me.sibling())
    yield
    for stage in (2, 1, 0):
        i, d = at[stage], order[stage]
        lo, hi, far = (i + 3) % 4, (i + 1) % 4, (i + 2) % 4
        right, left = me.hop(d, 1), me.hop(d, -1)
        r = rows if stage == 0 else None
        lead = stage

        def block(b, stage=stage):
            if stage == 0:
                return mine.at[at[2], at[1], b]
            if stage == 1:
                return mine.at[at[2], b]
            return mine.at[b]

        def settle(name, b, stage=stage):
            if stage == 2:
                cores[name].wait_recv()
                add_blocks(mine.at[b], [rx_core.at[b]], 2)

        R = (rx1, rx2, rx3)[stage]
        settle("far", far)
        m0 = link.copy(half(block(far), r, 0), half(R.at[0], r, 0), right)
        m1 = link.copy(half(block(far), r, 1), half(R.at[0], r, 1), left)
        settle("hi", hi)
        d1 = link.copy(half(block(hi), r, 1), half(R.at[1], r, 1), right)
        settle("lo", lo)
        d2 = link.copy(half(block(lo), r, 0), half(R.at[2], r, 0), left)
        yield
        m0.wait_recv()
        add_blocks(half(block(hi), r, 0), [half(R.at[0], r, 0)], lead)
        d3 = link.copy(half(block(hi), r, 0), half(R.at[1], r, 0), right)
        m1.wait_recv()
        add_blocks(half(block(lo), r, 1), [half(R.at[0], r, 1)], lead)
        d4 = link.copy(half(block(lo), r, 1), half(R.at[2], r, 1), left)
        settle("i", i)
        yield
        for c in (d1, d2, d3, d4):
            c.wait_recv()
        if stage > 0:
            add_blocks(block(i), [R.at[1], R.at[2]], lead)
        else:
            finish(
                block(i)[...].astype(F32)
                + R[1].astype(F32)
                + R[2].astype(F32)
            )


def run_all(gens):
    live = list(gens)
    while live:
        nxt = []
        for g in live:
            try:
                next(g)
                nxt.append(g)
            except StopIteration:
                pass
        live = nxt


def gather_kernel(
    qkv, out, up, down, proj, vecs,
    a0, a1, a2, u0, u1, u2, d0, d1, d2, pj, vo,
    aloc, arx, urx, drx, prx, vrx, p48, p32, vst, stage, send, recv, lsem,
):
    me = Place()
    link = Link(send, recv)
    s = (me.z % 2) * 4 + me.x
    aloc[:, 0:2304] = qkv[...]
    aloc[:, 2304:3072] = out[...]
    enter(me)
    got = {"a": [], "u": [], "v": []}
    for name, src, rx in (("a", aloc, arx), ("u", up, urx)):
        for k in range(1, 8):
            t = (s + k) % 8
            peer = me.dev(z=(me.z // 2) * 2 + t // 4, x=t % 4)
            cols = pl.ds(pl.multiple_of(384 * t, 128), 384)
            got[name].append(link.copy(src.at[:, cols], rx.at[s], peer))
        if name == "a":
            for k in range(1, 8):
                t = (s + k) % 8
                peer = me.dev(z=(me.z // 2) * 2 + t // 4, x=t % 4)
                got["v"].append(link.copy(vecs, vrx.at[s], peer))
    odd = me.x % 2
    other = pl.ds(pl.multiple_of(384 * (1 - odd), 128), 384)
    cd = link.copy(down.at[:, other], drx.at[odd], me.dev(x=me.x + 1 - 2 * odd))
    cp = []
    for k in range(1, 4):
        t = (me.x + k) % 4
        cols = pl.ds(pl.multiple_of(128 * t, 128), 128)
        cp.append(link.copy(proj.at[:, cols], prx.at[me.x], me.dev(x=t)))
    own = pl.ds(pl.multiple_of(384 * s, 128), 384)
    arx[s] = aloc[:, own]
    urx[s] = up[:, own]
    drx[odd] = down[:, pl.ds(pl.multiple_of(384 * odd, 128), 384)]
    prx[me.x] = proj[:, pl.ds(pl.multiple_of(128 * me.x, 128), 128)]
    vrx[s] = vecs[...]

    n_local = [0]

    def put(src, dst):
        c = pltpu.make_async_copy(src, dst, lsem.at[n_local[0]])
        n_local[0] += 1
        c.start()
        return c

    gens = []
    bufs = {"a": (a0, a1, a2), "u": (u0, u1, u2), "d": (d0, d1, d2)}
    places = [[getattr(me, d) for d in o] for o in ORDERS]

    def piece(ref, c):
        p = places[c]
        return ref.at[me.core, p[2], p[1], p[0]]

    for n, name in enumerate(("a", "u", "d")):
        if name == "d":
            cd.wait_recv()
            for j in range(2):
                p48[24 * j : 24 * j + 24, :] = drx[j]
        else:
            for c in got[name]:
                c.wait_recv()
            rx = arx if name == "a" else urx
            for j in range(8):
                p48[6 * j : 6 * j + 6, :] = rx[j]
        puts = []
        for c in range(3):
            stage[n, c] = p48[:, 128 * c : 128 * c + 128].astype(BF)
            puts.append(put(stage.at[n, c], piece(bufs[name][c], c)))
        for c in puts:
            c.wait()
        for c in range(3):
            gens.append(gather_steps(me, link, bufs[name][c], ORDERS[c], 48))
    for c in cp:
        c.wait_recv()
    p32[...] = jnp.zeros_like(p32)
    for j in range(4):
        p32[8 * j : 8 * j + 6, :] = prx[j]
    stage[3, 0, 0:32, :] = p32[...].astype(BF)
    put(stage.at[3, 0, pl.ds(0, 32)], piece(pj, 0)).wait()
    gens.append(gather_steps(me, link, pj, ORDERS[0], 32))

    for c in got["v"]:
        c.wait_recv()
    total = vrx[0]
    for j in range(1, 8):
        total = total + pltpu.roll(vrx[j], 6 * j, 1)
    v = me.dp * 2 + me.z // 2
    vst[v] = total
    cv = []
    for k in range(1, 16):
        t = (v + k) % 16
        peer = (t // 2, ((t % 2) * 2 + me.z % 2) * 4 + me.x)
        cv.append(link.copy(vst.at[v], vst.at[v], peer))
    run_all(gens)
    for c in cv:
        c.wait_recv()
    vo[...] = vst[...]
    link.drain()


def gathered(w_qkv, w_out, w_up, w_down, w_proj, vecs):
    any_ = pl.BlockSpec(memory_space=pl.ANY)
    vm = pl.BlockSpec(memory_space=pltpu.VMEM)
    big = jax.ShapeDtypeStruct((2, 4, 4, 4, 48, 128), BF)
    outs = [big] * 9 + [
        jax.ShapeDtypeStruct((2, 4, 4, 4, 32, 128), BF),
        jax.ShapeDtypeStruct((16, 8, 128), F32),
    ]
    n = 240
    return pl.pallas_call(
        gather_kernel,
        out_shape=outs,
        in_specs=[vm] * 6,
        out_specs=[any_] * 10 + [vm],
        scratch_shapes=[
            pltpu.VMEM((6, 3072), F32),
            pltpu.VMEM((8, 6, 384), F32),
            pltpu.VMEM((8, 6, 384), F32),
            pltpu.VMEM((2, 24, 384), F32),
            pltpu.VMEM((4, 6, 128), F32),
            pltpu.VMEM((8, 8, 128), F32),
            pltpu.VMEM((48, 384), F32),
            pltpu.VMEM((32, 128), F32),
            pltpu.VMEM((16, 8, 128), F32),
            pltpu.VMEM((4, 3, 48, 128), BF),
            pltpu.SemaphoreType.DMA((n,)),
            pltpu.SemaphoreType.DMA((n,)),
            pltpu.SemaphoreType.DMA((16,)),
        ],
        compiler_params=pltpu.CompilerParams(
            collective_id=0, has_side_effects=True, vmem_limit_bytes=32 << 20
        ),
    )(w_qkv, w_out, w_up, w_down, w_proj, vecs)


def scatter_kernel(
    a0, a1, a2, u0, u1, u2, d0, d1, d2, pj, gv,
    oqkv, oout, oup, odown, oproj, ovec,
    rc, r3, r2, r1, pc, p3, p2, p1, tot, ptot, orx, ust, drx, pst, prx, vst, vrx, vst2, vrx2, send, recv,
):
    me = Place()
    link = Link(send, recv)
    s = (me.z % 2) * 4 + me.x
    v = me.dp * 2 + me.z // 2
    enter(me)
    for k in range(16):
        lane = 48 * k
        t, off = lane // 128, lane % 128
        x0 = gv[:, 128 * t : 128 * t + 128]
        y0 = pltpu.roll(x0, (128 - off) % 128, 1) if off else x0
        if off > 80:
            x1 = gv[:, 128 * t + 128 : 128 * t + 256]
            y1 = pltpu.roll(x1, (128 - off) % 128, 1)
            lanes = lax.broadcasted_iota(jnp.int32, (8, 128), 1)
            y0 = jnp.where(lanes < 128 - off, y0, y1)
        vst[k] = y0
    cv = []
    for k in range(1, 16):
        t = (v + k) % 16
        peer = (t // 2, ((t % 2) * 2 + me.z % 2) * 4 + me.x)
        cv.append(link.copy(vst.at[t], vrx.at[v], peer))
    vrx[v] = vst[v]
    bufs = {"d": (d0, d1, d2), "u": (u0, u1, u2), "a": (a0, a1, a2)}
    gens = []

    def keep(n, c):
        def finish(total):
            tot[n, :, 128 * c : 128 * c + 128] = total

        return finish

    def keep_p(total):
        ptot[...] = total

    for n, name in enumerate(("d", "u", "a")):
        for c in range(3):
            k = 3 * n + c
            gens.append(
                scatter_steps(
                    me, link, bufs[name][c],
                    (rc.at[k], r3.at[k], r2.at[k], r1.at[k]),
                    ORDERS[c], 48, keep(n, c),
                )
            )
    gens.append(scatter_steps(me, link, pj, (pc, p3, p2, p1), ORDERS[0], 32, keep_p))
    run_all(gens)
    for c in cv:
        c.wait_recv()
    vtot = vrx[0]
    for k in range(1, 16):
        vtot = vtot + vrx[k]
    vst2[...] = vtot
    got = []
    for k in range(1, 8):
        t = (s + k) % 8
        peer = me.dev(z=(me.z // 2) * 2 + t // 4, x=t % 4)
        got.append(link.copy(vst2, vrx2.at[s], peer))
    vrx2[s] = vst2[...]
    for n in (1, 2):
        for j in range(8):
            ust[n - 1, j] = tot[n, 6 * j : 6 * j + 6, :]
        for k in range(1, 8):
            t = (s + k) % 8
            peer = me.dev(z=(me.z // 2) * 2 + t // 4, x=t % 4)
            got.append(link.copy(ust.at[n - 1, t], orx.at[n - 1, s], peer))
        orx[n - 1, s] = ust[n - 1, s]
    odd = me.x % 2
    got.append(
        link.copy(
            tot.at[0, pl.ds(pl.multiple_of(24 * (1 - odd), 8), 24)],
            drx.at[odd],
            me.dev(x=me.x + 1 - 2 * odd),
        )
    )
    drx[odd] = tot[0, pl.ds(pl.multiple_of(24 * odd, 8), 24), :]
    for j in range(4):
        pst[j] = ptot[8 * j : 8 * j + 6, :]
    for k in range(1, 4):
        t = (me.x + k) % 4
        got.append(link.copy(pst.at[t], prx.at[me.x], me.dev(x=t)))
    prx[me.x] = pst[me.x]
    for c in got:
        c.wait_recv()
    vtot = vrx2[0]
    for k in range(1, 8):
        vtot = vtot + vrx2[k]
    ovec[...] = pltpu.roll(vtot, (128 - 6 * s) % 128, 1)
    for j in range(8):
        oup[:, 384 * j : 384 * j + 384] = orx[0, j]
        if j < 6:
            oqkv[:, 384 * j : 384 * j + 384] = orx[1, j]
        else:
            oout[:, 384 * (j - 6) : 384 * (j - 6) + 384] = orx[1, j]
    for j in range(2):
        odown[:, 384 * j : 384 * j + 384] = drx[j]
    for j in range(4):
        oproj[:, 128 * j : 128 * j + 128] = prx[j]
    link.drain()


def scattered(bufs, gv):
    vm = pl.BlockSpec(memory_space=pltpu.VMEM)
    n = 340
    S = jax.ShapeDtypeStruct
    V = pltpu.VMEM
    return pl.pallas_call(
        scatter_kernel,
        out_shape=[
            S((6, 2304), F32), S((6, 768), F32), S((6, 3072), F32), S((24, 768), F32), S((6, 512), F32), S((8, 128), F32)
        ],
        in_specs=[vm] * 11,
        out_specs=[vm] * 6,
        scratch_shapes=[
            V((9, 4, 4, 4, 48, 128), BF), V((9, 3, 4, 4, 48, 128), BF), V((9, 3, 4, 48, 128), BF), V((9, 3, 48, 128), BF),
            V((4, 4, 4, 32, 128), BF), V((3, 4, 4, 32, 128), BF), V((3, 4, 32, 128), BF), V((3, 32, 128), BF),
            V((3, 48, 384), F32), V((32, 128), F32), V((2, 8, 6, 384), F32), V((2, 8, 6, 384), F32),
            V((2, 24, 384), F32), V((4, 6, 128), F32), V((4, 6, 128), F32),
            V((16, 8, 128), F32), V((16, 8, 128), F32), V((8, 128), F32), V((8, 8, 128), F32),
            pltpu.SemaphoreType.DMA((n,)),
            pltpu.SemaphoreType.DMA((n,)),
        ],
        compiler_params=pltpu.CompilerParams(
            collective_id=1, has_side_effects=True, vmem_limit_bytes=56 << 20
        ),
    )(*bufs, gv)


def canonical(buf, c):
    names = ("core",) + ORDERS[c][::-1]
    return jnp.transpose(buf, [names.index(d) for d in ("y", "core", "z", "x")] + [4, 5])


def classed(arr, c):
    names = ("y", "core", "z", "x")
    want = ("core",) + ORDERS[c][::-1]
    return jnp.transpose(arr, [names.index(d) for d in want] + [4, 5])


def wide(bufs):
    full = jnp.stack([canonical(b, c) for c, b in enumerate(bufs)], axis=5)
    full = full.reshape(4, 2, 2, 2, 4, 48, 3, 128)
    return jnp.transpose(full, (0, 1, 2, 5, 3, 4, 6, 7)).reshape(768, 3072)


def narrow(mat):
    full = mat.reshape(4, 2, 2, 48, 2, 4, 3, 128)
    full = jnp.transpose(full, (6, 0, 1, 2, 4, 5, 3, 7)).reshape(3, 4, 2, 4, 4, 48, 128)
    return [classed(full[c], c) for c in range(3)]


def tall(bufs):
    full = jnp.stack([canonical(b, c) for c, b in enumerate(bufs)], axis=5)
    full = full.reshape(4, 2, 4, 2, 2, 48, 3, 128)
    return jnp.transpose(full, (0, 1, 2, 3, 5, 4, 6, 7)).reshape(3072, 768)


def untall(mat):
    full = mat.reshape(4, 2, 4, 2, 48, 2, 3, 128)
    full = jnp.transpose(full, (6, 0, 1, 2, 3, 5, 4, 7)).reshape(3, 4, 2, 4, 4, 48, 128)
    return [classed(full[c], c) for c in range(3)]


def proj_of(buf):
    full = canonical(buf, 0)
    full = jnp.transpose(full, (0, 1, 2, 4, 3, 5)).reshape(128, 8, 512)
    return full[:, :6].reshape(768, 512)


def proj_back(mat):
    full = jnp.pad(mat.reshape(128, 6, 512), ((0, 0), (0, 2), (0, 0))).reshape(4, 2, 4, 32, 4, 128)
    return classed(jnp.transpose(full, (0, 1, 2, 4, 3, 5)), 0)


HEADS = 12
HDIM = 64


def norm_rows(values, norm_gain, norm_shift):
    center = jnp.mean(values, axis=-1, keepdims=True)
    centred = values - center
    spread = jnp.mean(centred * centred, axis=-1, keepdims=True)
    return centred * lax.rsqrt(spread + 1e-05) * norm_gain + norm_shift


def unit_rows(values):
    row_total = jnp.sum(values * values, axis=-1, keepdims=True) + 1e-06
    return values * lax.rsqrt(row_total)


def pooled_rows(residual_two, norm_gain, norm_shift, query_vec, kept_mask):
    images_here, patches = kept_mask.shape
    final = norm_rows(residual_two, norm_gain, norm_shift).reshape(images_here, patches, -1)
    pool_logits = jnp.sum(final * query_vec, axis=-1) / math.sqrt(final.shape[-1])
    pool_logits = jnp.where(kept_mask > 0, pool_logits, -1e30)
    shares = jax.nn.softmax(pool_logits, axis=-1)
    return jnp.sum(shares[:, :, None] * final, axis=1)


def head_loss(image_rows, text_rows, scale_log, pairing):
    total_rows = image_rows.shape[0]
    logits = jnp.exp(scale_log[0]) * jnp.dot(
        image_rows, text_rows.T, precision=lax.Precision.HIGHEST
    )
    target = (pairing[:, None] == jnp.arange(total_rows, dtype=jnp.int32)[None, :]).astype(
        logits.dtype
    )
    row_totals = jax.nn.logsumexp(logits, axis=1)
    col_totals = jax.nn.logsumexp(logits, axis=0)
    matched = jnp.sum(logits * target)
    return (jnp.sum(row_totals) + jnp.sum(col_totals) - 2.0 * matched) / (2.0 * total_rows)


def shards(
    tokens,
    keep_mask,
    pairing,
    text_vectors,
    logit_scale,
    w_qkv,
    w_out,
    w_up,
    w_down,
    w_proj,
    gain_one,
    shift_one,
    gain_two,
    shift_two,
    gain_post,
    shift_post,
    pool_query,
):
    vecs = jnp.stack(
        [gain_one, shift_one, gain_two, shift_two, gain_post, shift_post, pool_query]
    )
    vecs = jnp.pad(vecs.astype(BF).astype(F32), ((0, 1), (0, 122)))
    got = gathered(w_qkv, w_out, w_up, w_down, w_proj, vecs)
    mat_a = wide(got[0:3])
    qkv_full, out_full = mat_a[:, :2304], mat_a[:, 2304:]
    up_full = wide(got[3:6])
    down_full = tall(got[6:9])
    proj_full = proj_of(got[9])
    vec_full = jnp.transpose(got[10][:, :, :48], (1, 0, 2)).reshape(8, 768)
    gain_first, shift_first, gain_second, shift_second, gain_last, shift_last, query_full = [
        vec_full[k] for k in range(7)
    ]
    qkv_back, out_back, up_back, down_back, proj_back_w = qkv_full, out_full, up_full, down_full, proj_full
    images_here, patches = keep_mask.shape
    model_width = tokens.shape[1]
    row_count = images_here * patches
    scaling = HDIM ** (-0.5)
    live_keys = (keep_mask > 0)[:, None, None, :]
    inputs = tokens.astype(jnp.float32)
    normed_one, norm_one_back = jax.vjp(norm_rows, inputs, gain_first, shift_first)
    normed = normed_one.astype(jnp.bfloat16)
    mixed = jnp.dot(normed, qkv_full, preferred_element_type=jnp.float32).astype(jnp.bfloat16)
    mixed = mixed.reshape(images_here, patches, 3, HEADS, HDIM)
    queries = mixed[:, :, 0]
    key_rows = mixed[:, :, 1]
    values = mixed[:, :, 2]
    raw_scores = (
        jnp.einsum("bqhd,bkhd->bhqk", queries, key_rows, preferred_element_type=jnp.float32)
        * scaling
    )
    raw_scores = jnp.where(live_keys, raw_scores, -1e30)
    log_total = jax.nn.logsumexp(raw_scores, axis=-1, keepdims=True)
    softmaxed = jnp.exp(raw_scores - log_total).astype(jnp.bfloat16)
    attended = jnp.einsum("bhqk,bkhd->bqhd", softmaxed, values, preferred_element_type=jnp.float32)
    attended = attended.astype(jnp.bfloat16).reshape(row_count, model_width)
    residual_one = inputs + jnp.dot(attended, out_full, preferred_element_type=jnp.float32)
    normed_mid, norm_two_back = jax.vjp(norm_rows, residual_one, gain_second, shift_second)
    normed_two = normed_mid.astype(jnp.bfloat16)
    upward = jnp.dot(normed_two, up_full, preferred_element_type=jnp.float32)
    active_full, gelu_back = jax.vjp(partial(jax.nn.gelu, approximate=False), upward)
    active = active_full.astype(jnp.bfloat16)
    residual_two = residual_one + jnp.dot(active, down_full, preferred_element_type=jnp.float32)
    pooled, pool_back = jax.vjp(
        partial(pooled_rows, kept_mask=keep_mask), residual_two, gain_last, shift_last, query_full
    )
    pooled_half = pooled.astype(jnp.bfloat16)
    embedded = jnp.dot(pooled_half, proj_full, preferred_element_type=jnp.float32)
    unit_image, unit_back = jax.vjp(unit_rows, embedded)
    unit_text, text_back = jax.vjp(unit_rows, text_vectors)
    image_all, text_all = (
        lax.all_gather(unit_image.astype(jnp.bfloat16), ("dp", "fsdp"), axis=0, tiled=True),
        lax.all_gather(unit_text.astype(jnp.bfloat16), ("dp", "fsdp"), axis=0, tiled=True),
    )
    loss_value, head_back = jax.vjp(
        partial(head_loss, pairing=pairing),
        image_all.astype(jnp.float32),
        text_all.astype(jnp.float32),
        logit_scale,
    )
    grad_image_all, grad_text_all, grad_scale = head_back(jnp.ones_like(loss_value))
    offset = lax.axis_index(("dp", "fsdp")) * images_here
    grad_unit = lax.dynamic_slice_in_dim(grad_image_all, offset, images_here, 0)
    grad_unit_text = lax.dynamic_slice_in_dim(grad_text_all, offset, images_here, 0)
    grad_text = text_back(grad_unit_text)[0]
    grad_embed = unit_back(grad_unit)[0].astype(jnp.bfloat16)
    grad_proj = jnp.dot(pooled_half.T, grad_embed, preferred_element_type=jnp.float32)
    grad_pooled = jnp.dot(grad_embed, proj_back_w.T, preferred_element_type=jnp.float32)
    grad_second, grad_gain_post, grad_shift_post, grad_query = pool_back(grad_pooled)
    grad_branch_two = grad_second.astype(jnp.bfloat16)
    grad_down = jnp.dot(active.T, grad_branch_two, preferred_element_type=jnp.float32)
    grad_active = jnp.dot(grad_branch_two, down_back.T, preferred_element_type=jnp.float32)
    grad_upward = gelu_back(grad_active)[0].astype(jnp.bfloat16)
    grad_up = jnp.dot(normed_two.T, grad_upward, preferred_element_type=jnp.float32)
    grad_normed_two = jnp.dot(grad_upward, up_back.T, preferred_element_type=jnp.float32)
    grad_first_norm, grad_gain_two, grad_shift_two = norm_two_back(grad_normed_two)
    grad_first = grad_second + grad_first_norm
    grad_branch = grad_first.astype(jnp.bfloat16)
    grad_out = jnp.dot(attended.T, grad_branch, preferred_element_type=jnp.float32)
    grad_attended = jnp.dot(grad_branch, out_back.T, preferred_element_type=jnp.float32)
    grad_attended = grad_attended.astype(jnp.bfloat16).reshape(images_here, patches, HEADS, HDIM)
    again_scores = (
        jnp.einsum("bqhd,bkhd->bhqk", queries, key_rows, preferred_element_type=jnp.float32)
        * scaling
    )
    again_scores = jnp.where(live_keys, again_scores, -1e30)
    probs_again = jnp.exp(again_scores - log_total)
    grad_probs = jnp.einsum(
        "bqhd,bkhd->bhqk", grad_attended, values, preferred_element_type=jnp.float32
    )
    grad_values = jnp.einsum(
        "bhqk,bqhd->bkhd",
        probs_again.astype(jnp.bfloat16),
        grad_attended,
        preferred_element_type=jnp.float32,
    )
    grad_scores = probs_again * (
        grad_probs - jnp.sum(probs_again * grad_probs, axis=-1, keepdims=True)
    )
    grad_scores = grad_scores.astype(jnp.bfloat16)
    grad_queries = (
        jnp.einsum("bhqk,bkhd->bqhd", grad_scores, key_rows, preferred_element_type=jnp.float32)
        * scaling
    )
    grad_keys = (
        jnp.einsum("bhqk,bqhd->bkhd", grad_scores, queries, preferred_element_type=jnp.float32)
        * scaling
    )
    grad_mixed = jnp.stack([grad_queries, grad_keys, grad_values], axis=2).astype(jnp.bfloat16)
    grad_mixed = grad_mixed.reshape(row_count, 3 * model_width)
    grad_qkv = jnp.dot(normed.T, grad_mixed, preferred_element_type=jnp.float32)
    grad_normed = jnp.dot(grad_mixed, qkv_back.T, preferred_element_type=jnp.float32)
    grad_input_norm, grad_gain_one, grad_shift_one = norm_one_back(grad_normed)
    grad_tokens = grad_first + grad_input_norm
    grads_a = narrow(jnp.concatenate([grad_qkv, grad_out], axis=1).astype(BF))
    grads_u = narrow(grad_up.astype(BF))
    grads_d = untall(grad_down.astype(BF))
    grads_p = proj_back(grad_proj.astype(BF))
    grads_v = jnp.stack(
        [grad_gain_one, grad_shift_one, grad_gain_two, grad_shift_two, grad_gain_post, grad_shift_post, grad_query]
    )
    grads_v = jnp.pad(grads_v, ((0, 1), (0, 0)))
    *mats, vec_out = scattered((*grads_a, *grads_u, *grads_d, grads_p), grads_v)
    owned = (*mats, *[vec_out[k, :6] for k in range(7)])
    return (
        loss_value.reshape(1),
        grad_tokens,
        grad_text,
        owned[0],
        owned[1],
        owned[2],
        owned[3],
        owned[4],
        owned[5],
        owned[6],
        owned[7],
        owned[8],
        owned[9],
        owned[10],
        owned[11],
        grad_scale,
    )


def solution(mesh):
    in_specs = (
        P(("dp", "fsdp"), None),
        P(("dp", "fsdp"), None),
        P(),
        P(("dp", "fsdp"), None),
        P(),
        P(("dp", "fsdp"), None),
        P(("dp", "fsdp"), None),
        P(("dp", "fsdp"), None),
        P(("dp", "fsdp"), None),
        P(("dp", "fsdp"), None),
        P(("dp", "fsdp")),
        P(("dp", "fsdp")),
        P(("dp", "fsdp")),
        P(("dp", "fsdp")),
        P(("dp", "fsdp")),
        P(("dp", "fsdp")),
        P(("dp", "fsdp")),
    )
    out_specs = (
        P(),
        P(("dp", "fsdp"), None),
        P(("dp", "fsdp"), None),
        P(("dp", "fsdp"), None),
        P(("dp", "fsdp"), None),
        P(("dp", "fsdp"), None),
        P(("dp", "fsdp"), None),
        P(("dp", "fsdp"), None),
        P(("dp", "fsdp")),
        P(("dp", "fsdp")),
        P(("dp", "fsdp")),
        P(("dp", "fsdp")),
        P(("dp", "fsdp")),
        P(("dp", "fsdp")),
        P(("dp", "fsdp")),
        P(),
    )
    return jax.shard_map(shards, mesh=mesh, in_specs=in_specs, out_specs=out_specs, check_vma=False)
```

```python
from functools import partial
import math

import jax
import jax.numpy as jnp
from jax import lax
from jax.experimental import pallas as pl
from jax.experimental.pallas import tpu as pltpu
from jax.sharding import PartitionSpec as P

MESH = pl.DeviceIdType.MESH
BF = jnp.bfloat16
F32 = jnp.float32
IMG = 208
R = 4 * IMG
D = 768
ROOT = math.sqrt(768.0)


class Place:
    def __init__(self):
        dp = lax.axis_index("dp")
        fs = lax.axis_index("fsdp")
        self.y, self.core = dp // 2, dp % 2
        self.z, self.x = fs // 4, fs % 4
        self.s = (self.z % 2) * 4 + self.x
        self.v = dp * 2 + self.z // 2

    def dev(self, **moved):
        at = dict(x=self.x, y=self.y, z=self.z, core=self.core)
        at.update(moved)
        return (at["y"] * 2 + at["core"], at["z"] * 4 + at["x"])

    def hop(self, dim, step):
        return self.dev(**{dim: (getattr(self, dim) + step + 4) % 4})

    def sibling(self):
        return self.dev(core=1 - self.core)

    def s_peer(self, k):
        t = (self.s + k) % 8
        return t, self.dev(z=(self.z // 2) * 2 + t // 4, x=t % 4)

    def v_peer(self, k):
        t = (self.v + k) % 16
        return t, (t // 2, ((t % 2) * 2 + self.z % 2) * 4 + self.x)


class Link:
    def __init__(self, send, recv):
        self.send, self.recv, self.n = send, recv, 0
        self.open = []

    def copy(self, src, dst, dev):
        k = self.n
        self.n += 1
        c = pltpu.make_async_remote_copy(
            src_ref=src,
            dst_ref=dst,
            send_sem=self.send.at[k],
            recv_sem=self.recv.at[k],
            device_id=dev,
            device_id_type=MESH,
        )
        c.start()
        self.open.append(c)
        return c

    def drain(self):
        for c in self.open:
            c.wait_send()
        self.open = []


ORDERS = (("x", "y", "z"), ("y", "z", "x"), ("z", "x", "y"))


def enter(me):
    sem = pltpu.get_barrier_semaphore()
    peers = [me.s_peer(k)[1] for k in range(1, 8)]
    peers += [me.v_peer(k)[1] for k in range(1, 16)]
    other = jnp.where(me.z % 2 == 0, (me.z + 3) % 4, (me.z + 1) % 4)
    peers.append(me.dev(z=other))
    for p in peers:
        pl.semaphore_signal(sem, inc=1, device_id=p, device_id_type=MESH)
    pl.semaphore_wait(sem, len(peers))


def ds(start, size, unit=None):
    if isinstance(start, int):
        return pl.ds(start, size)
    return pl.ds(pl.multiple_of(start, unit or size), size)


class Pieces:
    def __init__(self, ref, base, order, rows):
        self.ref, self.base, self.order, self.rows = ref, base, order, rows

    def start(self, core, **at):
        d1, d2, d3 = (at[d] for d in self.order)
        return self.base + (((core * 4 + d3) * 4 + d2) * 4 + d1) * self.rows

    def piece(self, core, **at):
        return self.ref.at[ds(self.start(core, **at), self.rows, 16)]

    def load(self, core, lo=0, n=None, **at):
        return self.ref[pl.ds(self.start(core, **at) + lo, n or self.rows), :]

    def store(self, value, core, lo=0, **at):
        self.ref[pl.ds(self.start(core, **at) + lo, value.shape[0]), :] = value

    def block(self, core, stage, me, b):
        at = [getattr(me, d) for d in self.order]
        at[stage] = b
        for k in range(stage):
            at[k] = 0
        return self.start(core, **dict(zip(self.order, at))), self.rows * 4**stage


def cut(block, which):
    start, size = block
    first = (size // 2 + 15) // 16 * 16
    return (start, first) if which == 0 else (start + first, size - first)


def rows_of(ref, block):
    return ref.at[ds(block[0], block[1], 16)]


def gather_steps(me, link, buf):
    ref = buf.ref

    def send(block, dev):
        return link.copy(rows_of(ref, block), rows_of(ref, block), dev)

    at = [getattr(me, d) for d in buf.order]
    for stage in range(3):
        i, d = at[stage], buf.order[stage]

        def block(b, stage=stage):
            return buf.block(me.core, stage, me, b)

        lo, hi, far = (i + 3) % 4, (i + 1) % 4, (i + 2) % 4
        right, left = me.hop(d, 1), me.hop(d, -1)
        cr = send(block(i), right)
        cl = send(block(i), left)
        sib = []
        if stage == 2:
            sib.append(send(block(i), me.sibling()))
        yield
        cr.wait_recv()
        fr = send(cut(block(lo), 0), right)
        if stage == 2:
            sib.append(send(block(lo), me.sibling()))
        cl.wait_recv()
        fl = send(cut(block(hi), 1), left)
        if stage == 2:
            sib.append(send(block(hi), me.sibling()))
        yield
        fr.wait_recv()
        fl.wait_recv()
        if stage == 2:
            sib.append(send(block(far), me.sibling()))
    yield
    for c in sib:
        c.wait_recv()


def add_rows(dst_ref, dst, *srcs):
    size = dst[1]
    step = 96 if size % 96 == 0 else (64 if size % 64 == 0 else size)

    def body(k, _):
        total = dst_ref[ds(dst[0] + k * step, step, 16), :].astype(F32)
        for ref, start in srcs:
            total = total + ref[ds(start + k * step, step, 16), :].astype(F32)
        dst_ref[ds(dst[0] + k * step, step, 16), :] = total.astype(BF)
        return 0

    if size == step:
        body(0, 0)
    else:
        lax.fori_loop(0, size // step, body, 0)


def scatter_steps(me, link, buf, rx_core, rx, finish, give=None, need=None):
    ref, rows = buf.ref, buf.rows
    at = [getattr(me, d) for d in buf.order]
    i = at[2]
    lo, hi, far = (i + 3) % 4, (i + 1) % 4, (i + 2) % 4
    if need is not None:
        pl.semaphore_wait(need, 1)
    cores = {}
    for name, b in (("far", far), ("hi", hi), ("lo", lo), ("i", i)):
        src = buf.block(1 - me.core, 2, me, b)
        dst = (b * src[1], src[1])
        cores[name] = link.copy(rows_of(ref, src), rows_of(rx_core, dst), me.sibling())
    yield
    base = {2: 0, 1: 3 * 16 * rows, 0: 3 * 20 * rows}
    for stage in (2, 1, 0):
        i, d = at[stage], buf.order[stage]
        lo, hi, far = (i + 3) % 4, (i + 1) % 4, (i + 2) % 4
        right, left = me.hop(d, 1), me.hop(d, -1)
        size = rows * 4**stage

        def block(b, stage=stage):
            return buf.block(me.core, stage, me, b)

        def slot(n, stage=stage, size=size):
            return (base[stage] + n * size, size)

        def settle(name, b, stage=stage):
            if stage == 2:
                cores[name].wait_recv()
                blk = block(b)
                add_rows(ref, blk, (rx_core, b * blk[1]))

        def send(src, dst, dev):
            return link.copy(rows_of(ref, src), rows_of(rx, dst), dev)

        settle("far", far)
        m0 = send(cut(block(far), 0), cut(slot(0), 0), right)
        m1 = send(cut(block(far), 1), cut(slot(0), 1), left)
        settle("hi", hi)
        d1 = send(cut(block(hi), 1), cut(slot(1), 1), right)
        settle("lo", lo)
        d2 = send(cut(block(lo), 0), cut(slot(2), 0), left)
        yield
        m0.wait_recv()
        add_rows(ref, cut(block(hi), 0), (rx, cut(slot(0), 0)[0]))
        d3 = send(cut(block(hi), 0), cut(slot(1), 0), right)
        m1.wait_recv()
        add_rows(ref, cut(block(lo), 1), (rx, cut(slot(0), 1)[0]))
        d4 = send(cut(block(lo), 1), cut(slot(2), 1), left)
        settle("i", i)
        if stage == 2 and give is not None:
            pl.semaphore_signal(give, inc=1, device_id=me.sibling(), device_id_type=MESH)
        yield
        for c in (d1, d2, d3, d4):
            c.wait_recv()
        if stage > 0:
            add_rows(ref, block(i), (rx, slot(1)[0]), (rx, slot(2)[0]))
        else:
            own = block(i)
            finish(
                ref[ds(own[0], rows, 16), :].astype(F32)
                + rx[pl.ds(slot(1)[0], rows), :].astype(F32)
                + rx[pl.ds(slot(2)[0], rows), :].astype(F32)
            )


class Queue:
    def __init__(self):
        self.live = []

    def add(self, name, gen):
        self.live.append((name, gen))

    def step(self, names=None):
        keep = []
        for name, gen in self.live:
            if names is None or name in names:
                try:
                    next(gen)
                except StopIteration:
                    continue
            keep.append((name, gen))
        self.live = keep

    def finish(self, names=None):
        while any(names is None or n in names for n, _ in self.live):
            self.step(names)


def nn(a, b):
    return lax.dot_general(a, b, (((1,), (0,)), ((), ())), preferred_element_type=F32)


def nt(a, b):
    return lax.dot_general(a, b, (((1,), (1,)), ((), ())), preferred_element_type=F32)


def tn(a, b):
    return lax.dot_general(a, b, (((0,), (0,)), ((), ())), preferred_element_type=F32)


def whiten(x):
    centred = x - jnp.mean(x, axis=-1, keepdims=True)
    r = lax.rsqrt(jnp.mean(centred * centred, axis=-1, keepdims=True) + 1e-05)
    return centred * r, r


def whiten_back(y, xh, r):
    return r * (y - jnp.mean(y, axis=-1, keepdims=True) - xh * jnp.mean(y * xh, axis=-1, keepdims=True))


def fold(x):
    return jnp.sum(x.reshape(x.shape[0] // 8, 8, x.shape[1]), axis=0)


def split(x, parts):
    got = []
    for _ in range(parts):
        h = x.astype(BF)
        got.append(h)
        x = x - h.astype(F32)
    return got


def gelu_parts(u):
    a = jnp.abs(u)
    t = 1.0 / (1.0 + (0.3275911 * math.sqrt(0.5)) * a)
    e = jnp.exp(-0.5 * u * u)
    poly = t * (0.5 * 0.254829592 + t * (-0.5 * 0.284496736 + t * (0.5 * 1.421413741 + t * (-0.5 * 1.453152027 + t * (0.5 * 1.061405429)))))
    tail = poly * e
    phi = jnp.where(u < 0, tail, 1.0 - tail)
    return u * phi, phi + u * (e * (1.0 / math.sqrt(2.0 * math.pi)))


def blocks(n, body, unroll=1):
    lax.fori_loop(0, n, lambda k, c: (body(k), 0)[1], 0, unroll=unroll)


N_SEM = 560


def kernel(
    pairing, scale, v0, v1, v2, v3, v4, v5, v6,
    tok, mask, text, w_qkv, w_out, w_up, w_down, w_proj,
    o_loss, o_tok, o_text, o_qkv, o_out, o_up, o_down, o_proj, o_vec, o_scale, spill,
    wa, wu, wd, wp, q, k, v, pb, xh2, nrm, att, gb, act, gel, res, acc, r2,
    rxc, rxd, rxu, rxa, rxpc, rxp,
    aloc, arx, urx, drx, ploc, prx, vrx, vst, p48, p64, vec, gvec,
    mrow, mcol, share, dlc, bias, pool, e3, emb, cs, crx, cst, crx2,
    tot, ptot, orx, ust, pst, prx2, gst, grx, gst2, grx2,
    send, recv, lsem, credit,
):
    me = Place()
    link = Link(send, recv)
    todo = Queue()
    s = me.s
    lanes = lax.broadcasted_iota(jnp.int32, (8, 128), 1)
    subs = lax.broadcasted_iota(jnp.int32, (8, 128), 0)

    WA = [Pieces(wa, 6144 * c, ORDERS[c], 48) for c in range(3)]
    WU = [Pieces(wu, 6144 * c, ORDERS[c], 48) for c in range(3)]
    WD = [Pieces(wd, 6144 * c, ORDERS[c], 48) for c in range(3)]
    WP = Pieces(wp, 0, ORDERS[0], 64)
    GA = [Pieces(act, 6144 * c, ORDERS[c], 48) for c in range(3)]

    aloc[:, 0:2304] = w_qkv[...]
    aloc[:, 2304:3072] = w_out[...]
    mine = jnp.zeros((8, 128), F32)
    for n, ref in enumerate((v0, v1, v2, v3, v4, v5, v6)):
        for e in range(6):
            mine = jnp.where((subs == n) & (lanes == e), ref[e], mine)
    vst[...] = mine.astype(BF).astype(F32)
    ploc[...] = jnp.zeros_like(ploc)
    ploc[0:6, :] = w_proj[...]
    txt = text[...]
    ploc[8:12, :] = txt * lax.rsqrt(jnp.sum(txt * txt, axis=-1, keepdims=True) + 1e-06)
    enter(me)
    got = {"a": [], "u": [], "v": []}
    for name, src, rx in (("a", aloc, arx), ("v", vst, vrx), ("u", w_up, urx)):
        for n in range(1, 8):
            t, peer = me.s_peer(n)
            part = src if name == "v" else src.at[:, ds(384 * t, 384, 128)]
            got[name].append(link.copy(part, rx.at[s], peer))
    odd = me.x % 2
    cp = []
    for n in range(1, 4):
        t = (me.x + n) % 4
        cp.append(link.copy(ploc.at[:, ds(128 * t, 128)], prx.at[me.x], me.dev(x=t)))
    cd = link.copy(
        w_down.at[:, ds(384 * (1 - odd), 384, 128)], drx.at[odd], me.dev(x=me.x + 1 - 2 * odd)
    )
    arx[s] = aloc[:, ds(384 * s, 384, 128)]
    urx[s] = w_up[:, ds(384 * s, 384, 128)]
    drx[odd] = w_down[:, ds(384 * odd, 384, 128)]
    prx[me.x] = ploc[:, ds(128 * me.x, 128)]
    vrx[s] = vst[...]
    here = dict(x=me.x, y=me.y, z=me.z)

    def launch(name, bufs, n):
        for c, b in enumerate(bufs):
            if n == 48:
                b.piece(me.core, **here)[...] = p48[:, 128 * c : 128 * c + 128].astype(BF)
            else:
                b.piece(me.core, **here)[...] = p64[...].astype(BF)
            todo.add(name, gather_steps(me, link, b))

    for c in got["a"]:
        c.wait_recv()
    for j in range(8):
        p48[6 * j : 6 * j + 6, :] = arx[j]
    launch("a", WA, 48)
    todo.step()
    for c in got["v"]:
        c.wait_recv()
    total = vrx[0]
    for j in range(1, 8):
        total = total + pltpu.roll(vrx[j], 6 * j, 1)
    gst[me.v] = total
    cv = []
    for n in range(1, 16):
        t, peer = me.v_peer(n)
        cv.append(link.copy(gst.at[me.v], gst.at[me.v], peer))
    for c in got["u"]:
        c.wait_recv()
    for j in range(8):
        p48[6 * j : 6 * j + 6, :] = urx[j]
    launch("u", WU, 48)
    todo.step()
    for c in cp:
        c.wait_recv()
    for j in range(4):
        p64[8 * j : 8 * j + 8, :] = prx[j, 0:8]
        p64[32 + 8 * j : 40 + 8 * j, :] = prx[j, 8:16]
    launch("p", [WP], 64)
    cd.wait_recv()
    for j in range(2):
        p48[24 * j : 24 * j + 24, :] = drx[j]
    launch("d", WD, 48)
    todo.step()

    mrow[...] = jnp.zeros_like(mrow)
    mrow[0:4, 0:196] = mask[...].astype(F32)
    mcol[...] = mrow[...].T
    for i in range(4):
        col = jnp.where(mcol[0:IMG, i : i + 1] > 0, 0.0, -1e30)
        bias[i] = jnp.broadcast_to(col, (IMG, 128))
    for ref in (q, att):
        ref[R : R + 48, :] = jnp.zeros((48, D), BF)
    pool[...] = jnp.zeros_like(pool)
    gvec[...] = jnp.zeros_like(gvec)
    row = lax.broadcasted_iota(jnp.int32, (384, 512), 0)
    col = lax.broadcasted_iota(jnp.int32, (384, 512), 1)
    e3[...] = jnp.where(((col >> 3) * 6 + (col & 7) == row) & ((col & 7) < 6), 1.0, 0.0).astype(BF)
    for c in cv:
        c.wait_recv()
    vec[...] = jnp.zeros_like(vec)
    for n in range(16):
        t, off = 48 * n // 128, 48 * n % 128
        part = pltpu.roll(gst[n], off, 1) if off else gst[n]
        if off <= 80:
            vec[:, 128 * t : 128 * t + 128] += part
        else:
            vec[:, 128 * t : 128 * t + 128] += jnp.where(lanes >= off, part, 0.0)
            vec[:, 128 * t + 128 : 128 * t + 256] += jnp.where(lanes < off, part, 0.0)

    def gain(n):
        return vec[2 * n : 2 * n + 1, :], vec[2 * n + 1 : 2 * n + 2, :]

    def query():
        return vec[6:7, :]

    def tick():
        todo.step()

    def norm_one(block):
        rows = ds(32 * block, 32)
        g, b = gain(0)
        xh, _ = whiten(tok[rows, :].astype(F32))
        nrm[rows, :] = (xh * g + b).astype(BF)

    blocks(R // 32, norm_one)

    def wide(bufs, ch):
        zlo, xp = ch // 2, ch % 2
        cols = []
        for l in range(6):
            at = [
                bufs[l % 3].load(core, x=2 * xp + l // 3, y=y, z=2 * h + zlo)
                for y in range(4) for core in range(2) for h in range(2)
            ]
            cols.append(jnp.concatenate(at, axis=0))
        return jnp.concatenate(cols, axis=1)

    def wide_store(bufs, ch, value):
        zlo, xp = ch // 2, ch % 2
        for l in range(6):
            n = 0
            for y in range(4):
                for core in range(2):
                    for h in range(2):
                        part = value[48 * n : 48 * n + 48, 128 * l : 128 * l + 128]
                        bufs[l % 3].store(part, core, x=2 * xp + l // 3, y=y, z=2 * h + zlo)
                        n += 1

    def tall(bufs, y):
        cols = []
        for l in range(6):
            at = [
                bufs[l % 3].load(core, x=2 * xh + l // 3, y=y, z=z)
                for core in range(2) for z in range(4) for xh in range(2)
            ]
            cols.append(jnp.concatenate(at, axis=0))
        return jnp.concatenate(cols, axis=1)

    def tall_store(bufs, y, value):
        for l in range(6):
            n = 0
            for core in range(2):
                for z in range(4):
                    for xh in range(2):
                        part = value[48 * n : 48 * n + 48, 128 * l : 128 * l + 128]
                        bufs[l % 3].store(part, core, x=2 * xh + l // 3, y=y, z=z)
                        n += 1

    def flat(ref, ch, rows=None):
        return jnp.concatenate([ref[R * (6 * ch + l) : R * (6 * ch + l) + R, :] for l in range(6)], axis=1)

    todo.finish({"a"})
    for ch, dst in enumerate((q, k, v)):
        out = nn(nrm[...], wide(WA, ch))
        if ch == 0:
            out = out * 0.125
        dst[0:R, :] = out.astype(BF)
        tick()
    lane = lax.broadcasted_iota(jnp.int32, (1, 128), 1)
    heads = [jnp.where(lane < 64, 1.0, 0.0).astype(BF), jnp.where(lane < 64, 0.0, 1.0).astype(BF)]

    def attend(img):
        rows, wide_rows = pl.ds(IMG * img, IMG), pl.ds(IMG * img, 256)

        def pair(pr):
            c = ds(128 * pr, 128)
            q2, k2, v2 = q[wide_rows, c], k[rows, c], v[rows, c]
            vt = v2.T
            b2 = jnp.concatenate([bias[img], bias[img]], axis=1)
            got = []
            for h in range(2):
                st = nt(k2, q2 * heads[h]) + b2
                e = jnp.exp(st - jnp.max(st, axis=0, keepdims=True))
                p = (e * (1.0 / jnp.sum(e, axis=0, keepdims=True))).astype(BF)
                pb[img % 2, 2 * pr + h] = p
                got.append(nn(vt[64 * h : 64 * h + 64, :], p).astype(BF))
            o = jnp.concatenate(got, axis=0).T
            att[rows, c] = o[0:IMG, :]

        blocks(6, pair)

    saves = []
    for img in range(4):
        if img >= 2:
            saves[img - 2].wait()
        attend(img)
        if img < 2:
            c = pltpu.make_async_copy(pb.at[img], spill.at[img], lsem.at[img])
            c.start()
            saves.append(c)
        tick()

    res[...] = tok[...].astype(F32) + nn(att[0:R, :], wide(WA, 3))
    tick()

    def norm_two(block):
        rows = ds(32 * block, 32)
        g, b = gain(1)
        xh, r = whiten(res[rows, :])
        xh2[rows, :] = xh.astype(BF)
        r2[rows, :] = r
        nrm[rows, :] = (xh * g + b).astype(BF)

    blocks(R // 32, norm_two)
    tick()
    todo.finish({"u"})
    for ch in range(4):
        acc[...] = nn(nrm[...], wide(WU, ch))

        def activate(n, ch=ch):
            l, rows = n // 26, n % 26
            u = acc[ds(32 * rows, 32), ds(128 * l, 128)]
            a, d = gelu_parts(u)
            act[ds(R * (6 * ch + l) + 32 * rows, 32), :] = a.astype(BF)
            gel[ds(R * (6 * ch + l) + 32 * rows, 32), :] = d.astype(BF)

        blocks(6 * 26, activate, unroll=2)
        tick()
    todo.finish({"d"})
    for y in range(4):
        res[...] += nn(flat(act, y), tall(WD, y))
        tick()

    def pooling(img):
        g, b = gain(2)

        def logits(n):
            xh, _ = whiten(res[ds(IMG * img + 16 * n, 16, 16), :])
            fin = xh * g + b
            share[ds(16 * n, 16), img : img + 1] = jnp.sum(fin * query(), axis=-1, keepdims=True) / ROOT

        blocks(IMG // 16, logits)
        lg = jnp.where(mcol[0:IMG, img : img + 1] > 0, share[0:IMG, img : img + 1], -1e30)
        e = jnp.exp(lg - jnp.max(lg, axis=0, keepdims=True))
        share[0:IMG, img : img + 1] = e / jnp.sum(e, axis=0, keepdims=True)

        def collect(n, total):
            xh, _ = whiten(res[ds(IMG * img + 16 * n, 16, 16), :])
            fin = xh * g + b
            return total + fold(share[ds(16 * n, 16), img : img + 1] * fin)

        total = lax.fori_loop(0, IMG // 16, collect, jnp.zeros((8, D), F32))
        pool[img : img + 1, :] = jnp.sum(total, axis=0, keepdims=True)

    for img in range(4):
        pooling(img)
    todo.finish()
    link.drain()

    def proj_cols(x, lo):
        at = [
            WP.load(core, lo, 32, x=x, y=y, z=z)
            for y in range(4) for core in range(2) for z in range(4)
        ]
        return jnp.concatenate(at, axis=0)

    pooled = pool[...].astype(BF)
    padded = jnp.concatenate(
        [nn(pooled[:, 384 * n : 384 * n + 384], e3[...]).astype(BF) for n in range(2)], axis=1
    )
    embedded = jnp.concatenate([nn(padded, proj_cols(x, 0)) for x in range(4)], axis=1)
    ri = lax.rsqrt(jnp.sum(embedded * embedded, axis=-1, keepdims=True) + 1e-06)
    unit = (embedded * ri).astype(BF)
    big = jnp.exp(jnp.full((1, 1), scale[0], F32))
    dots = nt(unit[:, 0:128], proj_cols(0, 32))
    for x in range(1, 4):
        dots = dots + nt(unit[:, 128 * x : 128 * x + 128], proj_cols(x, 32))
    logits = big * dots
    row = lax.broadcasted_iota(jnp.int32, (8, 1024), 0)
    col = lax.broadcasted_iota(jnp.int32, (8, 1024), 1)
    valid = (row < 4) & ((col & 7) < 4)
    target = jnp.zeros((8, 1024), F32)
    first = 4 * ((me.y * 2 + me.core) * 16 + me.z * 4 + me.x)
    for i in range(4):
        t = pairing[first + i]
        target = jnp.where((row == i) & (col == 8 * (t >> 2) + (t & 3)), 1.0, target)
    e = jnp.where(valid, jnp.exp(logits), 0.0)
    row_sum = jnp.where(row[:, 0:1] < 4, jnp.sum(e, axis=-1, keepdims=True), 1.0)
    col_sum = jnp.sum(e, axis=0, keepdims=True)
    for j in range(8):
        cs[j : j + 1, :] = col_sum[:, 128 * j : 128 * j + 128]
    rows_lse = jnp.sum(jnp.log(row_sum), axis=0, keepdims=True)
    matched = jnp.sum(jnp.sum(logits * target, axis=-1, keepdims=True), axis=0, keepdims=True)
    send_tile = cs[...]
    send_tile = jnp.where((subs == 0) & (lanes == 4), rows_lse, send_tile)
    send_tile = jnp.where((subs == 0) & (lanes == 5), matched, send_tile)
    cs[...] = send_tile
    got = []
    for n in range(1, 16):
        t, peer = me.v_peer(n)
        got.append(link.copy(cs, crx.at[me.v], peer))
    crx[me.v] = send_tile
    for c in got:
        c.wait_recv()
    total = crx[0]
    for n in range(1, 16):
        total = total + crx[n]
    cst[...] = total
    got = []
    for n in range(1, 8):
        t, peer = me.s_peer(n)
        got.append(link.copy(cst, crx2.at[s], peer))
    crx2[s] = total
    for c in got:
        c.wait_recv()
    total = crx2[0]
    for n in range(1, 8):
        total = total + crx2[n]
    cs_all = jnp.concatenate([total[j : j + 1, :] for j in range(8)], axis=1)
    ok = (lanes & 7) < 4
    cols_lse = jnp.sum(jnp.where(ok, jnp.log(jnp.where(ok, total, 1.0)), 0.0))
    loss = (total[0:1, 4:5] + cols_lse - 2.0 * total[0:1, 5:6]) / 1024.0
    o_loss[...] = jnp.broadcast_to(loss, (8, 128))
    ok = (col[0:1, :] & 7) < 4
    gl = e / row_sum + e / jnp.where(ok, cs_all, 1.0) - 2.0 * target
    gl = jnp.where(valid, gl, 0.0) * (1.0 / 1024.0)
    g_scale = jnp.sum(gl * logits)
    parts = split(gl, 2)
    gui = []
    for x in range(4):
        rhs = proj_cols(x, 32)
        gui.append(nn(parts[0], rhs) + nn(parts[1], rhs))
    gui = big * jnp.concatenate(gui, axis=1)
    ge = ri * gui - ri * ri * ri * embedded * jnp.sum(embedded * gui, axis=-1, keepdims=True)
    ge = ge.astype(BF)
    gp_pad = jnp.concatenate(
        [
            sum(nt(ge[:, 128 * x : 128 * x + 128], proj_cols(x, 0)) for x in range(4))
        ], axis=1
    )
    gp = []
    for n in range(2):
        gp.append(sum(nt(p, e3[...]) for p in split(gp_pad[:, 512 * n : 512 * n + 512], 3)))
    emb[...] = jnp.concatenate(gp, axis=1)
    both = jnp.concatenate([parts[0], parts[1]], axis=0)
    ub = jnp.concatenate([unit, unit], axis=0)
    for x in range(4):
        gproj = tn(padded, ge[:, 128 * x : 128 * x + 128]).astype(BF)
        gtext = (big * tn(both, ub[:, 128 * x : 128 * x + 128])).astype(BF)
        n = 0
        for y in range(4):
            for core in range(2):
                for z in range(4):
                    WP.store(gproj[32 * n : 32 * n + 32, :], core, 0, x=x, y=y, z=z)
                    WP.store(gtext[32 * n : 32 * n + 32, :], core, 32, x=x, y=y, z=z)
                    n += 1

    def keep(n, c):
        def finish(total):
            tot[n, :, 128 * c : 128 * c + 128] = total

        return finish

    def keep_p(total):
        ptot[...] = total

    def rx_part(ref, c, n):
        return ref.at[pl.ds(n * c, n)]

    todo.add("p", scatter_steps(me, link, WP, rxpc, rxp, keep_p))
    tick()

    def pooling_back(img):
        g, b = gain(2)
        gpi = emb[img : img + 1, :]

        def weigh(n):
            xh, _ = whiten(res[ds(IMG * img + 16 * n, 16, 16), :])
            fin = xh * g + b
            dlc[ds(16 * n, 16), 0:1] = jnp.sum(fin * gpi, axis=-1, keepdims=True)

        blocks(IMG // 16, weigh)
        sh, c = share[0:IMG, img : img + 1], dlc[0:IMG, 0:1]
        dlc[0:IMG, 0:1] = sh * (c - jnp.sum(sh * c, axis=0, keepdims=True))

        def back(n, carry):
            gg, gs, gq = carry
            rows = ds(IMG * img + 16 * n, 16, 16)
            xh, r = whiten(res[rows, :])
            fin = xh * g + b
            sh, dl = share[ds(16 * n, 16), img : img + 1], dlc[ds(16 * n, 16), 0:1]
            gf = sh * gpi + dl * (query() / ROOT)
            out = whiten_back(gf * g, xh, r)
            res[rows, :] = out
            gb[rows, :] = out.astype(BF)
            return gg + fold(gf * xh), gs + fold(gf), gq + fold(dl * fin)

        zero = jnp.zeros((8, D), F32)
        gg, gs, gq = lax.fori_loop(0, IMG // 16, back, (zero, zero, zero))
        gvec[4] += gg
        gvec[5] += gs
        gvec[6] += gq * (1.0 / ROOT)

    for img in range(4):
        pooling_back(img)
    tick()

    for y in range(4):
        acc[...] = nt(gb[...], tall(WD, y))

        def activate_back(n, y=y):
            l, rows = n // 26, n % 26
            at = ds(R * (6 * y + l) + 32 * rows, 32)
            gel[at, :] = (acc[ds(32 * rows, 32), ds(128 * l, 128)] * gel[at, :].astype(F32)).astype(BF)

        blocks(6 * 26, activate_back, unroll=2)
        tall_store(WD, y, tn(flat(act, y), gb[...]).astype(BF))
        tick()
    for c in range(3):
        todo.add("d", scatter_steps(me, link, WD[c], rx_part(rxc, c, 3072), rx_part(rxd, c, 3024), keep(0, c), give=credit.at[c]))
    tick()
    for ch in range(4):
        gu = flat(gel, ch)
        part = nt(gu, wide(WU, ch))
        if ch == 0:
            acc[...] = part
        else:
            acc[...] += part
        wide_store(WU, ch, tn(nrm[...], gu).astype(BF))
        tick()
    for c in range(3):
        todo.add("u", scatter_steps(me, link, WU[c], rx_part(rxc, 3 + c, 3072), rx_part(rxu, c, 3024), keep(1, c)))
    tick()

    def norm_two_back(n, carry):
        gg, gs = carry
        g, _ = gain(1)
        rows = ds(16 * n, 16)
        y, xh = acc[rows, :], xh2[rows, :].astype(F32)
        out = res[rows, :] + whiten_back(y * g, xh, r2[rows, :])
        res[rows, :] = out
        gb[rows, :] = out.astype(BF)
        return gg + fold(y * xh), gs + fold(y)

    zero = jnp.zeros((8, D), F32)
    gg, gs = lax.fori_loop(0, R // 16, norm_two_back, (zero, zero))
    gvec[2] += gg
    gvec[3] += gs
    tick()

    wide_store(GA, 3, tn(att[0:R, :], gb[...]).astype(BF))
    att[0:R, :] = nt(gb[...], wide(WA, 3)).astype(BF)
    blocks(R // 32, norm_one)
    tick()
    low = lax.broadcasted_iota(jnp.int32, (256, 128), 0) < IMG
    side = lax.broadcasted_iota(jnp.int32, (256, 128), 1) < 64
    own = [jnp.where(low & side, 1.0, 0.0).astype(BF), jnp.where(low & ~side, 1.0, 0.0).astype(BF)]

    def attend_back(img):
        rows, wide_rows = pl.ds(IMG * img, IMG), pl.ds(IMG * img, 256)

        def pair(pr):
            c = ds(128 * pr, 128)
            q2, k2, v2, do = q[wide_rows, c], k[rows, c], v[rows, c], att[wide_rows, c]
            kt = k2.T
            dqt = []
            dk = jnp.zeros((IMG, 128), F32)
            dv = jnp.zeros((IMG, 128), F32)
            for h in range(2):
                doh, qh = do * own[h], q2 * heads[h]
                p = pb[img % 2, 2 * pr + h]
                dv = dv + nn(p, doh)
                pf = p.astype(F32)
                dp = nt(v2, doh)
                t = pf * dp
                dst = (t - pf * jnp.sum(t, axis=0, keepdims=True)).astype(BF)
                dk = dk + nn(dst, qh)
                dqt.append(nn(kt[64 * h : 64 * h + 64, :], dst))
            dq = (jnp.concatenate(dqt, axis=0) * 0.125).astype(BF).T
            q[rows, c] = dq[0:IMG, :]
            k[rows, c] = dk.astype(BF)
            v[rows, c] = dv.astype(BF)

        blocks(6, pair)

    loads = {}
    for img in (2, 3, 0, 1):
        if img in loads:
            loads[img].wait()
        attend_back(img)
        if img >= 2:
            c = pltpu.make_async_copy(spill.at[img - 2], pb.at[img - 2], lsem.at[img])
            c.start()
            loads[img - 2] = c
        tick()
    for ch, src in enumerate((q, k, v)):
        wide_store(GA, ch, tn(nrm[...], src[0:R, :]).astype(BF))
        tick()
    for c in range(3):
        todo.add("a", scatter_steps(me, link, GA[c], rx_part(rxc, c, 3072), rx_part(rxa, c, 3024), keep(2, c), need=credit.at[c]))
    todo.finish({"d"})
    tick()
    for ch, src in enumerate((q, k, v)):
        part = nt(src[0:R, :], wide(WA, ch))
        if ch == 0:
            acc[...] = part
        else:
            acc[...] += part
        tick()

    def norm_one_back(n, carry):
        gg, gs = carry
        g, _ = gain(0)
        rows = ds(16 * n, 16)
        xh, r = whiten(tok[rows, :].astype(F32))
        y = acc[rows, :]
        res[rows, :] = res[rows, :] + whiten_back(y * g, xh, r)
        return gg + fold(y * xh), gs + fold(y)

    gg, gs = lax.fori_loop(0, R // 16, norm_one_back, (zero, zero))
    gvec[0] += gg
    gvec[1] += gs
    outs = []
    for img in range(4):
        c = pltpu.make_async_copy(res.at[pl.ds(IMG * img, 200)], o_tok.at[img], lsem.at[4 + img])
        c.start()
        outs.append(c)

    for n in range(7):
        vec[n : n + 1, :] = jnp.sum(gvec[n], axis=0, keepdims=True)
    vec[7:8, :] = jnp.zeros((1, D), F32)
    for n in range(16):
        t, off = 48 * n // 128, 48 * n % 128
        part = vec[:, 128 * t : 128 * t + 128]
        part = pltpu.roll(part, (128 - off) % 128, 1) if off else part
        if off > 80:
            more = pltpu.roll(vec[:, 128 * t + 128 : 128 * t + 256], 128 - off, 1)
            part = jnp.where(lanes < 128 - off, part, more)
        gst2[n] = jnp.where(subs == 7, g_scale, part)
    cv = []
    for n in range(1, 16):
        t, peer = me.v_peer(n)
        cv.append(link.copy(gst2.at[t], grx.at[me.v], peer))
    grx[me.v] = gst2[me.v]
    todo.finish()
    for c in cv:
        c.wait_recv()
    total = grx[0]
    for n in range(1, 16):
        total = total + grx[n]
    vst[...] = total
    got = []
    for n in range(1, 8):
        t, peer = me.s_peer(n)
        got.append(link.copy(vst, grx2.at[s], peer))
    grx2[s] = total
    for n in (1, 2):
        for j in range(8):
            ust[n - 1, j] = tot[n, 6 * j : 6 * j + 6, :]
        for m in range(1, 8):
            t, peer = me.s_peer(m)
            got.append(link.copy(ust.at[n - 1, t], orx.at[n - 1, s], peer))
        orx[n - 1, s] = ust[n - 1, s]
    drx2 = tot.at[3]
    got.append(
        link.copy(
            tot.at[0, ds(24 * (1 - odd), 24, 8)],
            drx2.at[ds(24 * odd, 24, 8)],
            me.dev(x=me.x + 1 - 2 * odd),
        )
    )
    tot[3, ds(24 * odd, 24, 8), :] = tot[0, ds(24 * odd, 24, 8), :]
    for j in range(4):
        pst[j, 0:8] = ptot[8 * j : 8 * j + 8, :]
        pst[j, 8:16] = ptot[32 + 8 * j : 40 + 8 * j, :]
    for n in range(1, 4):
        t = (me.x + n) % 4
        got.append(link.copy(pst.at[t], prx2.at[me.x], me.dev(x=t)))
    prx2[me.x] = pst[me.x]
    for c in got:
        c.wait_recv()
    total = grx2[0]
    for n in range(1, 8):
        total = total + grx2[n]
    o_vec[...] = pltpu.roll(total, (128 - 6 * s) % 128, 1)
    o_scale[...] = total
    for j in range(8):
        o_up[:, 384 * j : 384 * j + 384] = orx[0, j]
        if j < 6:
            o_qkv[:, 384 * j : 384 * j + 384] = orx[1, j]
        else:
            o_out[:, 384 * (j - 6) : 384 * (j - 6) + 384] = orx[1, j]
    for j in range(2):
        o_down[:, 384 * j : 384 * j + 384] = tot[3, 24 * j : 24 * j + 24, :]
    for j in range(4):
        o_proj[:, 128 * j : 128 * j + 128] = prx2[j, 0:6]
    gt = jnp.concatenate([prx2[j, 8:12] for j in range(4)], axis=1)
    txt = text[...]
    r = lax.rsqrt(jnp.sum(txt * txt, axis=-1, keepdims=True) + 1e-06)
    o_text[...] = r * gt - r * r * r * txt * jnp.sum(txt * gt, axis=-1, keepdims=True)
    for c in outs:
        c.wait()
    link.drain()


def shards(tokens, keep_mask, pairing, text_vectors, logit_scale, w_qkv, w_out, w_up, w_down, w_proj, *vectors):
    padded = jnp.pad(tokens.reshape(4, 196, D), ((0, 0), (0, IMG - 196), (0, 0))).reshape(R, D)
    vm = pl.BlockSpec(memory_space=pltpu.VMEM)
    sm = pl.BlockSpec(memory_space=pltpu.SMEM)
    hbm = pl.BlockSpec(memory_space=pl.ANY)
    S = jax.ShapeDtypeStruct
    V = pltpu.VMEM
    outs = pl.pallas_call(
        kernel,
        out_shape=[
            S((8, 128), F32), S((4, 200, D), F32), S((4, 512), F32), S((6, 2304), F32), S((6, 768), F32),
            S((6, 3072), F32), S((24, 768), F32), S((6, 512), F32), S((8, 128), F32), S((8, 128), F32),
            S((2, 12, IMG, 256), BF),
        ],
        in_specs=[sm] * 9 + [vm] * 8,
        out_specs=[vm, hbm, vm, vm, vm, vm, vm, vm, vm, vm, hbm],
        scratch_shapes=[
            V((18432, 128), BF), V((18432, 128), BF), V((18432, 128), BF), V((8192, 128), BF),
            V((R + 48, D), BF), V((R, D), BF), V((R, D), BF), V((2, 12, IMG, 256), BF),
            V((R, D), BF), V((R, D), BF), V((R + 48, D), BF), V((R, D), BF),
            V((24 * R, 128), BF), V((24 * R, 128), BF), V((R, D), F32), V((R, D), F32), V((R, 1), F32),
            V((6 * 3072, 128), BF), V((3 * 3024, 128), BF), V((3 * 3024, 128), BF), V((3 * 3024, 128), BF),
            V((4096, 128), BF), V((4032, 128), BF),
            V((6, 3072), F32), V((8, 6, 384), F32), V((8, 6, 384), F32), V((2, 24, 384), F32),
            V((16, 512), F32), V((4, 16, 128), F32), V((8, 8, 128), F32), V((8, 128), F32),
            V((48, 384), F32), V((64, 128), F32), V((8, D), F32), V((7, 8, D), F32),
            V((8, 256), F32), V((256, 8), F32), V((IMG, 8), F32), V((IMG, 8), F32), V((4, IMG, 128), F32),
            V((8, D), F32), V((384, 512), BF), V((8, D), F32),
            V((8, 128), F32), V((16, 8, 128), F32), V((8, 128), F32), V((8, 8, 128), F32),
            V((4, 48, 384), F32), V((64, 128), F32), V((2, 8, 6, 384), F32), V((2, 8, 6, 384), F32),
            V((4, 16, 128), F32), V((4, 16, 128), F32), V((16, 8, 128), F32), V((16, 8, 128), F32),
            V((16, 8, 128), F32), V((8, 8, 128), F32),
            pltpu.SemaphoreType.DMA((N_SEM,)), pltpu.SemaphoreType.DMA((N_SEM,)), pltpu.SemaphoreType.DMA((8,)),
            pltpu.SemaphoreType.REGULAR((3,)),
        ],
        compiler_params=pltpu.CompilerParams(
            collective_id=0, has_side_effects=True, vmem_limit_bytes=(64 << 20) - (256 << 10)
        ),
        cost_estimate=pl.CostEstimate(flops=40_000_000_000, bytes_accessed=20_000_000, transcendentals=0),
    )(pairing, logit_scale, *vectors, padded, keep_mask, text_vectors, w_qkv, w_out, w_up, w_down, w_proj)
    loss, g_tok, g_text, g_qkv, g_out, g_up, g_down, g_proj, g_vec, g_scale, _ = outs
    return (
        loss[0, 0:1],
        g_tok[:, 0:196].reshape(784, D),
        g_text, g_qkv, g_out, g_up, g_down, g_proj,
        *[g_vec[n, 0:6] for n in range(7)],
        g_scale[7, 0:1],
    )


def solution(mesh):
    rows, vector, whole = P(("dp", "fsdp"), None), P(("dp", "fsdp")), P()
    in_specs = (rows, rows, whole, rows, whole, *[rows] * 5, *[vector] * 7)
    out_specs = (whole, rows, rows, *[rows] * 5, *[vector] * 7, whole)
    return jax.shard_map(shards, mesh=mesh, in_specs=in_specs, out_specs=out_specs, check_vma=False)
```

```python
from functools import partial
import math

import jax
import jax.numpy as jnp
from jax import lax
from jax.experimental import pallas as pl
from jax.experimental.pallas import tpu as pltpu
from jax.sharding import PartitionSpec as P

MESH = pl.DeviceIdType.MESH
BF = jnp.bfloat16
F32 = jnp.float32
IMG = 208
R = 4 * IMG
D = 768
ROOT = math.sqrt(768.0)


class Place:
    def __init__(self):
        dp = lax.axis_index("dp")
        fs = lax.axis_index("fsdp")
        self.y, self.core = dp // 2, dp % 2
        self.z, self.x = fs // 4, fs % 4
        self.s = (self.z % 2) * 4 + self.x
        self.v = dp * 2 + self.z // 2

    def dev(self, **moved):
        at = dict(x=self.x, y=self.y, z=self.z, core=self.core)
        at.update(moved)
        return (at["y"] * 2 + at["core"], at["z"] * 4 + at["x"])

    def hop(self, dim, step):
        return self.dev(**{dim: (getattr(self, dim) + step + 4) % 4})

    def sibling(self):
        return self.dev(core=1 - self.core)

    def s_peer(self, k):
        t = (self.s + k) % 8
        return t, self.dev(z=(self.z // 2) * 2 + t // 4, x=t % 4)

    def v_peer(self, k):
        t = (self.v + k) % 16
        return t, (t // 2, ((t % 2) * 2 + self.z % 2) * 4 + self.x)


class Link:
    def __init__(self, send, recv):
        self.send, self.recv, self.n = send, recv, 0
        self.open = []

    def copy(self, src, dst, dev):
        k = self.n
        self.n += 1
        c = pltpu.make_async_remote_copy(
            src_ref=src,
            dst_ref=dst,
            send_sem=self.send.at[k],
            recv_sem=self.recv.at[k],
            device_id=dev,
            device_id_type=MESH,
        )
        c.start()
        self.open.append(c)
        return c

    def drain(self):
        for c in self.open:
            c.wait_send()
        self.open = []


ORDERS = (("x", "y", "z"), ("y", "z", "x"), ("z", "x", "y"))


def enter(me):
    sem = pltpu.get_barrier_semaphore()
    peers = []
    for n in range(1, 64):
        dx, dy, dz = n % 4, n // 4 % 4, n // 16
        if dx * dy * dz == 0:
            peers.append(me.dev(x=(me.x + dx) % 4, y=(me.y + dy) % 4, z=(me.z + dz) % 4))
    for n in range(8):
        peers.append(me.dev(y=(me.y + n % 4) % 4, z=(me.z + n // 4 * 2) % 4, core=1 - me.core))
    for p in peers:
        pl.semaphore_signal(sem, inc=1, device_id=p, device_id_type=MESH)
    pl.semaphore_wait(sem, len(peers))


def ds(start, size, unit=None):
    if isinstance(start, int):
        return pl.ds(start, size)
    return pl.ds(pl.multiple_of(start, unit or size), size)


class Pieces:
    def __init__(self, ref, base, order, rows):
        self.ref, self.base, self.order, self.rows = ref, base, order, rows

    def start(self, core, **at):
        d1, d2, d3 = (at[d] for d in self.order)
        return self.base + (((core * 4 + d3) * 4 + d2) * 4 + d1) * self.rows

    def piece(self, core, **at):
        return self.ref.at[ds(self.start(core, **at), self.rows, 16)]

    def load(self, core, lo=0, n=None, **at):
        return self.ref[pl.ds(self.start(core, **at) + lo, n or self.rows), :]

    def store(self, value, core, lo=0, **at):
        self.ref[pl.ds(self.start(core, **at) + lo, value.shape[0]), :] = value

    def block(self, core, stage, me, b):
        at = [getattr(me, d) for d in self.order]
        at[stage] = b
        for k in range(stage):
            at[k] = 0
        return self.start(core, **dict(zip(self.order, at))), self.rows * 4**stage


def rows_of(ref, block):
    return ref.at[ds(block[0], block[1], 16)]


def plane_peer(me, order, n):
    a, b = order[:2]
    i, j = (getattr(me, a) + n % 4) % 4, (getattr(me, b) + n // 4) % 4
    return {a: i, b: j}, me.dev(**{a: i, b: j})


def gather_steps(me, link, buf):
    ref, d = buf.ref, buf.order[2]
    i = getattr(me, d)

    def send(block, dev):
        return link.copy(rows_of(ref, block), rows_of(ref, block), dev)

    def block(b):
        return buf.block(me.core, 2, me, b)

    own = buf.block(me.core, 0, me, getattr(me, buf.order[0]))
    got = [send(own, plane_peer(me, buf.order, n)[1]) for n in range(1, 16)]
    yield
    for c in got:
        c.wait_recv()
    got = [(n, send(block(i), me.hop(d, n))) for n in (2, 1, 3)]
    sib = [send(block(i), me.sibling())]
    yield
    for n, c in got[1:] + got[:1]:
        c.wait_recv()
        sib.append(send(block((i + 4 - n) % 4), me.sibling()))
    yield
    for c in sib:
        c.wait_recv()


def add_rows(dst_ref, dst, *srcs):
    size = dst[1]
    step = 192 if size % 192 == 0 else 256

    def body(k, _):
        total = dst_ref[ds(dst[0] + k * step, step, 16), :].astype(F32)
        for ref, start in srcs:
            total = total + ref[ds(start + k * step, step, 16), :].astype(F32)
        dst_ref[ds(dst[0] + k * step, step, 16), :] = total.astype(BF)
        return 0

    if size == step:
        body(0, 0)
    else:
        lax.fori_loop(0, size // step, body, 0)


def scatter_steps(me, link, buf, rx_core, rx, finish, give=None, need=None):
    ref, rows, d = buf.ref, buf.rows, buf.order[2]
    i, size = getattr(me, d), 16 * buf.rows

    def block(b, core=me.core):
        return buf.block(core, 2, me, b)

    if need is not None:
        pl.semaphore_wait(need, 1)
    cores = {}
    for n in (2, 1, 3, 0):
        b = (i + n) % 4
        cores[n] = link.copy(rows_of(ref, block(b, 1 - me.core)), rows_of(rx_core, (b * size, size)), me.sibling())
    yield
    got = []
    for n in (2, 1, 3, 0):
        b = (i + n) % 4
        cores[n].wait_recv()
        add_rows(ref, block(b), (rx_core, b * size))
        if n:
            got.append(link.copy(rows_of(ref, block(b)), rows_of(rx, ((n - 1) * size, size)), me.hop(d, n)))
    if give is not None:
        pl.semaphore_signal(give, inc=1, device_id=me.sibling(), device_id_type=MESH)
    yield
    for c in got:
        c.wait_recv()
    add_rows(ref, block(i), (rx, 0), (rx, size), (rx, 2 * size))
    got = []
    for n in range(1, 16):
        at, peer = plane_peer(me, buf.order, n)
        src = (buf.start(me.core, **{**at, d: i}), rows)
        got.append(link.copy(rows_of(ref, src), rows_of(rx, (3 * size + (n - 1) * rows, rows)), peer))
    yield
    for c in got:
        c.wait_recv()
    own = buf.block(me.core, 0, me, getattr(me, buf.order[0]))
    total = ref[ds(own[0], rows, 16), :].astype(F32)
    for n in range(15):
        total = total + rx[pl.ds(3 * size + n * rows, rows), :].astype(F32)
    finish(total)


class Queue:
    def __init__(self):
        self.live = []

    def add(self, name, gen):
        self.live.append((name, gen))

    def step(self, names=None):
        keep = []
        for name, gen in self.live:
            if names is None or name in names:
                try:
                    next(gen)
                except StopIteration:
                    continue
            keep.append((name, gen))
        self.live = keep

    def finish(self, names=None):
        while any(names is None or n in names for n, _ in self.live):
            self.step(names)


def nn(a, b):
    return lax.dot_general(a, b, (((1,), (0,)), ((), ())), preferred_element_type=F32)


def nt(a, b):
    return lax.dot_general(a, b, (((1,), (1,)), ((), ())), preferred_element_type=F32)


def tn(a, b):
    return lax.dot_general(a, b, (((0,), (0,)), ((), ())), preferred_element_type=F32)


def whiten(x):
    centred = x - jnp.mean(x, axis=-1, keepdims=True)
    r = lax.rsqrt(jnp.mean(centred * centred, axis=-1, keepdims=True) + 1e-05)
    return centred * r, r


def whiten_back(y, xh, r):
    return r * (y - jnp.mean(y, axis=-1, keepdims=True) - xh * jnp.mean(y * xh, axis=-1, keepdims=True))


def fold(x):
    return jnp.sum(x.reshape(x.shape[0] // 8, 8, x.shape[1]), axis=0)


def split(x, parts):
    got = []
    for _ in range(parts):
        h = x.astype(BF)
        got.append(h)
        x = x - h.astype(F32)
    return got


def gelu_parts(u):
    a = jnp.abs(u)
    den = 1.0 + (0.3275911 * math.sqrt(0.5)) * a
    t = pl.reciprocal(den, approx=True)
    t = t * (2.0 - den * t)
    e = jnp.exp2((-0.5 * math.log2(math.e)) * (u * u))
    poly = t * (0.5 * 0.254829592 + t * (-0.5 * 0.284496736 + t * (0.5 * 1.421413741 + t * (-0.5 * 1.453152027 + t * (0.5 * 1.061405429)))))
    tail = poly * e
    phi = jnp.where(u < 0, tail, 1.0 - tail)
    return u * phi, phi + u * (e * (1.0 / math.sqrt(2.0 * math.pi)))


def blocks(n, body, unroll=1):
    lax.fori_loop(0, n, lambda k, c: (body(k), 0)[1], 0, unroll=unroll)


N_SEM = 600


def kernel(
    pairing, scale, v0, v1, v2, v3, v4, v5, v6,
    tokens, mask, text, w_qkv, w_out, w_up, w_down, w_proj,
    o_loss, o_tok, o_text, o_qkv, o_out, o_up, o_down, o_proj, o0, o1, o2, o3, o4, o5, o6, o_scale, spill,
    wa, wu, wd, wp, tok, q, k, v, pb, xh2, nrm, att, gb, act, gel, res, acc, r2,
    rxc, rxd, rxu, rxa, rxpc, rxp,
    aloc, arx, urx, drx, ploc, prx, vrx, vst, p48, p64, vec, gvec,
    mrow, mcol, cols, bias, pool, s1, e3, emb, scal, scal_s, cs, crx, cst, crx2,
    tot, ptot, orx, ust, pst, prx2, gst, grx, gst2, grx2,
    send, recv, lsem, credit,
):
    me = Place()
    link = Link(send, recv)
    todo = Queue()
    s = me.s
    lanes = lax.broadcasted_iota(jnp.int32, (8, 128), 1)
    subs = lax.broadcasted_iota(jnp.int32, (8, 128), 0)

    WA = [Pieces(wa, 6144 * c, ORDERS[c], 48) for c in range(3)]
    WU = [Pieces(wu, 6144 * c, ORDERS[c], 48) for c in range(3)]
    WD = [Pieces(wd, 6144 * c, ORDERS[c], 48) for c in range(3)]
    WP = Pieces(wp, 0, ORDERS[0], 64)
    GA = [Pieces(act, 6144 * c, ORDERS[c], 48) for c in range(3)]

    raw = pltpu.make_async_copy(tokens, gb.at[pl.ds(0, 784)], lsem.at[7])
    raw.start()

    aloc[:, 0:2304] = w_qkv[...]
    aloc[:, 2304:3072] = w_out[...]
    mine = jnp.zeros((8, 128), F32)
    for n, ref in enumerate((v0, v1, v2, v3, v4, v5, v6)):
        for e in range(6):
            mine = jnp.where((subs == n) & (lanes == e), ref[e], mine)
    vst[...] = mine.astype(BF).astype(F32)
    ploc[...] = jnp.zeros_like(ploc)
    ploc[0:6, :] = w_proj[...]
    txt = text[...]
    ploc[8:12, :] = txt * lax.rsqrt(jnp.sum(txt * txt, axis=-1, keepdims=True) + 1e-06)

    enter(me)
    got = {"a": [], "u": [], "v": []}
    for name, src, rx in (("a", aloc, arx), ("v", vst, vrx), ("u", w_up, urx)):
        for n in range(1, 8):
            t, peer = me.s_peer(n)
            part = src if name == "v" else src.at[:, ds(384 * t, 384, 128)]
            got[name].append(link.copy(part, rx.at[s], peer))
    odd = me.x % 2
    cp = []
    for n in range(1, 4):
        t = (me.x + n) % 4
        cp.append(link.copy(ploc.at[:, ds(128 * t, 128)], prx.at[me.x], me.dev(x=t)))
    cd = link.copy(
        w_down.at[:, ds(384 * (1 - odd), 384, 128)], drx.at[odd], me.dev(x=me.x + 1 - 2 * odd)
    )
    arx[s] = aloc[:, ds(384 * s, 384, 128)]
    urx[s] = w_up[:, ds(384 * s, 384, 128)]
    drx[odd] = w_down[:, ds(384 * odd, 384, 128)]
    prx[me.x] = ploc[:, ds(128 * me.x, 128)]
    vrx[s] = vst[...]
    here = dict(x=me.x, y=me.y, z=me.z)

    def launch(name, bufs, n):
        for c, b in enumerate(bufs):
            if n == 48:
                b.piece(me.core, **here)[...] = p48[:, 128 * c : 128 * c + 128].astype(BF)
            else:
                b.piece(me.core, **here)[...] = p64[...].astype(BF)
            todo.add(name, gather_steps(me, link, b))


    for c in got["a"]:
        c.wait_recv()
    for j in range(8):
        p48[6 * j : 6 * j + 6, :] = arx[j]
    launch("a", WA, 48)
    todo.step({"a"})

    for c in got["v"]:
        c.wait_recv()
    total = vrx[0]
    for j in range(1, 8):
        total = total + pltpu.roll(vrx[j], 6 * j, 1)
    gst[me.v] = total
    cv = []
    for n in range(1, 16):
        t, peer = me.v_peer(n)
        cv.append(link.copy(gst.at[me.v], gst.at[me.v], peer))
    for c in got["u"]:
        c.wait_recv()
    for j in range(8):
        p48[6 * j : 6 * j + 6, :] = urx[j]
    launch("u", WU, 48)
    todo.step({"u"})
    for c in cp:
        c.wait_recv()
    for j in range(4):
        p64[8 * j : 8 * j + 8, :] = prx[j, 0:8]
        p64[32 + 8 * j : 40 + 8 * j, :] = prx[j, 8:16]
    launch("p", [WP], 64)
    todo.step({"p"})
    cd.wait_recv()
    for j in range(2):
        p48[24 * j : 24 * j + 24, :] = drx[j]
    launch("d", WD, 48)
    todo.step({"d"})
    todo.step({"a"})


    mrow[...] = jnp.zeros_like(mrow)
    mrow[0:4, 0:196] = mask[...].astype(F32)
    mcol[...] = mrow[...].T
    for i in range(4):
        col = jnp.where(mcol[0:IMG, i : i + 1] > 0, 0.0, -1e30)
        bias[i] = jnp.broadcast_to(col, (IMG, 128))
    raw.wait()
    acc[0:784, :] = gb[0:784, :].astype(F32)
    acc[784:R, :] = jnp.zeros((R - 784, D), F32)
    for i in range(4):
        tok[IMG * i : IMG * i + IMG, :] = acc[196 * i : 196 * i + IMG, :].astype(BF)
    for ref in (q, att):
        ref[R : R + 48, :] = jnp.zeros((48, D), BF)
    pool[...] = jnp.zeros_like(pool)
    gvec[...] = jnp.zeros_like(gvec)
    row = lax.broadcasted_iota(jnp.int32, (384, 512), 0)
    col = lax.broadcasted_iota(jnp.int32, (384, 512), 1)
    e3[...] = jnp.where(((col >> 3) * 6 + (col & 7) == row) & ((col & 7) < 6), 1.0, 0.0).astype(BF)
    for c in cv:
        c.wait_recv()
    vec[...] = jnp.zeros_like(vec)
    for n in range(16):
        t, off = 48 * n // 128, 48 * n % 128
        part = pltpu.roll(gst[n], off, 1) if off else gst[n]
        if off <= 80:
            vec[:, 128 * t : 128 * t + 128] += part
        else:
            vec[:, 128 * t : 128 * t + 128] += jnp.where(lanes >= off, part, 0.0)
            vec[:, 128 * t + 128 : 128 * t + 256] += jnp.where(lanes < off, part, 0.0)

    def gain(n):
        return vec[2 * n : 2 * n + 1, :], vec[2 * n + 1 : 2 * n + 2, :]

    def query():
        return vec[6:7, :]

    def tick(*names):
        for name in names:
            todo.step({name})

    def norm_one():
        g, b = gain(0)
        for i in range(4):
            rows = pl.ds(IMG * i, IMG)
            xh, _ = whiten(tok[rows, :].astype(F32))
            nrm[rows, :] = (xh * g + b).astype(BF)

    norm_one()


    def wide(bufs, ch):
        zlo, xp = ch // 2, ch % 2
        cols = []
        for l in range(6):
            at = [
                bufs[l % 3].load(core, x=2 * xp + l // 3, y=y, z=2 * h + zlo)
                for y in range(4) for core in range(2) for h in range(2)
            ]
            cols.append(jnp.concatenate(at, axis=0))
        return jnp.concatenate(cols, axis=1)

    def wide_store(bufs, ch, value):
        zlo, xp = ch // 2, ch % 2
        for l in range(6):
            n = 0
            for y in range(4):
                for core in range(2):
                    for h in range(2):
                        part = value[48 * n : 48 * n + 48, 128 * l : 128 * l + 128]
                        bufs[l % 3].store(part, core, x=2 * xp + l // 3, y=y, z=2 * h + zlo)
                        n += 1

    def tall(bufs, y):
        cols = []
        for l in range(6):
            at = [
                bufs[l % 3].load(core, x=2 * xh + l // 3, y=y, z=z)
                for core in range(2) for z in range(4) for xh in range(2)
            ]
            cols.append(jnp.concatenate(at, axis=0))
        return jnp.concatenate(cols, axis=1)

    def tall_store(bufs, y, value):
        for l in range(6):
            n = 0
            for core in range(2):
                for z in range(4):
                    for xh in range(2):
                        part = value[48 * n : 48 * n + 48, 128 * l : 128 * l + 128]
                        bufs[l % 3].store(part, core, x=2 * xh + l // 3, y=y, z=z)
                        n += 1

    def flat(ref, ch, rows=None):
        return jnp.concatenate([ref[R * (6 * ch + l) : R * (6 * ch + l) + R, :] for l in range(6)], axis=1)

    tick("a", "u", "p", "d")
    todo.finish({"a"})
    for ch, dst in enumerate((q, k, v)):
        out = nn(nrm[...], wide(WA, ch))
        if ch == 0:
            out = out * 0.125
        dst[0:R, :] = out.astype(BF)

    lane = lax.broadcasted_iota(jnp.int32, (1, 128), 1)
    heads = [jnp.where(lane < 64, 1.0, 0.0).astype(BF), jnp.where(lane < 64, 0.0, 1.0).astype(BF)]

    def attend(img):
        rows, wide_rows = pl.ds(IMG * img, IMG), pl.ds(IMG * img, 256)

        def pair(pr):
            c = ds(128 * pr, 128)
            q2, k2, v2 = q[wide_rows, c], k[rows, c], v[rows, c]
            vt = v2.T
            b2 = jnp.concatenate([bias[img], bias[img]], axis=1)
            got = []
            for h in range(2):
                st = nt(k2, q2 * heads[h]) + b2
                e = jnp.exp(st - jnp.max(st, axis=0, keepdims=True))
                p = (e * (1.0 / jnp.sum(e, axis=0, keepdims=True))).astype(BF)
                pb[img % 2, 2 * pr + h] = p
                got.append(nn(vt[64 * h : 64 * h + 64, :], p).astype(BF))
            o = jnp.concatenate(got, axis=0).T
            att[rows, c] = o[0:IMG, :]

        for pr in range(6):
            pair(pr)

    saves = []
    for img in range(4):
        if img >= 2:
            saves[img - 2].wait()
        attend(img)
        if img < 2:
            c = pltpu.make_async_copy(pb.at[img], spill.at[img], lsem.at[img])
            c.start()
            saves.append(c)
        if img == 0:
            tick("u")
        if img == 2:
            tick("p", "d")


    res[...] = tok[...].astype(F32) + nn(att[0:R, :], wide(WA, 3))


    g, b = gain(1)
    for i in range(4):
        rows = pl.ds(IMG * i, IMG)
        xh, r = whiten(res[rows, :])
        xh2[rows, :] = xh.astype(BF)
        r2[rows, :] = r
        nrm[rows, :] = (xh * g + b).astype(BF)

    todo.finish({"u"})
    for ch in range(4):
        a, d = gelu_parts(nn(nrm[...], wide(WU, ch)))
        for l in range(6):
            at = pl.ds(R * (6 * ch + l), R)
            act[at, :] = a[:, 128 * l : 128 * l + 128].astype(BF)
            gel[at, :] = d[:, 128 * l : 128 * l + 128].astype(BF)

    todo.finish({"d"})
    for y in range(4):
        res[...] += nn(flat(act, y), tall(WD, y))


    g, b = gain(2)
    for i in range(4):
        x = res[IMG * i : IMG * i + IMG, :]
        m = jnp.mean(x, axis=-1, keepdims=True)
        xc = x - m
        r = lax.rsqrt(jnp.mean(xc * xc, axis=-1, keepdims=True) + 1e-05)
        e = r * jnp.sum(xc * (g * query()), axis=-1, keepdims=True)
        lg = (e + jnp.sum(b * query(), axis=-1, keepdims=True)) / ROOT
        lg = jnp.where(mcol[0:IMG, i : i + 1] > 0, lg, -1e30)
        ex = jnp.exp(lg - jnp.max(lg, axis=0, keepdims=True))
        sh = ex / jnp.sum(ex, axis=0, keepdims=True)
        row = jnp.sum((sh * r) * xc, axis=0, keepdims=True)
        s1[i : i + 1, :] = row
        pool[i : i + 1, :] = row * g + b * jnp.sum(sh, axis=0, keepdims=True)
        for n, c in enumerate((m, r, e, sh)):
            cols[i, :, n : n + 1] = c
    todo.finish()
    link.drain()


    def proj_cols(x, lo):
        at = [
            WP.load(core, lo, 32, x=x, y=y, z=z)
            for y in range(4) for core in range(2) for z in range(4)
        ]
        return jnp.concatenate(at, axis=0)

    pooled = pool[...].astype(BF)
    padded = jnp.concatenate(
        [nn(pooled[:, 384 * n : 384 * n + 384], e3[...]).astype(BF) for n in range(2)], axis=1
    )
    embedded = jnp.concatenate([nn(padded, proj_cols(x, 0)) for x in range(4)], axis=1)
    ri = lax.rsqrt(jnp.sum(embedded * embedded, axis=-1, keepdims=True) + 1e-06)
    unit = (embedded * ri).astype(BF)
    big = jnp.exp(jnp.full((1, 1), scale[0], F32))
    dots = nt(unit[:, 0:128], proj_cols(0, 32))
    for x in range(1, 4):
        dots = dots + nt(unit[:, 128 * x : 128 * x + 128], proj_cols(x, 32))
    logits = big * dots
    row = lax.broadcasted_iota(jnp.int32, (8, 1024), 0)
    col = lax.broadcasted_iota(jnp.int32, (8, 1024), 1)
    valid = (row < 4) & ((col & 7) < 4)
    target = jnp.zeros((8, 1024), F32)
    first = 4 * ((me.y * 2 + me.core) * 16 + me.z * 4 + me.x)
    for i in range(4):
        t = pairing[first + i]
        target = jnp.where((row == i) & (col == 8 * (t >> 2) + (t & 3)), 1.0, target)
    e = jnp.where(valid, jnp.exp(logits), 0.0)
    row_sum = jnp.where(row[:, 0:1] < 4, jnp.sum(e, axis=-1, keepdims=True), 1.0)
    col_sum = jnp.sum(e, axis=0, keepdims=True)
    for j in range(8):
        cs[j : j + 1, :] = col_sum[:, 128 * j : 128 * j + 128]
    rows_lse = jnp.sum(jnp.log(row_sum), axis=0, keepdims=True)
    matched = jnp.sum(jnp.sum(logits * target, axis=-1, keepdims=True), axis=0, keepdims=True)
    send_tile = cs[...]
    send_tile = jnp.where((subs == 0) & (lanes == 4), rows_lse, send_tile)
    send_tile = jnp.where((subs == 0) & (lanes == 5), matched, send_tile)
    cs[...] = send_tile
    got = []
    for n in range(1, 16):
        t, peer = me.v_peer(n)
        got.append(link.copy(cs, crx.at[me.v], peer))
    crx[me.v] = send_tile
    for c in got:
        c.wait_recv()
    total = crx[0]
    for n in range(1, 16):
        total = total + crx[n]
    cst[...] = total
    got = []
    for n in range(1, 8):
        t, peer = me.s_peer(n)
        got.append(link.copy(cst, crx2.at[s], peer))
    crx2[s] = total
    for c in got:
        c.wait_recv()
    total = crx2[0]
    for n in range(1, 8):
        total = total + crx2[n]
    cs_all = jnp.concatenate([total[j : j + 1, :] for j in range(8)], axis=1)
    ok = (lanes & 7) < 4
    cols_lse = jnp.sum(jnp.where(ok, jnp.log(jnp.where(ok, total, 1.0)), 0.0))
    loss = (total[0:1, 4:5] + cols_lse - 2.0 * total[0:1, 5:6]) / 1024.0
    ok = (col[0:1, :] & 7) < 4
    gl = e / row_sum + e / jnp.where(ok, cs_all, 1.0) - 2.0 * target
    gl = jnp.where(valid, gl, 0.0) * (1.0 / 1024.0)
    g_scale = jnp.sum(gl * logits)
    parts = split(gl, 2)
    gui = []
    for x in range(4):
        rhs = proj_cols(x, 32)
        gui.append(nn(parts[0], rhs) + nn(parts[1], rhs))
    gui = big * jnp.concatenate(gui, axis=1)
    ge = ri * gui - ri * ri * ri * embedded * jnp.sum(embedded * gui, axis=-1, keepdims=True)
    ge = ge.astype(BF)
    gp_pad = jnp.concatenate(
        [
            sum(nt(ge[:, 128 * x : 128 * x + 128], proj_cols(x, 0)) for x in range(4))
        ], axis=1
    )
    gp = []
    for n in range(2):
        gp.append(sum(nt(p, e3[...]) for p in split(gp_pad[:, 512 * n : 512 * n + 512], 3)))
    emb[...] = jnp.concatenate(gp, axis=1)
    both = jnp.concatenate([parts[0], parts[1]], axis=0)
    ub = jnp.concatenate([unit, unit], axis=0)
    for x in range(4):
        gproj = tn(padded, ge[:, 128 * x : 128 * x + 128]).astype(BF)
        gtext = (big * tn(both, ub[:, 128 * x : 128 * x + 128])).astype(BF)
        n = 0
        for y in range(4):
            for core in range(2):
                for z in range(4):
                    WP.store(gproj[32 * n : 32 * n + 32, :], core, 0, x=x, y=y, z=z)
                    WP.store(gtext[32 * n : 32 * n + 32, :], core, 32, x=x, y=y, z=z)
                    n += 1

    def keep(n, c):
        def finish(total):
            tot[n, :, 128 * c : 128 * c + 128] = total

        return finish

    def keep_p(total):
        ptot[...] = total

    def rx_part(ref, c, n):
        return ref.at[pl.ds(n * c, n)]

    todo.add("p", scatter_steps(me, link, WP, rxpc, rxp, keep_p))
    tick("p")


    g, b = gain(2)
    side_q = query() / ROOT
    for i in range(4):
        rows = pl.ds(IMG * i, IMG)
        gpi = emb[i : i + 1, :]
        m, r, e, sh = (cols[i, :, n : n + 1] for n in range(4))
        one, two = gpi * g, side_q * g
        xc = res[rows, :] - m
        w = r * jnp.sum(xc * one, axis=-1, keepdims=True)
        c = w + jnp.sum(b * gpi, axis=-1, keepdims=True)
        dl = sh * (c - jnp.sum(sh * c, axis=0, keepdims=True))
        pull = r * r * (sh * w + dl * (e / ROOT)) * (1.0 / D)
        one_c = one - jnp.mean(one, axis=-1, keepdims=True)
        two_c = two - jnp.mean(two, axis=-1, keepdims=True)
        out = (r * sh) * one_c + (r * dl) * two_c - pull * xc
        res[rows, :] = out
        gb[rows, :] = out.astype(BF)
        row = jnp.sum((r * dl) * xc, axis=0, keepdims=True)
        sum_dl = jnp.sum(dl, axis=0, keepdims=True)
        gvec[4, 0:1, :] += gpi * s1[i : i + 1, :] + side_q * row
        gvec[5, 0:1, :] += gpi * jnp.sum(sh, axis=0, keepdims=True) + side_q * sum_dl
        gvec[6, 0:1, :] += (row * g + b * sum_dl) / ROOT

    for y in range(4):
        ga = nt(gb[...], tall(WD, y))
        for l in range(6):
            at = pl.ds(R * (6 * y + l), R)
            gel[at, :] = (ga[:, 128 * l : 128 * l + 128] * gel[at, :].astype(F32)).astype(BF)
        tall_store(WD, y, tn(flat(act, y), gb[...]).astype(BF))
        if y == 1 or y == 3:
            tick("p")

    for c in range(3):
        todo.add("d", scatter_steps(me, link, WD[c], rx_part(rxc, c, 3072), rx_part(rxd, c, 3024), keep(0, c), give=credit.at[c]))
    tick("d")
    for ch in range(4):
        gu = flat(gel, ch)
        part = nt(gu, wide(WU, ch))
        if ch == 0:
            acc[...] = part
        else:
            acc[...] += part
        wide_store(WU, ch, tn(nrm[...], gu).astype(BF))
        if ch == 0:
            tick("d")
        if ch == 3:
            tick("p")

    for c in range(3):
        todo.add("u", scatter_steps(me, link, WU[c], rx_part(rxc, c, 3072), rx_part(rxu, c, 3024), keep(1, c), give=credit.at[3 + c], need=credit.at[c]))
    tick("u")

    def fold_in(n, gg, gs):
        gvec[n] += gg
        gvec[n + 1] += gs

    g, _ = gain(1)
    for i in range(4):
        rows = pl.ds(IMG * i, IMG)
        y, xh = acc[rows, :], xh2[rows, :].astype(F32)
        out = res[rows, :] + whiten_back(y * g, xh, r2[rows, :])
        res[rows, :] = out
        gb[rows, :] = out.astype(BF)
        fold_in(2, fold(y * xh), fold(y))

    wide_store(GA, 3, tn(att[0:R, :], gb[...]).astype(BF))
    att[0:R, :] = nt(gb[...], wide(WA, 3)).astype(BF)
    norm_one()
    tick("d", "u")

    low = lax.broadcasted_iota(jnp.int32, (256, 128), 0) < IMG
    side = lax.broadcasted_iota(jnp.int32, (256, 128), 1) < 64
    own = [jnp.where(low & side, 1.0, 0.0).astype(BF), jnp.where(low & ~side, 1.0, 0.0).astype(BF)]

    def attend_back(img):
        rows, wide_rows = pl.ds(IMG * img, IMG), pl.ds(IMG * img, 256)

        def pair(pr):
            c = ds(128 * pr, 128)
            q2, k2, v2, do = q[wide_rows, c], k[rows, c], v[rows, c], att[wide_rows, c]
            kt = k2.T
            dqt = []
            dk = jnp.zeros((IMG, 128), F32)
            dv = jnp.zeros((IMG, 128), F32)
            for h in range(2):
                doh, qh = do * own[h], q2 * heads[h]
                p = pb[img % 2, 2 * pr + h]
                dv = dv + nn(p, doh)
                pf = p.astype(F32)
                dp = nt(v2, doh)
                t = pf * dp
                dst = (t - pf * jnp.sum(t, axis=0, keepdims=True)).astype(BF)
                dk = dk + nn(dst, qh)
                dqt.append(nn(kt[64 * h : 64 * h + 64, :], dst))
            dq = (jnp.concatenate(dqt, axis=0) * 0.125).astype(BF).T
            q[rows, c] = dq[0:IMG, :]
            k[rows, c] = dk.astype(BF)
            v[rows, c] = dv.astype(BF)

        for pr in range(6):
            pair(pr)

    loads = {}
    for img in (2, 3, 0, 1):
        if img in loads:
            loads[img].wait()
        attend_back(img)
        if img >= 2:
            c = pltpu.make_async_copy(spill.at[img - 2], pb.at[img - 2], lsem.at[img])
            c.start()
            loads[img - 2] = c
        if img == 2:
            tick("d")
        if img == 0:
            tick("u")

    for ch, src in enumerate((q, k, v)):
        wide_store(GA, ch, tn(nrm[...], src[0:R, :]).astype(BF))

    for c in range(3):
        todo.add("a", scatter_steps(me, link, GA[c], rx_part(rxc, c, 3072), rx_part(rxa, c, 3024), keep(2, c), need=credit.at[3 + c]))
    tick("a")
    for ch, src in enumerate((q, k, v)):
        part = nt(src[0:R, :], wide(WA, ch))
        if ch == 0:
            acc[...] = part
            tick("a")
        else:
            acc[...] += part

    g, _ = gain(0)
    outs = []
    for i in range(4):
        rows = pl.ds(IMG * i, IMG)
        xh, r = whiten(tok[rows, :].astype(F32))
        y = acc[rows, :]
        out = res[rows, :] + whiten_back(y * g, xh, r)
        fold_in(0, fold(y * xh), fold(y))
        acc[196 * i : 196 * i + 196, :] = out[0:196, :]
        if i % 2 == 1:
            rows = pl.ds(392 * (i // 2), 392)
            outs.append(pltpu.make_async_copy(acc.at[rows], o_tok.at[rows], lsem.at[4 + i // 2]))
            outs[-1].start()


    for n in range(7):
        vec[n : n + 1, :] = jnp.sum(gvec[n], axis=0, keepdims=True)
    vec[7:8, :] = jnp.zeros((1, D), F32)
    for n in range(16):
        t, off = 48 * n // 128, 48 * n % 128
        part = vec[:, 128 * t : 128 * t + 128]
        part = pltpu.roll(part, (128 - off) % 128, 1) if off else part
        if off > 80:
            more = pltpu.roll(vec[:, 128 * t + 128 : 128 * t + 256], 128 - off, 1)
            part = jnp.where(lanes < 128 - off, part, more)
        gst2[n] = jnp.where(subs == 7, g_scale, part)
    cv = []
    for n in range(1, 16):
        t, peer = me.v_peer(n)
        cv.append(link.copy(gst2.at[t], grx.at[me.v], peer))
    grx[me.v] = gst2[me.v]

    def own_rows(n):
        for j in range(8):
            ust[n - 1, j] = tot[n, 6 * j : 6 * j + 6, :]
        got = []
        for m in range(1, 8):
            t, peer = me.s_peer(m)
            got.append(link.copy(ust.at[n - 1, t], orx.at[n - 1, s], peer))
        orx[n - 1, s] = ust[n - 1, s]
        return got

    todo.finish({"p", "d", "u"})
    tick("a")
    got = own_rows(1)
    drx2 = tot.at[3]
    got.append(
        link.copy(
            tot.at[0, ds(24 * (1 - odd), 24, 8)],
            drx2.at[ds(24 * odd, 24, 8)],
            me.dev(x=me.x + 1 - 2 * odd),
        )
    )
    tot[3, ds(24 * odd, 24, 8), :] = tot[0, ds(24 * odd, 24, 8), :]
    for j in range(4):
        pst[j, 0:8] = ptot[8 * j : 8 * j + 8, :]
        pst[j, 8:16] = ptot[32 + 8 * j : 40 + 8 * j, :]
    for n in range(1, 4):
        t = (me.x + n) % 4
        got.append(link.copy(pst.at[t], prx2.at[me.x], me.dev(x=t)))
    prx2[me.x] = pst[me.x]
    for c in cv:
        c.wait_recv()
    total = grx[0]
    for n in range(1, 16):
        total = total + grx[n]
    vst[...] = total
    for n in range(1, 8):
        t, peer = me.s_peer(n)
        got.append(link.copy(vst, grx2.at[s], peer))
    grx2[s] = total
    todo.finish({"a"})
    last = own_rows(2)
    for c in got:
        c.wait_recv()
    total = grx2[0]
    for n in range(1, 8):
        total = total + grx2[n]
    total = pltpu.roll(total, (128 - 6 * s) % 128, 1)
    scal[...] = jnp.where((subs == 7) & (lanes == 1), loss, total)
    to_smem = pltpu.make_async_copy(scal, scal_s, lsem.at[6])
    to_smem.start()
    for j in range(8):
        o_up[:, 384 * j : 384 * j + 384] = orx[0, j]
    for j in range(2):
        o_down[:, 384 * j : 384 * j + 384] = tot[3, 24 * j : 24 * j + 24, :]
    for j in range(4):
        o_proj[:, 128 * j : 128 * j + 128] = prx2[j, 0:6]
    gt = jnp.concatenate([prx2[j, 8:12] for j in range(4)], axis=1)
    txt = text[...]
    r = lax.rsqrt(jnp.sum(txt * txt, axis=-1, keepdims=True) + 1e-06)
    o_text[...] = r * gt - r * r * r * txt * jnp.sum(txt * gt, axis=-1, keepdims=True)
    to_smem.wait()
    for n, ref in enumerate((o0, o1, o2, o3, o4, o5, o6)):
        for e in range(6):
            ref[e] = scal_s[n, e]
    o_scale[0] = scal_s[7, 0]
    o_loss[0] = scal_s[7, 1]
    for c in last:
        c.wait_recv()
    for j in range(8):
        if j < 6:
            o_qkv[:, 384 * j : 384 * j + 384] = orx[1, j]
        else:
            o_out[:, 384 * (j - 6) : 384 * (j - 6) + 384] = orx[1, j]
    for c in outs:
        c.wait()
    link.drain()


def shards(tokens, keep_mask, pairing, text_vectors, logit_scale, w_qkv, w_out, w_up, w_down, w_proj, *vectors):
    vm = pl.BlockSpec(memory_space=pltpu.VMEM)
    sm = pl.BlockSpec(memory_space=pltpu.SMEM)
    hbm = pl.BlockSpec(memory_space=pl.ANY)
    S = jax.ShapeDtypeStruct
    V = pltpu.VMEM
    outs = pl.pallas_call(
        kernel,
        out_shape=[
            S((1,), F32), S((784, D), F32), S((4, 512), F32), S((6, 2304), F32), S((6, 768), F32),
            S((6, 3072), F32), S((24, 768), F32), S((6, 512), F32), *[S((6,), F32)] * 7, S((1,), F32),
            S((2, 12, IMG, 256), BF),
        ],
        in_specs=[sm] * 9 + [hbm] + [vm] * 7,
        out_specs=[sm, hbm, vm, vm, vm, vm, vm, vm, *[sm] * 8, hbm],
        scratch_shapes=[
            V((18432, 128), BF), V((18432, 128), BF), V((18432, 128), BF), V((8192, 128), BF), V((R, D), BF),
            V((R + 48, D), BF), V((R, D), BF), V((R, D), BF), V((2, 12, IMG, 256), BF),
            V((R, D), BF), V((R, D), BF), V((R + 48, D), BF), V((R, D), BF),
            V((24 * R, 128), BF), V((24 * R, 128), BF), V((R, D), F32), V((R, D), F32), V((R, 1), F32),
            V((3 * 3072, 128), BF), V((3 * 3024, 128), BF), V((3 * 3024, 128), BF), V((3 * 3024, 128), BF),
            V((4096, 128), BF), V((4032, 128), BF),
            V((6, 3072), F32), V((8, 6, 384), F32), V((8, 6, 384), F32), V((2, 24, 384), F32),
            V((16, 512), F32), V((4, 16, 128), F32), V((8, 8, 128), F32), V((8, 128), F32),
            V((48, 384), F32), V((64, 128), F32), V((8, D), F32), V((7, 8, D), F32),
            V((8, 256), F32), V((256, 8), F32), V((4, IMG, 8), F32), V((4, IMG, 128), F32),
            V((8, D), F32), V((8, D), F32), V((384, 512), BF), V((8, D), F32),
            V((8, 128), F32), pltpu.SMEM((8, 128), F32),
            V((8, 128), F32), V((16, 8, 128), F32), V((8, 128), F32), V((8, 8, 128), F32),
            V((4, 48, 384), F32), V((64, 128), F32), V((2, 8, 6, 384), F32), V((2, 8, 6, 384), F32),
            V((4, 16, 128), F32), V((4, 16, 128), F32), V((16, 8, 128), F32), V((16, 8, 128), F32),
            V((16, 8, 128), F32), V((8, 8, 128), F32),
            pltpu.SemaphoreType.DMA((N_SEM,)), pltpu.SemaphoreType.DMA((N_SEM,)), pltpu.SemaphoreType.DMA((8,)),
            pltpu.SemaphoreType.REGULAR((6,)),
        ],
        compiler_params=pltpu.CompilerParams(
            collective_id=0, has_side_effects=True, vmem_limit_bytes=(64 << 20) - (256 << 10)
        ),
        cost_estimate=pl.CostEstimate(flops=40_000_000_000, bytes_accessed=20_000_000, transcendentals=0),
    )(pairing, logit_scale, *vectors, tokens, keep_mask, text_vectors, w_qkv, w_out, w_up, w_down, w_proj)
    return tuple(outs[:16])


def solution(mesh):
    rows, vector, whole = P(("dp", "fsdp"), None), P(("dp", "fsdp")), P()
    in_specs = (rows, rows, whole, rows, whole, *[rows] * 5, *[vector] * 7)
    out_specs = (whole, rows, rows, *[rows] * 5, *[vector] * 7, whole)
    return jax.shard_map(shards, mesh=mesh, in_specs=in_specs, out_specs=out_specs, check_vma=False)
```

```python
from functools import partial
import math

import jax
import jax.numpy as jnp
from jax import lax
from jax.experimental import pallas as pl
from jax.experimental.pallas import tpu as pltpu
from jax.sharding import PartitionSpec as P

MESH = pl.DeviceIdType.MESH
BF = jnp.bfloat16
F32 = jnp.float32
IMG = 208
R = 4 * IMG
D = 768
ROOT = math.sqrt(768.0)


class Place:
    def __init__(self):
        dp = lax.axis_index("dp")
        fs = lax.axis_index("fsdp")
        self.y, self.core = dp // 2, dp % 2
        self.z, self.x = fs // 4, fs % 4
        self.s = (self.z % 2) * 4 + self.x
        self.v = dp * 2 + self.z // 2

    def dev(self, **moved):
        at = dict(x=self.x, y=self.y, z=self.z, core=self.core)
        at.update(moved)
        return (at["y"] * 2 + at["core"], at["z"] * 4 + at["x"])

    def hop(self, dim, step):
        return self.dev(**{dim: (getattr(self, dim) + step + 4) % 4})

    def sibling(self):
        return self.dev(core=1 - self.core)

    def s_peer(self, k):
        t = (self.s + k) % 8
        return t, self.dev(z=(self.z // 2) * 2 + t // 4, x=t % 4)

    def v_peer(self, k):
        t = (self.v + k) % 16
        return t, (t // 2, ((t % 2) * 2 + self.z % 2) * 4 + self.x)


class Group:
    def __init__(self, link, total):
        self.link, self.total = link, total
        self.k = link.n
        link.n += 1
        link.open.append(self)
        self.sems = dict(send_sem=link.send.at[self.k], recv_sem=link.recv.at[self.k])

    def copy(self, src, dst, dev):
        c = pltpu.make_async_remote_copy(
            src_ref=src, dst_ref=dst, device_id=dev, device_id_type=MESH, **self.sems
        )
        c.start()

    def whole(self):
        return pltpu.make_async_remote_copy(
            src_ref=self.total,
            dst_ref=self.total,
            device_id=self.link.any_device,
            device_id_type=MESH,
            **self.sems,
        )

    def wait_recv(self):
        self.whole().wait_recv()


class Link:
    def __init__(self, send, recv, any_device):
        self.send, self.recv, self.n = send, recv, 0
        self.any_device = any_device
        self.open = []

    def group(self, total):
        return Group(self, total)

    def drain(self):
        for g in self.open:
            g.whole().wait_send()
        self.open = []


ORDERS = (("x", "y", "z"), ("y", "z", "x"), ("z", "x", "y"))


def enter(me):
    sem = pltpu.get_barrier_semaphore()
    peers = []
    for n in range(1, 64):
        dx, dy, dz = n % 4, n // 4 % 4, n // 16
        if dx * dy * dz == 0:
            peers.append(me.dev(x=(me.x + dx) % 4, y=(me.y + dy) % 4, z=(me.z + dz) % 4))
    for n in range(8):
        peers.append(me.dev(y=(me.y + n % 4) % 4, z=(me.z + n // 4 * 2) % 4, core=1 - me.core))
    for p in peers:
        pl.semaphore_signal(sem, inc=1, device_id=p, device_id_type=MESH)
    pl.semaphore_wait(sem, len(peers))


def ds(start, size, unit=None):
    if isinstance(start, int):
        return pl.ds(start, size)
    return pl.ds(pl.multiple_of(start, unit or size), size)


class Pieces:
    def __init__(self, ref, base, order, rows):
        self.ref, self.base, self.order, self.rows = ref, base, order, rows

    def start(self, core, **at):
        d1, d2, d3 = (at[d] for d in self.order)
        return self.base + (((core * 4 + d3) * 4 + d2) * 4 + d1) * self.rows

    def piece(self, core, **at):
        return self.ref.at[ds(self.start(core, **at), self.rows, 16)]

    def load(self, core, lo=0, n=None, **at):
        return self.ref[pl.ds(self.start(core, **at) + lo, n or self.rows), :]

    def store(self, value, core, lo=0, **at):
        self.ref[pl.ds(self.start(core, **at) + lo, value.shape[0]), :] = value

    def block(self, core, stage, me, b):
        at = [getattr(me, d) for d in self.order]
        at[stage] = b
        for k in range(stage):
            at[k] = 0
        return self.start(core, **dict(zip(self.order, at))), self.rows * 4**stage


def rows_of(ref, block):
    return ref.at[ds(block[0], block[1], 16)]


def plane_peer(me, order, n):
    a, b = order[:2]
    i, j = (getattr(me, a) + n % 4) % 4, (getattr(me, b) + n // 4) % 4
    return {a: i, b: j}, me.dev(**{a: i, b: j})


def cut(block, which):
    start, size = block
    return (start + which * (size // 2), size // 2)


def gather_steps(me, link, buf):
    ref, d, rows = buf.ref, buf.order[2], buf.rows
    i, size = getattr(me, d), 16 * buf.rows
    lo, hi, far = (i + 3) % 4, (i + 1) % 4, (i + 2) % 4
    right, left = me.hop(d, 1), me.hop(d, -1)

    def bytes_of(pieces):
        return ref.at[pl.ds(buf.base, pieces * rows)]

    def send(group, block, dev):
        group.copy(rows_of(ref, block), rows_of(ref, block), dev)

    def block(b):
        return buf.block(me.core, 2, me, b)

    own = buf.block(me.core, 0, me, getattr(me, buf.order[0]))
    plane = link.group(bytes_of(15))
    for n in range(1, 16):
        send(plane, own, plane_peer(me, buf.order, n)[1])
    yield
    plane.wait_recv()
    from_lo, from_hi = link.group(bytes_of(16)), link.group(bytes_of(16))
    send(from_lo, block(i), right)
    send(from_hi, block(i), left)
    sib = link.group(bytes_of(64))
    send(sib, block(i), me.sibling())
    yield
    from_lo.wait_recv()
    rest = link.group(bytes_of(16))
    send(rest, cut(block(lo), 0), right)
    from_hi.wait_recv()
    send(rest, cut(block(hi), 1), left)
    send(sib, block(lo), me.sibling())
    send(sib, block(hi), me.sibling())
    yield
    rest.wait_recv()
    send(sib, block(far), me.sibling())
    yield
    sib.wait_recv()


def add_rows(dst_ref, dst, *srcs):
    size = dst[1]
    step = next(n for n in (192, 128) if size % n == 0)

    def body(k, _):
        total = dst_ref[ds(dst[0] + k * step, step, 16), :].astype(F32)
        for ref, start in srcs:
            total = total + ref[ds(start + k * step, step, 16), :].astype(F32)
        dst_ref[ds(dst[0] + k * step, step, 16), :] = total.astype(BF)
        return 0

    if size == step:
        body(0, 0)
    else:
        lax.fori_loop(0, size // step, body, 0)


def scatter_steps(me, link, buf, rx_core, rx, finish, give=None, need=None):
    ref, rows, d = buf.ref, buf.rows, buf.order[2]
    i, size = getattr(me, d), 16 * buf.rows
    lo, hi, far = (i + 3) % 4, (i + 1) % 4, (i + 2) % 4
    right, left = me.hop(d, 1), me.hop(d, -1)

    def bytes_of(pieces):
        return ref.at[pl.ds(buf.base, pieces * rows)]

    def block(b, core=me.core):
        return buf.block(core, 2, me, b)

    def slot(n):
        return (n * size, size)

    if need is not None:
        pl.semaphore_wait(need, 1)
    core = link.group(bytes_of(64))
    for b in range(4):
        core.copy(rows_of(ref, block(b, 1 - me.core)), rows_of(rx_core, (b * size, size)), me.sibling())
    yield
    core.wait_recv()

    def settle(b):
        add_rows(ref, block(b), (rx_core, b * size))

    def send(group, src, dst, dev):
        group.copy(rows_of(ref, src), rows_of(rx, dst), dev)

    settle(far)
    merge = link.group(bytes_of(16))
    send(merge, cut(block(far), 0), cut(slot(0), 0), right)
    send(merge, cut(block(far), 1), cut(slot(0), 1), left)
    settle(hi)
    ends = link.group(bytes_of(32))
    send(ends, cut(block(hi), 1), cut(slot(1), 1), right)
    settle(lo)
    send(ends, cut(block(lo), 0), cut(slot(2), 0), left)
    settle(i)
    if give is not None:
        pl.semaphore_signal(give, inc=1, device_id=me.sibling(), device_id_type=MESH)
    yield
    merge.wait_recv()
    add_rows(ref, cut(block(hi), 0), (rx, cut(slot(0), 0)[0]))
    send(ends, cut(block(hi), 0), cut(slot(1), 0), right)
    add_rows(ref, cut(block(lo), 1), (rx, cut(slot(0), 1)[0]))
    send(ends, cut(block(lo), 1), cut(slot(2), 1), left)
    yield
    ends.wait_recv()
    add_rows(ref, block(i), (rx, size), (rx, 2 * size))
    plane = link.group(bytes_of(15))
    for n in range(1, 16):
        at, peer = plane_peer(me, buf.order, n)
        src = (buf.start(me.core, **{**at, d: i}), rows)
        send(plane, src, (3 * size + (n - 1) * rows, rows), peer)
    yield
    plane.wait_recv()
    own = buf.block(me.core, 0, me, getattr(me, buf.order[0]))
    total = ref[ds(own[0], rows, 16), :].astype(F32)
    for n in range(15):
        total = total + rx[pl.ds(3 * size + n * rows, rows), :].astype(F32)
    finish(total)


class Queue:
    def __init__(self):
        self.live = []

    def add(self, name, gen):
        self.live.append((name, gen))

    def step(self, names=None):
        keep = []
        for name, gen in self.live:
            if names is None or name in names:
                try:
                    next(gen)
                except StopIteration:
                    continue
            keep.append((name, gen))
        self.live = keep

    def finish(self, names=None):
        while any(names is None or n in names for n, _ in self.live):
            self.step(names)


def nn(a, b):
    return lax.dot_general(a, b, (((1,), (0,)), ((), ())), preferred_element_type=F32)


def nt(a, b):
    return lax.dot_general(a, b, (((1,), (1,)), ((), ())), preferred_element_type=F32)


def tn(a, b):
    return lax.dot_general(a, b, (((0,), (0,)), ((), ())), preferred_element_type=F32)


def whiten(x):
    centred = x - jnp.mean(x, axis=-1, keepdims=True)
    r = lax.rsqrt(jnp.mean(centred * centred, axis=-1, keepdims=True) + 1e-05)
    return centred * r, r


def whiten_back(y, xh, r):
    return r * (y - jnp.mean(y, axis=-1, keepdims=True) - xh * jnp.mean(y * xh, axis=-1, keepdims=True))


def fold(x):
    return jnp.sum(x.reshape(x.shape[0] // 8, 8, x.shape[1]), axis=0)


def split(x, parts):
    got = []
    for _ in range(parts):
        h = x.astype(BF)
        got.append(h)
        x = x - h.astype(F32)
    return got


def gelu_parts(u):
    a = jnp.abs(u)
    den = 1.0 + (0.3275911 * math.sqrt(0.5)) * a
    t = pltpu.reciprocal(den, approx=True)
    t = t * (2.0 - den * t)
    e = jnp.exp2((-0.5 * math.log2(math.e)) * (u * u))
    poly = t * (0.5 * 0.254829592 + t * (-0.5 * 0.284496736 + t * (0.5 * 1.421413741 + t * (-0.5 * 1.453152027 + t * (0.5 * 1.061405429)))))
    tail = poly * e
    phi = jnp.where(u < 0, tail, 1.0 - tail)
    return u * phi, phi + u * (e * (1.0 / math.sqrt(2.0 * math.pi)))


def blocks(n, body, unroll=1):
    lax.fori_loop(0, n, lambda k, c: (body(k), 0)[1], 0, unroll=unroll)


N_SEM = 112


def kernel(
    pairing, scale, v0, v1, v2, v3, v4, v5, v6,
    tokens, mask, text, w_qkv, w_out, w_up, w_down, w_proj,
    o_loss, o_tok, o_text, o_qkv, o_out, o_up, o_down, o_proj, o0, o1, o2, o3, o4, o5, o6, o_scale, spill,
    wa, wu, wd, wp, tok, q, k, v, pb, xh2, nrm, att, gb, act, gel, res, acc, r2,
    rxc, rxd, rxu, rxa, rxpc, rxp,
    aloc, arx, urx, drx, ploc, prx, vrx, vst, p48, p64, vec, gvec,
    mrow, mcol, cols, bias, pool, s1, e3, emb, scal, scal_s, cs, crx, cst, crx2,
    tot, ptot, orx, ust, pst, prx2, gst, grx, gst2, grx2,
    send, recv, lsem, credit,
):
    me = Place()
    link = Link(send, recv, me.sibling())
    todo = Queue()
    s = me.s
    lanes = lax.broadcasted_iota(jnp.int32, (8, 128), 1)
    subs = lax.broadcasted_iota(jnp.int32, (8, 128), 0)

    WA = [Pieces(wa, 6144 * c, ORDERS[c], 48) for c in range(3)]
    WU = [Pieces(wu, 6144 * c, ORDERS[c], 48) for c in range(3)]
    WD = [Pieces(wd, 6144 * c, ORDERS[c], 48) for c in range(3)]
    WP = Pieces(wp, 0, ORDERS[0], 64)
    GA = [Pieces(act, 6144 * c, ORDERS[c], 48) for c in range(3)]

    raw = pltpu.make_async_copy(tokens, gb.at[pl.ds(0, 784)], lsem.at[7])
    raw.start()
    aloc[:, 0:2304] = w_qkv[...]
    aloc[:, 2304:3072] = w_out[...]
    mine = jnp.zeros((8, 128), F32)
    for n, ref in enumerate((v0, v1, v2, v3, v4, v5, v6)):
        for e in range(6):
            mine = jnp.where((subs == n) & (lanes == e), ref[e], mine)
    vst[...] = mine.astype(BF).astype(F32)
    ploc[...] = jnp.zeros_like(ploc)
    ploc[0:6, :] = w_proj[...]
    txt = text[...]
    ploc[8:12, :] = txt * lax.rsqrt(jnp.sum(txt * txt, axis=-1, keepdims=True) + 1e-06)
    enter(me)
    firsts = {}
    for name, src, rx in (("a", aloc, arx), ("v", vst, vrx), ("u", w_up, urx)):
        firsts[name] = link.group(rx.at[pl.ds(0, 7)])
        for n in range(1, 8):
            t, peer = me.s_peer(n)
            part = src if name == "v" else src.at[:, ds(384 * t, 384, 128)]
            firsts[name].copy(part, rx.at[s], peer)
    odd = me.x % 2
    cp = link.group(prx.at[pl.ds(0, 3)])
    for n in range(1, 4):
        t = (me.x + n) % 4
        cp.copy(ploc.at[:, ds(128 * t, 128)], prx.at[me.x], me.dev(x=t))
    cd = link.group(drx.at[0])
    cd.copy(w_down.at[:, ds(384 * (1 - odd), 384, 128)], drx.at[odd], me.dev(x=me.x + 1 - 2 * odd))
    arx[s] = aloc[:, ds(384 * s, 384, 128)]
    urx[s] = w_up[:, ds(384 * s, 384, 128)]
    drx[odd] = w_down[:, ds(384 * odd, 384, 128)]
    prx[me.x] = ploc[:, ds(128 * me.x, 128)]
    vrx[s] = vst[...]
    here = dict(x=me.x, y=me.y, z=me.z)

    def launch(name, bufs, n):
        for c, b in enumerate(bufs):
            if n == 48:
                b.piece(me.core, **here)[...] = p48[:, 128 * c : 128 * c + 128].astype(BF)
            else:
                b.piece(me.core, **here)[...] = p64[...].astype(BF)
            todo.add(name, gather_steps(me, link, b))

    firsts["a"].wait_recv()
    for j in range(8):
        p48[6 * j : 6 * j + 6, :] = arx[j]
    launch("a", WA, 48)
    todo.step({"a"})
    firsts["v"].wait_recv()
    total = vrx[0]
    for j in range(1, 8):
        total = total + pltpu.roll(vrx[j], 6 * j, 1)
    gst[me.v] = total
    cv = link.group(gst.at[pl.ds(0, 15)])
    for n in range(1, 16):
        t, peer = me.v_peer(n)
        cv.copy(gst.at[me.v], gst.at[me.v], peer)
    firsts["u"].wait_recv()
    for j in range(8):
        p48[6 * j : 6 * j + 6, :] = urx[j]
    launch("u", WU, 48)
    todo.step({"u"})
    cp.wait_recv()
    for j in range(4):
        p64[8 * j : 8 * j + 8, :] = prx[j, 0:8]
        p64[32 + 8 * j : 40 + 8 * j, :] = prx[j, 8:16]
    launch("p", [WP], 64)
    todo.step({"p"})
    cd.wait_recv()
    for j in range(2):
        p48[24 * j : 24 * j + 24, :] = drx[j]
    launch("d", WD, 48)
    todo.step({"d"})
    todo.step({"a"})
    todo.step({"a"})
    todo.step({"u"})

    mrow[...] = jnp.zeros_like(mrow)
    mrow[0:4, 0:196] = mask[...].astype(F32)
    mcol[...] = mrow[...].T
    for i in range(4):
        col = jnp.where(mcol[0:IMG, i : i + 1] > 0, 0.0, -1e30)
        bias[i] = jnp.broadcast_to(col, (IMG, 128))
    raw.wait()
    acc[0:784, :] = gb[0:784, :].astype(F32)
    acc[784:R, :] = jnp.zeros((R - 784, D), F32)
    for i in range(4):
        tok[IMG * i : IMG * i + IMG, :] = acc[196 * i : 196 * i + IMG, :].astype(BF)
    for ref in (q, att):
        ref[R : R + 48, :] = jnp.zeros((48, D), BF)
    pool[...] = jnp.zeros_like(pool)
    gvec[...] = jnp.zeros_like(gvec)
    row = lax.broadcasted_iota(jnp.int32, (384, 512), 0)
    col = lax.broadcasted_iota(jnp.int32, (384, 512), 1)
    e3[...] = jnp.where(((col >> 3) * 6 + (col & 7) == row) & ((col & 7) < 6), 1.0, 0.0).astype(BF)
    cv.wait_recv()
    vec[...] = jnp.zeros_like(vec)
    for n in range(16):
        t, off = 48 * n // 128, 48 * n % 128
        part = pltpu.roll(gst[n], off, 1) if off else gst[n]
        if off <= 80:
            vec[:, 128 * t : 128 * t + 128] += part
        else:
            vec[:, 128 * t : 128 * t + 128] += jnp.where(lanes >= off, part, 0.0)
            vec[:, 128 * t + 128 : 128 * t + 256] += jnp.where(lanes < off, part, 0.0)

    def gain(n):
        return vec[2 * n : 2 * n + 1, :], vec[2 * n + 1 : 2 * n + 2, :]

    def query():
        return vec[6:7, :]

    def tick(*names):
        for name in names:
            todo.step({name})

    def norm_one():
        g, b = gain(0)
        for i in range(4):
            rows = pl.ds(IMG * i, IMG)
            xh, _ = whiten(tok[rows, :].astype(F32))
            nrm[rows, :] = (xh * g + b).astype(BF)

    norm_one()

    def wide(bufs, ch):
        zlo, xp = ch // 2, ch % 2
        cols = []
        for l in range(6):
            at = [
                bufs[l % 3].load(core, x=2 * xp + l // 3, y=y, z=2 * h + zlo)
                for y in range(4) for core in range(2) for h in range(2)
            ]
            cols.append(jnp.concatenate(at, axis=0))
        return jnp.concatenate(cols, axis=1)

    def wide_store(bufs, ch, value):
        zlo, xp = ch // 2, ch % 2
        for l in range(6):
            n = 0
            for y in range(4):
                for core in range(2):
                    for h in range(2):
                        part = value[48 * n : 48 * n + 48, 128 * l : 128 * l + 128]
                        bufs[l % 3].store(part, core, x=2 * xp + l // 3, y=y, z=2 * h + zlo)
                        n += 1

    def tall(bufs, y):
        cols = []
        for l in range(6):
            at = [
                bufs[l % 3].load(core, x=2 * xh + l // 3, y=y, z=z)
                for core in range(2) for z in range(4) for xh in range(2)
            ]
            cols.append(jnp.concatenate(at, axis=0))
        return jnp.concatenate(cols, axis=1)

    def tall_store(bufs, y, value):
        for l in range(6):
            n = 0
            for core in range(2):
                for z in range(4):
                    for xh in range(2):
                        part = value[48 * n : 48 * n + 48, 128 * l : 128 * l + 128]
                        bufs[l % 3].store(part, core, x=2 * xh + l // 3, y=y, z=z)
                        n += 1

    def flat(ref, ch, rows=None):
        return jnp.concatenate([ref[R * (6 * ch + l) : R * (6 * ch + l) + R, :] for l in range(6)], axis=1)

    tick("a", "p", "d")
    todo.finish({"a"})
    for ch, dst in enumerate((q, k, v)):
        out = nn(nrm[...], wide(WA, ch))
        if ch == 0:
            out = out * 0.125
        dst[0:R, :] = out.astype(BF)
        if ch == 0:
            tick("u")
        if ch == 2:
            tick("p")
    lane = lax.broadcasted_iota(jnp.int32, (1, 128), 1)
    heads = [jnp.where(lane < 64, 1.0, 0.0).astype(BF), jnp.where(lane < 64, 0.0, 1.0).astype(BF)]

    def attend(img):
        rows, wide_rows = pl.ds(IMG * img, IMG), pl.ds(IMG * img, 256)

        def pair(pr):
            c = ds(128 * pr, 128)
            q2, k2, v2 = q[wide_rows, c], k[rows, c], v[rows, c]
            vt = v2.T
            b2 = jnp.concatenate([bias[img], bias[img]], axis=1)
            got = []
            for h in range(2):
                st = nt(k2, q2 * heads[h]) + b2
                e = jnp.exp(st - jnp.max(st, axis=0, keepdims=True))
                p = (e * (1.0 / jnp.sum(e, axis=0, keepdims=True))).astype(BF)
                pb[img % 2, 2 * pr + h] = p
                got.append(nn(vt[64 * h : 64 * h + 64, :], p).astype(BF))
            o = jnp.concatenate(got, axis=0).T
            att[rows, c] = o[0:IMG, :]

        for pr in range(6):
            pair(pr)

    saves = []
    for img in range(4):
        if img >= 2:
            saves[img - 2].wait()
        attend(img)
        if img < 2:
            c = pltpu.make_async_copy(pb.at[img], spill.at[img], lsem.at[img])
            c.start()
            saves.append(c)
        tick(*(("d",), ("u",), ("p", "d"), ())[img])

    res[...] = tok[...].astype(F32) + nn(att[0:R, :], wide(WA, 3))

    g, b = gain(1)
    for i in range(4):
        rows = pl.ds(IMG * i, IMG)
        xh, r = whiten(res[rows, :])
        xh2[rows, :] = xh.astype(BF)
        r2[rows, :] = r
        nrm[rows, :] = (xh * g + b).astype(BF)
    todo.finish({"u"})
    for ch in range(4):
        a, d = gelu_parts(nn(nrm[...], wide(WU, ch)))
        for l in range(6):
            at = pl.ds(R * (6 * ch + l), R)
            act[at, :] = a[:, 128 * l : 128 * l + 128].astype(BF)
            gel[at, :] = d[:, 128 * l : 128 * l + 128].astype(BF)
    todo.finish({"d"})
    for y in range(4):
        res[...] += nn(flat(act, y), tall(WD, y))

    g, b = gain(2)
    for i in range(4):
        x = res[IMG * i : IMG * i + IMG, :]
        m = jnp.mean(x, axis=-1, keepdims=True)
        xc = x - m
        r = lax.rsqrt(jnp.mean(xc * xc, axis=-1, keepdims=True) + 1e-05)
        e = r * jnp.sum(xc * (g * query()), axis=-1, keepdims=True)
        lg = (e + jnp.sum(b * query(), axis=-1, keepdims=True)) / ROOT
        lg = jnp.where(mcol[0:IMG, i : i + 1] > 0, lg, -1e30)
        ex = jnp.exp(lg - jnp.max(lg, axis=0, keepdims=True))
        sh = ex / jnp.sum(ex, axis=0, keepdims=True)
        row = jnp.sum((sh * r) * xc, axis=0, keepdims=True)
        s1[i : i + 1, :] = row
        pool[i : i + 1, :] = row * g + b * jnp.sum(sh, axis=0, keepdims=True)
        for n, c in enumerate((m, r, e, sh)):
            cols[i, :, n : n + 1] = c
    todo.finish()
    link.drain()

    def proj_cols(x, lo):
        at = [
            WP.load(core, lo, 32, x=x, y=y, z=z)
            for y in range(4) for core in range(2) for z in range(4)
        ]
        return jnp.concatenate(at, axis=0)

    pooled = pool[...].astype(BF)
    padded = jnp.concatenate(
        [nn(pooled[:, 384 * n : 384 * n + 384], e3[...]).astype(BF) for n in range(2)], axis=1
    )
    embedded = jnp.concatenate([nn(padded, proj_cols(x, 0)) for x in range(4)], axis=1)
    ri = lax.rsqrt(jnp.sum(embedded * embedded, axis=-1, keepdims=True) + 1e-06)
    unit = (embedded * ri).astype(BF)
    big = jnp.exp(jnp.full((1, 1), scale[0], F32))
    dots = nt(unit[:, 0:128], proj_cols(0, 32))
    for x in range(1, 4):
        dots = dots + nt(unit[:, 128 * x : 128 * x + 128], proj_cols(x, 32))
    logits = big * dots
    row = lax.broadcasted_iota(jnp.int32, (8, 1024), 0)
    col = lax.broadcasted_iota(jnp.int32, (8, 1024), 1)
    valid = (row < 4) & ((col & 7) < 4)
    target = jnp.zeros((8, 1024), F32)
    first = 4 * ((me.y * 2 + me.core) * 16 + me.z * 4 + me.x)
    for i in range(4):
        t = pairing[first + i]
        target = jnp.where((row == i) & (col == 8 * (t >> 2) + (t & 3)), 1.0, target)
    e = jnp.where(valid, jnp.exp(logits), 0.0)
    row_sum = jnp.where(row[:, 0:1] < 4, jnp.sum(e, axis=-1, keepdims=True), 1.0)
    col_sum = jnp.sum(e, axis=0, keepdims=True)
    for j in range(8):
        cs[j : j + 1, :] = col_sum[:, 128 * j : 128 * j + 128]
    rows_lse = jnp.sum(jnp.log(row_sum), axis=0, keepdims=True)
    matched = jnp.sum(jnp.sum(logits * target, axis=-1, keepdims=True), axis=0, keepdims=True)
    send_tile = cs[...]
    send_tile = jnp.where((subs == 0) & (lanes == 4), rows_lse, send_tile)
    send_tile = jnp.where((subs == 0) & (lanes == 5), matched, send_tile)
    cs[...] = send_tile
    got = link.group(crx.at[pl.ds(0, 15)])
    for n in range(1, 16):
        t, peer = me.v_peer(n)
        got.copy(cs, crx.at[me.v], peer)
    crx[me.v] = send_tile
    got.wait_recv()
    total = crx[0]
    for n in range(1, 16):
        total = total + crx[n]
    cst[...] = total
    got = link.group(crx2.at[pl.ds(0, 7)])
    for n in range(1, 8):
        t, peer = me.s_peer(n)
        got.copy(cst, crx2.at[s], peer)
    crx2[s] = total
    got.wait_recv()
    total = crx2[0]
    for n in range(1, 8):
        total = total + crx2[n]
    cs_all = jnp.concatenate([total[j : j + 1, :] for j in range(8)], axis=1)
    ok = (lanes & 7) < 4
    cols_lse = jnp.sum(jnp.where(ok, jnp.log(jnp.where(ok, total, 1.0)), 0.0))
    loss = (total[0:1, 4:5] + cols_lse - 2.0 * total[0:1, 5:6]) / 1024.0
    ok = (col[0:1, :] & 7) < 4
    gl = e / row_sum + e / jnp.where(ok, cs_all, 1.0) - 2.0 * target
    gl = jnp.where(valid, gl, 0.0) * (1.0 / 1024.0)
    g_scale = jnp.sum(gl * logits)
    parts = split(gl, 2)
    gui = []
    for x in range(4):
        rhs = proj_cols(x, 32)
        gui.append(nn(parts[0], rhs) + nn(parts[1], rhs))
    gui = big * jnp.concatenate(gui, axis=1)
    ge = ri * gui - ri * ri * ri * embedded * jnp.sum(embedded * gui, axis=-1, keepdims=True)
    ge = ge.astype(BF)
    gp_pad = jnp.concatenate(
        [
            sum(nt(ge[:, 128 * x : 128 * x + 128], proj_cols(x, 0)) for x in range(4))
        ], axis=1
    )
    gp = []
    for n in range(2):
        gp.append(sum(nt(p, e3[...]) for p in split(gp_pad[:, 512 * n : 512 * n + 512], 3)))
    emb[...] = jnp.concatenate(gp, axis=1)
    both = jnp.concatenate([parts[0], parts[1]], axis=0)
    ub = jnp.concatenate([unit, unit], axis=0)
    for x in range(4):
        gproj = tn(padded, ge[:, 128 * x : 128 * x + 128]).astype(BF)
        gtext = (big * tn(both, ub[:, 128 * x : 128 * x + 128])).astype(BF)
        n = 0
        for y in range(4):
            for core in range(2):
                for z in range(4):
                    WP.store(gproj[32 * n : 32 * n + 32, :], core, 0, x=x, y=y, z=z)
                    WP.store(gtext[32 * n : 32 * n + 32, :], core, 32, x=x, y=y, z=z)
                    n += 1

    def keep(n, c):
        def finish(total):
            tot[n, :, 128 * c : 128 * c + 128] = total

        return finish

    def keep_p(total):
        ptot[...] = total

    def rx_part(ref, c, n):
        return ref.at[pl.ds(n * c, n)]

    todo.add("p", scatter_steps(me, link, WP, rxpc, rxp, keep_p))
    tick("p")

    def own_rows(n):
        for j in range(8):
            ust[n - 1, j] = tot[n, 6 * j : 6 * j + 6, :]
        group = link.group(orx.at[n - 1, pl.ds(0, 7)])
        for m in range(1, 8):
            t, peer = me.s_peer(m)
            group.copy(ust.at[n - 1, t], orx.at[n - 1, s], peer)
        orx[n - 1, s] = ust[n - 1, s]
        return group

    def own_down():
        group = link.group(tot.at[3, pl.ds(0, 24)])
        group.copy(
            tot.at[0, ds(24 * (1 - odd), 24, 8)],
            tot.at[3, ds(24 * odd, 24, 8)],
            me.dev(x=me.x + 1 - 2 * odd),
        )
        tot[3, ds(24 * odd, 24, 8), :] = tot[0, ds(24 * odd, 24, 8), :]
        return group

    def own_proj():
        for j in range(4):
            pst[j, 0:8] = ptot[8 * j : 8 * j + 8, :]
            pst[j, 8:16] = ptot[32 + 8 * j : 40 + 8 * j, :]
        group = link.group(prx2.at[pl.ds(0, 3)])
        for n in range(1, 4):
            t = (me.x + n) % 4
            group.copy(pst.at[t], prx2.at[me.x], me.dev(x=t))
        prx2[me.x] = pst[me.x]
        return group

    g, b = gain(2)
    side_q = query() / ROOT
    for i in range(4):
        rows = pl.ds(IMG * i, IMG)
        gpi = emb[i : i + 1, :]
        m, r, e, sh = (cols[i, :, n : n + 1] for n in range(4))
        one, two = gpi * g, side_q * g
        xc = res[rows, :] - m
        w = r * jnp.sum(xc * one, axis=-1, keepdims=True)
        c = w + jnp.sum(b * gpi, axis=-1, keepdims=True)
        dl = sh * (c - jnp.sum(sh * c, axis=0, keepdims=True))
        pull = r * r * (sh * w + dl * (e / ROOT)) * (1.0 / D)
        one_c = one - jnp.mean(one, axis=-1, keepdims=True)
        two_c = two - jnp.mean(two, axis=-1, keepdims=True)
        out = (r * sh) * one_c + (r * dl) * two_c - pull * xc
        res[rows, :] = out
        gb[rows, :] = out.astype(BF)
        row = jnp.sum((r * dl) * xc, axis=0, keepdims=True)
        sum_dl = jnp.sum(dl, axis=0, keepdims=True)
        gvec[4, 0:1, :] += gpi * s1[i : i + 1, :] + side_q * row
        gvec[5, 0:1, :] += gpi * jnp.sum(sh, axis=0, keepdims=True) + side_q * sum_dl
        gvec[6, 0:1, :] += (row * g + b * sum_dl) / ROOT
    for y in range(4):
        ga = nt(gb[...], tall(WD, y))
        for l in range(6):
            at = pl.ds(R * (6 * y + l), R)
            gel[at, :] = (ga[:, 128 * l : 128 * l + 128] * gel[at, :].astype(F32)).astype(BF)
        tall_store(WD, y, tn(flat(act, y), gb[...]).astype(BF))
        tick("p")
    for c in range(3):
        todo.add("d", scatter_steps(me, link, WD[c], rx_part(rxc, c, 3072), rx_part(rxd, c, 3024), keep(0, c), give=credit.at[c]))
    tick("d")
    for ch in range(4):
        gu = flat(gel, ch)
        part = nt(gu, wide(WU, ch))
        if ch == 0:
            acc[...] = part
        else:
            acc[...] += part
        wide_store(WU, ch, tn(nrm[...], gu).astype(BF))
        if ch == 0:
            got_proj = own_proj()
            tick("d")
        if ch == 2:
            tick("d")
    for c in range(3):
        todo.add("u", scatter_steps(me, link, WU[c], rx_part(rxc, c, 3072), rx_part(rxu, c, 3024), keep(1, c), give=credit.at[3 + c], need=credit.at[c]))
    tick("u")

    def fold_in(n, gg, gs):
        gvec[n] += gg
        gvec[n + 1] += gs

    g, _ = gain(1)
    for i in range(4):
        rows = pl.ds(IMG * i, IMG)
        y, xh = acc[rows, :], xh2[rows, :].astype(F32)
        out = res[rows, :] + whiten_back(y * g, xh, r2[rows, :])
        res[rows, :] = out
        gb[rows, :] = out.astype(BF)
        fold_in(2, fold(y * xh), fold(y))
    wide_store(GA, 3, tn(att[0:R, :], gb[...]).astype(BF))
    att[0:R, :] = nt(gb[...], wide(WA, 3)).astype(BF)
    norm_one()
    tick("d", "u")
    low = lax.broadcasted_iota(jnp.int32, (256, 128), 0) < IMG
    side = lax.broadcasted_iota(jnp.int32, (256, 128), 1) < 64
    own = [jnp.where(low & side, 1.0, 0.0).astype(BF), jnp.where(low & ~side, 1.0, 0.0).astype(BF)]

    def attend_back(img):
        rows, wide_rows = pl.ds(IMG * img, IMG), pl.ds(IMG * img, 256)

        def pair(pr):
            c = ds(128 * pr, 128)
            q2, k2, v2, do = q[wide_rows, c], k[rows, c], v[rows, c], att[wide_rows, c]
            kt = k2.T
            dqt = []
            dk = jnp.zeros((IMG, 128), F32)
            dv = jnp.zeros((IMG, 128), F32)
            for h in range(2):
                doh, qh = do * own[h], q2 * heads[h]
                p = pb[img % 2, 2 * pr + h]
                dv = dv + nn(p, doh)
                pf = p.astype(F32)
                dp = nt(v2, doh)
                t = pf * dp
                dst = (t - pf * jnp.sum(t, axis=0, keepdims=True)).astype(BF)
                dk = dk + nn(dst, qh)
                dqt.append(nn(kt[64 * h : 64 * h + 64, :], dst))
            dq = (jnp.concatenate(dqt, axis=0) * 0.125).astype(BF).T
            q[rows, c] = dq[0:IMG, :]
            k[rows, c] = dk.astype(BF)
            v[rows, c] = dv.astype(BF)

        for pr in range(6):
            pair(pr)

    loads = {}
    for img in (2, 3, 0, 1):
        if img in loads:
            loads[img].wait()
        attend_back(img)
        if img >= 2:
            c = pltpu.make_async_copy(spill.at[img - 2], pb.at[img - 2], lsem.at[img])
            c.start()
            loads[img - 2] = c
        tick(*(("u",), (), ("d",), ("u",))[img])
    for ch, src in enumerate((q, k, v)):
        wide_store(GA, ch, tn(nrm[...], src[0:R, :]).astype(BF))
    for c in range(3):
        todo.add("a", scatter_steps(me, link, GA[c], rx_part(rxc, c, 3072), rx_part(rxa, c, 3024), keep(2, c), need=credit.at[3 + c]))
    tick("a")
    for ch, src in enumerate((q, k, v)):
        part = nt(src[0:R, :], wide(WA, ch))
        if ch == 0:
            acc[...] = part
            tick("a")
        else:
            acc[...] += part
    tick("u", "a")
    g, _ = gain(0)
    outs = []
    for i in range(4):
        rows = pl.ds(IMG * i, IMG)
        xh, r = whiten(tok[rows, :].astype(F32))
        y = acc[rows, :]
        out = res[rows, :] + whiten_back(y * g, xh, r)
        fold_in(0, fold(y * xh), fold(y))
        acc[196 * i : 196 * i + 196, :] = out[0:196, :]
        if i % 2 == 1:
            rows = pl.ds(392 * (i // 2), 392)
            outs.append(pltpu.make_async_copy(acc.at[rows], o_tok.at[rows], lsem.at[4 + i // 2]))
            outs[-1].start()

    for n in range(7):
        vec[n : n + 1, :] = jnp.sum(gvec[n], axis=0, keepdims=True)
    vec[7:8, :] = jnp.zeros((1, D), F32)
    for n in range(16):
        t, off = 48 * n // 128, 48 * n % 128
        part = vec[:, 128 * t : 128 * t + 128]
        part = pltpu.roll(part, (128 - off) % 128, 1) if off else part
        if off > 80:
            more = pltpu.roll(vec[:, 128 * t + 128 : 128 * t + 256], 128 - off, 1)
            part = jnp.where(lanes < 128 - off, part, more)
        gst2[n] = jnp.where(subs == 7, g_scale, part)
    cv = link.group(grx.at[pl.ds(0, 15)])
    for n in range(1, 16):
        t, peer = me.v_peer(n)
        cv.copy(gst2.at[t], grx.at[me.v], peer)
    grx[me.v] = gst2[me.v]

    todo.finish({"d", "u"})
    tick("a")
    got_down, got_up = own_down(), own_rows(1)
    cv.wait_recv()
    total = grx[0]
    for n in range(1, 16):
        total = total + grx[n]
    vst[...] = total
    got_vec = link.group(grx2.at[pl.ds(0, 7)])
    for n in range(1, 8):
        t, peer = me.s_peer(n)
        got_vec.copy(vst, grx2.at[s], peer)
    grx2[s] = total
    todo.finish({"a"})
    last = own_rows(2)
    got_vec.wait_recv()
    total = grx2[0]
    for n in range(1, 8):
        total = total + grx2[n]
    total = pltpu.roll(total, (128 - 6 * s) % 128, 1)
    scal[...] = jnp.where((subs == 7) & (lanes == 1), loss, total)
    to_smem = pltpu.make_async_copy(scal, scal_s, lsem.at[6])
    to_smem.start()
    got_up.wait_recv()
    got_down.wait_recv()
    for j in range(8):
        o_up[:, 384 * j : 384 * j + 384] = orx[0, j]
    for j in range(2):
        o_down[:, 384 * j : 384 * j + 384] = tot[3, 24 * j : 24 * j + 24, :]
    got_proj.wait_recv()
    for j in range(4):
        o_proj[:, 128 * j : 128 * j + 128] = prx2[j, 0:6]
    gt = jnp.concatenate([prx2[j, 8:12] for j in range(4)], axis=1)
    txt = text[...]
    r = lax.rsqrt(jnp.sum(txt * txt, axis=-1, keepdims=True) + 1e-06)
    o_text[...] = r * gt - r * r * r * txt * jnp.sum(txt * gt, axis=-1, keepdims=True)
    to_smem.wait()
    for n, ref in enumerate((o0, o1, o2, o3, o4, o5, o6)):
        for e in range(6):
            ref[e] = scal_s[n, e]
    o_scale[0] = scal_s[7, 0]
    o_loss[0] = scal_s[7, 1]
    last.wait_recv()
    for j in range(8):
        if j < 6:
            o_qkv[:, 384 * j : 384 * j + 384] = orx[1, j]
        else:
            o_out[:, 384 * (j - 6) : 384 * (j - 6) + 384] = orx[1, j]
    for c in outs:
        c.wait()
    link.drain()


def shards(tokens, keep_mask, pairing, text_vectors, logit_scale, w_qkv, w_out, w_up, w_down, w_proj, *vectors):
    vm = pl.BlockSpec(memory_space=pltpu.VMEM)
    sm = pl.BlockSpec(memory_space=pltpu.SMEM)
    hbm = pl.BlockSpec(memory_space=pl.ANY)
    S = jax.ShapeDtypeStruct
    V = pltpu.VMEM
    outs = pl.pallas_call(
        kernel,
        out_shape=[
            S((1,), F32), S((784, D), F32), S((4, 512), F32), S((6, 2304), F32), S((6, 768), F32),
            S((6, 3072), F32), S((24, 768), F32), S((6, 512), F32), *[S((6,), F32)] * 7, S((1,), F32),
            S((2, 12, IMG, 256), BF),
        ],
        in_specs=[sm] * 9 + [hbm] + [vm] * 7,
        out_specs=[sm, hbm, vm, vm, vm, vm, vm, vm, *[sm] * 8, hbm],
        scratch_shapes=[
            V((18432, 128), BF), V((18432, 128), BF), V((18432, 128), BF), V((8192, 128), BF), V((R, D), BF),
            V((R + 48, D), BF), V((R, D), BF), V((R, D), BF), V((2, 12, IMG, 256), BF),
            V((R, D), BF), V((R, D), BF), V((R + 48, D), BF), V((R, D), BF),
            V((24 * R, 128), BF), V((24 * R, 128), BF), V((R, D), F32), V((R, D), F32), V((R, 1), F32),
            V((3 * 3072, 128), BF), V((3 * 3024, 128), BF), V((3 * 3024, 128), BF), V((3 * 3024, 128), BF),
            V((4096, 128), BF), V((4032, 128), BF),
            V((6, 3072), F32), V((8, 6, 384), F32), V((8, 6, 384), F32), V((2, 24, 384), F32),
            V((16, 512), F32), V((4, 16, 128), F32), V((8, 8, 128), F32), V((8, 128), F32),
            V((48, 384), F32), V((64, 128), F32), V((8, D), F32), V((7, 8, D), F32),
            V((8, 256), F32), V((256, 8), F32), V((4, IMG, 8), F32), V((4, IMG, 128), F32),
            V((8, D), F32), V((8, D), F32), V((384, 512), BF), V((8, D), F32),
            V((8, 128), F32), pltpu.SMEM((8, 128), F32),
            V((8, 128), F32), V((16, 8, 128), F32), V((8, 128), F32), V((8, 8, 128), F32),
            V((4, 48, 384), F32), V((64, 128), F32), V((2, 8, 6, 384), F32), V((2, 8, 6, 384), F32),
            V((4, 16, 128), F32), V((4, 16, 128), F32), V((16, 8, 128), F32), V((16, 8, 128), F32),
            V((16, 8, 128), F32), V((8, 8, 128), F32),
            pltpu.SemaphoreType.DMA((N_SEM,)), pltpu.SemaphoreType.DMA((N_SEM,)), pltpu.SemaphoreType.DMA((8,)),
            pltpu.SemaphoreType.REGULAR((6,)),
        ],
        compiler_params=pltpu.CompilerParams(
            collective_id=0, has_side_effects=True, vmem_limit_bytes=(64 << 20) - (256 << 10)
        ),
        cost_estimate=pl.CostEstimate(flops=40_000_000_000, bytes_accessed=20_000_000, transcendentals=0),
    )(pairing, logit_scale, *vectors, tokens, keep_mask, text_vectors, w_qkv, w_out, w_up, w_down, w_proj)
    return tuple(outs[:16])


def solution(mesh):
    rows, vector, whole = P(("dp", "fsdp"), None), P(("dp", "fsdp")), P()
    in_specs = (rows, rows, whole, rows, whole, *[rows] * 5, *[vector] * 7)
    out_specs = (whole, rows, rows, *[rows] * 5, *[vector] * 7, whole)
    return jax.shard_map(shards, mesh=mesh, in_specs=in_specs, out_specs=out_specs, check_vma=False)
```

```python
from functools import partial
import math

import jax
import jax.numpy as jnp
from jax import lax
from jax.experimental import pallas as pl
from jax.experimental.pallas import tpu as pltpu
from jax.sharding import PartitionSpec as P

MESH = pl.DeviceIdType.MESH
BF = jnp.bfloat16
F32 = jnp.float32
IMG = 208
R = 4 * IMG
D = 768
ROOT = math.sqrt(768.0)


class Place:
    def __init__(self):
        dp = lax.axis_index("dp")
        fs = lax.axis_index("fsdp")
        self.y, self.core = dp // 2, dp % 2
        self.z, self.x = fs // 4, fs % 4
        self.s = (self.z % 2) * 4 + self.x
        self.v = dp * 2 + self.z // 2

    def dev(self, **moved):
        at = dict(x=self.x, y=self.y, z=self.z, core=self.core)
        at.update(moved)
        return (at["y"] * 2 + at["core"], at["z"] * 4 + at["x"])

    def hop(self, dim, step):
        return self.dev(**{dim: (getattr(self, dim) + step + 4) % 4})

    def sibling(self):
        return self.dev(core=1 - self.core)

    def s_peer(self, k):
        t = (self.s + k) % 8
        return t, self.dev(z=(self.z // 2) * 2 + t // 4, x=t % 4)

    def v_peer(self, k):
        t = (self.v + k) % 16
        return t, (t // 2, ((t % 2) * 2 + self.z % 2) * 4 + self.x)


class Group:
    def __init__(self, link, total):
        self.link, self.total = link, total
        self.k = link.n
        link.n += 1
        link.open.append(self)
        self.sems = dict(send_sem=link.send.at[self.k], recv_sem=link.recv.at[self.k])

    def copy(self, src, dst, dev):
        c = pltpu.make_async_remote_copy(
            src_ref=src, dst_ref=dst, device_id=dev, device_id_type=MESH, **self.sems
        )
        c.start()

    def whole(self):
        return pltpu.make_async_remote_copy(
            src_ref=self.total,
            dst_ref=self.total,
            device_id=self.link.any_device,
            device_id_type=MESH,
            **self.sems,
        )

    def wait_recv(self):
        self.whole().wait_recv()


class Link:
    def __init__(self, send, recv, any_device):
        self.send, self.recv, self.n = send, recv, 0
        self.any_device = any_device
        self.open = []

    def group(self, total):
        return Group(self, total)

    def drain(self):
        for g in self.open:
            g.whole().wait_send()
        self.open = []


ORDERS = (("x", "y", "z"), ("y", "z", "x"), ("z", "x", "y"))


def enter(me):
    sem = pltpu.get_barrier_semaphore()
    peers = []
    for n in range(1, 64):
        dx, dy, dz = n % 4, n // 4 % 4, n // 16
        if dx * dy * dz == 0:
            peers.append(me.dev(x=(me.x + dx) % 4, y=(me.y + dy) % 4, z=(me.z + dz) % 4))
    for n in range(8):
        peers.append(me.dev(y=(me.y + n % 4) % 4, z=(me.z + n // 4 * 2) % 4, core=1 - me.core))
    for p in peers:
        pl.semaphore_signal(sem, inc=1, device_id=p, device_id_type=MESH)
    pl.semaphore_wait(sem, len(peers))


def ds(start, size, unit=None):
    if isinstance(start, int):
        return pl.ds(start, size)
    return pl.ds(pl.multiple_of(start, unit or size), size)


class Pieces:
    def __init__(self, ref, base, order, rows):
        self.ref, self.base, self.order, self.rows = ref, base, order, rows

    def start(self, core, **at):
        d1, d2, d3 = (at[d] for d in self.order)
        return self.base + (((core * 4 + d3) * 4 + d2) * 4 + d1) * self.rows

    def piece(self, core, **at):
        return self.ref.at[ds(self.start(core, **at), self.rows, 16)]

    def load(self, core, lo=0, n=None, **at):
        return self.ref[pl.ds(self.start(core, **at) + lo, n or self.rows), :]

    def store(self, value, core, lo=0, **at):
        self.ref[pl.ds(self.start(core, **at) + lo, value.shape[0]), :] = value

    def block(self, core, stage, me, b):
        at = [getattr(me, d) for d in self.order]
        at[stage] = b
        for k in range(stage):
            at[k] = 0
        return self.start(core, **dict(zip(self.order, at))), self.rows * 4**stage


def rows_of(ref, block):
    return ref.at[ds(block[0], block[1], 16)]


def plane_peer(me, order, n):
    a, b = order[:2]
    i, j = (getattr(me, a) + n % 4) % 4, (getattr(me, b) + n // 4) % 4
    return {a: i, b: j}, me.dev(**{a: i, b: j})


def cut(block, which):
    start, size = block
    return (start + which * (size // 2), size // 2)


def gather_steps(me, link, buf):
    ref, d, rows = buf.ref, buf.order[2], buf.rows
    i, size = getattr(me, d), 16 * buf.rows
    lo, hi, far = (i + 3) % 4, (i + 1) % 4, (i + 2) % 4
    right, left = me.hop(d, 1), me.hop(d, -1)

    def bytes_of(pieces):
        return ref.at[pl.ds(buf.base, pieces * rows)]

    def send(group, block, dev):
        group.copy(rows_of(ref, block), rows_of(ref, block), dev)

    def block(b):
        return buf.block(me.core, 2, me, b)

    own = buf.block(me.core, 0, me, getattr(me, buf.order[0]))
    plane = link.group(bytes_of(15))
    for n in range(1, 16):
        send(plane, own, plane_peer(me, buf.order, n)[1])
    yield
    plane.wait_recv()
    from_lo, from_hi = link.group(bytes_of(16)), link.group(bytes_of(16))
    send(from_lo, block(i), right)
    send(from_hi, block(i), left)
    sib = link.group(bytes_of(64))
    send(sib, block(i), me.sibling())
    yield
    from_lo.wait_recv()
    rest = link.group(bytes_of(16))
    send(rest, cut(block(lo), 0), right)
    from_hi.wait_recv()
    send(rest, cut(block(hi), 1), left)
    send(sib, block(lo), me.sibling())
    send(sib, block(hi), me.sibling())
    yield
    rest.wait_recv()
    send(sib, block(far), me.sibling())
    yield
    sib.wait_recv()


def add_rows(dst_ref, dst, *srcs):
    size = dst[1]
    rows = ds(dst[0], size, 16)
    if len(srcs) == 1:
        ref, start = srcs[0]
        dst_ref[rows, :] = dst_ref[rows, :] + ref[ds(start, size, 16), :]
        return
    total = dst_ref[rows, :].astype(F32)
    for ref, start in srcs:
        total = total + ref[ds(start, size, 16), :].astype(F32)
    dst_ref[rows, :] = total.astype(BF)


def scatter_steps(me, link, buf, rx_core, rx, finish, give=None, need=None):
    ref, rows, d = buf.ref, buf.rows, buf.order[2]
    i, size = getattr(me, d), 16 * buf.rows
    lo, hi, far = (i + 3) % 4, (i + 1) % 4, (i + 2) % 4
    right, left = me.hop(d, 1), me.hop(d, -1)

    def bytes_of(pieces):
        return ref.at[pl.ds(buf.base, pieces * rows)]

    def block(b, core=me.core):
        return buf.block(core, 2, me, b)

    def slot(n):
        return (n * size, size)

    if need is not None:
        pl.semaphore_wait(need, 1)
    def cross(group, b):
        group.copy(rows_of(ref, block(b, 1 - me.core)), rows_of(rx_core, (b * size, size)), me.sibling())

    first, rest = link.group(bytes_of(16)), link.group(bytes_of(48))
    cross(first, far)
    yield
    for b in (hi, lo, i):
        cross(rest, b)
    yield
    first.wait_recv()

    def settle(b):
        add_rows(ref, block(b), (rx_core, b * size))

    def send(group, src, dst, dev):
        group.copy(rows_of(ref, src), rows_of(rx, dst), dev)

    settle(far)
    merge = link.group(bytes_of(16))
    send(merge, cut(block(far), 0), cut(slot(0), 0), right)
    send(merge, cut(block(far), 1), cut(slot(0), 1), left)
    yield
    rest.wait_recv()
    settle(hi)
    ends = link.group(bytes_of(32))
    send(ends, cut(block(hi), 1), cut(slot(1), 1), right)
    settle(lo)
    send(ends, cut(block(lo), 0), cut(slot(2), 0), left)
    settle(i)
    if give is not None:
        pl.semaphore_signal(give, inc=1, device_id=me.sibling(), device_id_type=MESH)
    yield
    merge.wait_recv()
    add_rows(ref, cut(block(hi), 0), (rx, cut(slot(0), 0)[0]))
    send(ends, cut(block(hi), 0), cut(slot(1), 0), right)
    add_rows(ref, cut(block(lo), 1), (rx, cut(slot(0), 1)[0]))
    send(ends, cut(block(lo), 1), cut(slot(2), 1), left)
    yield
    ends.wait_recv()
    add_rows(ref, block(i), (rx, size), (rx, 2 * size))
    plane = link.group(bytes_of(15))
    for n in range(1, 16):
        at, peer = plane_peer(me, buf.order, n)
        src = (buf.start(me.core, **{**at, d: i}), rows)
        send(plane, src, (3 * size + (n - 1) * rows, rows), peer)
    yield
    plane.wait_recv()
    own = buf.block(me.core, 0, me, getattr(me, buf.order[0]))
    total = ref[ds(own[0], rows, 16), :].astype(F32)
    for n in range(15):
        total = total + rx[pl.ds(3 * size + n * rows, rows), :].astype(F32)
    finish(total)


class Queue:
    def __init__(self):
        self.live = []

    def add(self, name, gen):
        self.live.append((name, gen))

    def step(self, names=None):
        keep = []
        for name, gen in self.live:
            if names is None or name in names:
                try:
                    next(gen)
                except StopIteration:
                    continue
            keep.append((name, gen))
        self.live = keep

    def finish(self, names=None):
        while any(names is None or n in names for n, _ in self.live):
            self.step(names)


def nn(a, b):
    return lax.dot_general(a, b, (((1,), (0,)), ((), ())), preferred_element_type=F32)


def nt(a, b):
    return lax.dot_general(a, b, (((1,), (1,)), ((), ())), preferred_element_type=F32)


def tn(a, b):
    return lax.dot_general(a, b, (((0,), (0,)), ((), ())), preferred_element_type=F32)


def whiten(x):
    centred = x - jnp.mean(x, axis=-1, keepdims=True)
    r = lax.rsqrt(jnp.mean(centred * centred, axis=-1, keepdims=True) + 1e-05)
    return centred * r, r


def whiten_back(y, xh, r):
    return r * (y - jnp.mean(y, axis=-1, keepdims=True) - xh * jnp.mean(y * xh, axis=-1, keepdims=True))


def fold(x):
    return jnp.sum(x.reshape(x.shape[0] // 8, 8, x.shape[1]), axis=0)


def split(x, parts):
    got = []
    for _ in range(parts):
        h = x.astype(BF)
        got.append(h)
        x = x - h.astype(F32)
    return got


def gelu_parts(u):
    a = jnp.abs(u)
    den = 1.0 + (0.3275911 * math.sqrt(0.5)) * a
    t = pltpu.reciprocal(den, approx=True)
    t = t * (2.0 - den * t)
    e = jnp.exp2((-0.5 * math.log2(math.e)) * (u * u))
    poly = t * (0.5 * 0.254829592 + t * (-0.5 * 0.284496736 + t * (0.5 * 1.421413741 + t * (-0.5 * 1.453152027 + t * (0.5 * 1.061405429)))))
    tail = poly * e
    phi = jnp.where(u < 0, tail, 1.0 - tail)
    return u * phi, phi + u * (e * (1.0 / math.sqrt(2.0 * math.pi)))


def blocks(n, body, unroll=1):
    lax.fori_loop(0, n, lambda k, c: (body(k), 0)[1], 0, unroll=unroll)


N_SEM = 120


def kernel(
    pairing, scale, v0, v1, v2, v3, v4, v5, v6,
    tokens, mask, text, w_qkv, w_out, w_up, w_down, w_proj,
    o_loss, o_tok, o_text, o_qkv, o_out, o_up, o_down, o_proj, o0, o1, o2, o3, o4, o5, o6, o_scale, spill,
    wa, wu, wd, wp, tok, q, k, v, pb, xh2, nrm, att, gb, act, gel, res, acc, r2,
    rxc, rxd, rxu, rxa, rxpc, rxp,
    aloc, arx, urx, drx, ploc, prx, vrx, vst, p48, p64, vec, gvec,
    mrow, mcol, cols, bias, pool, s1, e3, emb, scal, scal_s, cs, crx, cst, crx2,
    tot, ptot, orx, ust, pst, prx2, gst, grx, gst2, grx2,
    send, recv, lsem, credit,
):
    me = Place()
    link = Link(send, recv, me.sibling())
    todo = Queue()
    s = me.s
    lanes = lax.broadcasted_iota(jnp.int32, (8, 128), 1)
    subs = lax.broadcasted_iota(jnp.int32, (8, 128), 0)

    WA = [Pieces(wa, 6144 * c, ORDERS[c], 48) for c in range(3)]
    WU = [Pieces(wu, 6144 * c, ORDERS[c], 48) for c in range(3)]
    WD = [Pieces(wd, 6144 * c, ORDERS[c], 48) for c in range(3)]
    WP = Pieces(wp, 0, ORDERS[0], 64)
    GA = [Pieces(act, 6144 * c, ORDERS[c], 48) for c in range(3)]

    raw = pltpu.make_async_copy(tokens, gb.at[pl.ds(0, 784)], lsem.at[7])
    raw.start()
    aloc[:, 0:2304] = w_qkv[...]
    aloc[:, 2304:3072] = w_out[...]
    mine = jnp.zeros((8, 128), F32)
    for n, ref in enumerate((v0, v1, v2, v3, v4, v5, v6)):
        for e in range(6):
            mine = jnp.where((subs == n) & (lanes == e), ref[e], mine)
    vst[...] = mine.astype(BF).astype(F32)
    ploc[...] = jnp.zeros_like(ploc)
    ploc[0:6, :] = w_proj[...]
    txt = text[...]
    ploc[8:12, :] = txt * lax.rsqrt(jnp.sum(txt * txt, axis=-1, keepdims=True) + 1e-06)
    enter(me)
    firsts = {}

    def meet(name, src, rx):
        firsts[name] = link.group(rx.at[pl.ds(0, 7)])
        for n in range(1, 8):
            t, peer = me.s_peer(n)
            part = src if name == "v" else src.at[:, ds(384 * t, 384, 128)]
            firsts[name].copy(part, rx.at[s], peer)

    here = dict(x=me.x, y=me.y, z=me.z)

    def launch(name, bufs, n):
        for c, b in enumerate(bufs):
            if n == 48:
                b.piece(me.core, **here)[...] = p48[:, 128 * c : 128 * c + 128].astype(BF)
            else:
                b.piece(me.core, **here)[...] = p64[...].astype(BF)
            todo.add(name, gather_steps(me, link, b))

    meet("a", aloc, arx)
    meet("v", vst, vrx)
    arx[s] = aloc[:, ds(384 * s, 384, 128)]
    urx[s] = w_up[:, ds(384 * s, 384, 128)]
    odd = me.x % 2
    drx[odd] = w_down[:, ds(384 * odd, 384, 128)]
    prx[me.x] = ploc[:, ds(128 * me.x, 128)]
    vrx[s] = vst[...]
    firsts["a"].wait_recv()
    for j in range(8):
        p48[6 * j : 6 * j + 6, :] = arx[j]
    launch("a", WA, 48)
    todo.step({"a"})
    meet("u", w_up, urx)
    cp = link.group(prx.at[pl.ds(0, 3)])
    for n in range(1, 4):
        t = (me.x + n) % 4
        cp.copy(ploc.at[:, ds(128 * t, 128)], prx.at[me.x], me.dev(x=t))
    cd = link.group(drx.at[0])
    cd.copy(w_down.at[:, ds(384 * (1 - odd), 384, 128)], drx.at[odd], me.dev(x=me.x + 1 - 2 * odd))
    firsts["v"].wait_recv()
    total = vrx[0]
    for j in range(1, 8):
        total = total + pltpu.roll(vrx[j], 6 * j, 1)
    gst[me.v] = total
    cv = link.group(gst.at[pl.ds(0, 15)])
    for n in range(1, 16):
        t, peer = me.v_peer(n)
        cv.copy(gst.at[me.v], gst.at[me.v], peer)

    mrow[...] = jnp.zeros_like(mrow)
    mrow[0:4, 0:196] = mask[...].astype(F32)
    mcol[...] = mrow[...].T
    for i in range(4):
        col = jnp.where(mcol[0:IMG, i : i + 1] > 0, 0.0, -1e30)
        bias[i] = jnp.broadcast_to(col, (IMG, 128))
    raw.wait()
    acc[0:784, :] = gb[0:784, :].astype(F32)
    acc[784:R, :] = jnp.zeros((R - 784, D), F32)
    for i in range(4):
        tok[IMG * i : IMG * i + IMG, :] = acc[196 * i : 196 * i + IMG, :].astype(BF)
    for ref in (q, att):
        ref[R : R + 48, :] = jnp.zeros((48, D), BF)
    pool[...] = jnp.zeros_like(pool)
    gvec[...] = jnp.zeros_like(gvec)
    row = lax.broadcasted_iota(jnp.int32, (384, 512), 0)
    col = lax.broadcasted_iota(jnp.int32, (384, 512), 1)
    e3[...] = jnp.where(((col >> 3) * 6 + (col & 7) == row) & ((col & 7) < 6), 1.0, 0.0).astype(BF)
    todo.step({"a"})
    firsts["u"].wait_recv()
    for j in range(8):
        p48[6 * j : 6 * j + 6, :] = urx[j]
    launch("u", WU, 48)
    cp.wait_recv()
    for j in range(4):
        p64[8 * j : 8 * j + 8, :] = prx[j, 0:8]
        p64[32 + 8 * j : 40 + 8 * j, :] = prx[j, 8:16]
    launch("p", [WP], 64)
    cd.wait_recv()
    for j in range(2):
        p48[24 * j : 24 * j + 24, :] = drx[j]
    launch("d", WD, 48)
    cv.wait_recv()
    vec[...] = jnp.zeros_like(vec)
    for n in range(16):
        t, off = 48 * n // 128, 48 * n % 128
        part = pltpu.roll(gst[n], off, 1) if off else gst[n]
        if off <= 80:
            vec[:, 128 * t : 128 * t + 128] += part
        else:
            vec[:, 128 * t : 128 * t + 128] += jnp.where(lanes >= off, part, 0.0)
            vec[:, 128 * t + 128 : 128 * t + 256] += jnp.where(lanes < off, part, 0.0)

    def gain(n):
        return vec[2 * n : 2 * n + 1, :], vec[2 * n + 1 : 2 * n + 2, :]

    def query():
        return vec[6:7, :]

    def tick(*names):
        for name in names:
            todo.step({name})

    def norm_one():
        g, b = gain(0)
        for i in range(4):
            rows = pl.ds(IMG * i, IMG)
            xh, _ = whiten(tok[rows, :].astype(F32))
            nrm[rows, :] = (xh * g + b).astype(BF)

    norm_one()

    def wide(bufs, ch):
        zlo, xp = ch // 2, ch % 2
        cols = []
        for l in range(6):
            at = [
                bufs[l % 3].load(core, x=2 * xp + l // 3, y=y, z=2 * h + zlo)
                for y in range(4) for core in range(2) for h in range(2)
            ]
            cols.append(jnp.concatenate(at, axis=0))
        return jnp.concatenate(cols, axis=1)

    def wide_store(bufs, ch, value):
        zlo, xp = ch // 2, ch % 2
        for l in range(6):
            n = 0
            for y in range(4):
                for core in range(2):
                    for h in range(2):
                        part = value[48 * n : 48 * n + 48, 128 * l : 128 * l + 128]
                        bufs[l % 3].store(part, core, x=2 * xp + l // 3, y=y, z=2 * h + zlo)
                        n += 1

    def tall(bufs, y):
        cols = []
        for l in range(6):
            at = [
                bufs[l % 3].load(core, x=2 * xh + l // 3, y=y, z=z)
                for core in range(2) for z in range(4) for xh in range(2)
            ]
            cols.append(jnp.concatenate(at, axis=0))
        return jnp.concatenate(cols, axis=1)

    def tall_store(bufs, y, value):
        for l in range(6):
            n = 0
            for core in range(2):
                for z in range(4):
                    for xh in range(2):
                        part = value[48 * n : 48 * n + 48, 128 * l : 128 * l + 128]
                        bufs[l % 3].store(part, core, x=2 * xh + l // 3, y=y, z=z)
                        n += 1

    def flat(ref, ch, rows=None):
        return jnp.concatenate([ref[R * (6 * ch + l) : R * (6 * ch + l) + R, :] for l in range(6)], axis=1)

    tick("a", "u", "a")
    todo.finish({"a"})
    for ch, dst in enumerate((q, k, v)):
        out = nn(nrm[...], wide(WA, ch))
        if ch == 0:
            out = out * 0.125
        dst[0:R, :] = out.astype(BF)
        if ch == 2:
            tick("u", "p", "d")
    lane = lax.broadcasted_iota(jnp.int32, (1, 128), 1)
    heads = [jnp.where(lane < 64, 1.0, 0.0).astype(BF), jnp.where(lane < 64, 0.0, 1.0).astype(BF)]

    def attend(img):
        rows, wide_rows = pl.ds(IMG * img, IMG), pl.ds(IMG * img, 256)

        def pair(pr):
            c = ds(128 * pr, 128)
            q2, k2, v2 = q[wide_rows, c], k[rows, c], v[rows, c]
            vt = v2.T
            b2 = jnp.concatenate([bias[img], bias[img]], axis=1)
            got = []
            for h in range(2):
                st = nt(k2, q2 * heads[h]) + b2
                e = jnp.exp(st - jnp.max(st, axis=0, keepdims=True))
                p = (e * (1.0 / jnp.sum(e, axis=0, keepdims=True))).astype(BF)
                pb[img % 2, 2 * pr + h] = p
                got.append(nn(vt[64 * h : 64 * h + 64, :], p).astype(BF))
            o = jnp.concatenate(got, axis=0).T
            att[rows, c] = o[0:IMG, :]

        for pr in range(6):
            pair(pr)

    saves = []
    for img in range(4):
        if img >= 2:
            saves[img - 2].wait()
        attend(img)
        if img < 2:
            c = pltpu.make_async_copy(pb.at[img], spill.at[img], lsem.at[img])
            c.start()
            saves.append(c)
        if img % 2 == 1:
            tick("u", "p", "d")

    res[...] = tok[...].astype(F32) + nn(att[0:R, :], wide(WA, 3))

    g, b = gain(1)
    for i in range(4):
        rows = pl.ds(IMG * i, IMG)
        xh, r = whiten(res[rows, :])
        xh2[rows, :] = xh.astype(BF)
        r2[rows, :] = r
        nrm[rows, :] = (xh * g + b).astype(BF)
    todo.finish({"u"})
    for ch in range(4):
        a, d = gelu_parts(nn(nrm[...], wide(WU, ch)))
        for l in range(6):
            at = pl.ds(R * (6 * ch + l), R)
            act[at, :] = a[:, 128 * l : 128 * l + 128].astype(BF)
            gel[at, :] = d[:, 128 * l : 128 * l + 128].astype(BF)
        if ch == 0:
            tick("p", "d")
    todo.finish({"d"})
    for y in range(4):
        res[...] += nn(flat(act, y), tall(WD, y))

    g, b = gain(2)
    for i in range(4):
        x = res[IMG * i : IMG * i + IMG, :]
        m = jnp.mean(x, axis=-1, keepdims=True)
        xc = x - m
        r = lax.rsqrt(jnp.mean(xc * xc, axis=-1, keepdims=True) + 1e-05)
        e = r * jnp.sum(xc * (g * query()), axis=-1, keepdims=True)
        lg = (e + jnp.sum(b * query(), axis=-1, keepdims=True)) / ROOT
        lg = jnp.where(mcol[0:IMG, i : i + 1] > 0, lg, -1e30)
        ex = jnp.exp(lg - jnp.max(lg, axis=0, keepdims=True))
        sh = ex / jnp.sum(ex, axis=0, keepdims=True)
        row = jnp.sum((sh * r) * xc, axis=0, keepdims=True)
        s1[i : i + 1, :] = row
        pool[i : i + 1, :] = row * g + b * jnp.sum(sh, axis=0, keepdims=True)
        for n, c in enumerate((m, r, e, sh)):
            cols[i, :, n : n + 1] = c
    todo.finish()
    link.drain()

    def proj_cols(x, lo):
        at = [
            WP.load(core, lo, 32, x=x, y=y, z=z)
            for y in range(4) for core in range(2) for z in range(4)
        ]
        return jnp.concatenate(at, axis=0)

    pooled = pool[...].astype(BF)
    padded = jnp.concatenate(
        [nn(pooled[:, 384 * n : 384 * n + 384], e3[...]).astype(BF) for n in range(2)], axis=1
    )
    embedded = jnp.concatenate([nn(padded, proj_cols(x, 0)) for x in range(4)], axis=1)
    ri = lax.rsqrt(jnp.sum(embedded * embedded, axis=-1, keepdims=True) + 1e-06)
    unit = (embedded * ri).astype(BF)
    big = jnp.exp(jnp.full((1, 1), scale[0], F32))
    dots = nt(unit[:, 0:128], proj_cols(0, 32))
    for x in range(1, 4):
        dots = dots + nt(unit[:, 128 * x : 128 * x + 128], proj_cols(x, 32))
    logits = big * dots
    row = lax.broadcasted_iota(jnp.int32, (8, 1024), 0)
    col = lax.broadcasted_iota(jnp.int32, (8, 1024), 1)
    valid = (row < 4) & ((col & 7) < 4)
    target = jnp.zeros((8, 1024), F32)
    first = 4 * ((me.y * 2 + me.core) * 16 + me.z * 4 + me.x)
    for i in range(4):
        t = pairing[first + i]
        target = jnp.where((row == i) & (col == 8 * (t >> 2) + (t & 3)), 1.0, target)
    e = jnp.where(valid, jnp.exp(logits), 0.0)
    row_sum = jnp.where(row[:, 0:1] < 4, jnp.sum(e, axis=-1, keepdims=True), 1.0)
    col_sum = jnp.sum(e, axis=0, keepdims=True)
    for j in range(8):
        cs[j : j + 1, :] = col_sum[:, 128 * j : 128 * j + 128]
    rows_lse = jnp.sum(jnp.log(row_sum), axis=0, keepdims=True)
    matched = jnp.sum(jnp.sum(logits * target, axis=-1, keepdims=True), axis=0, keepdims=True)
    send_tile = cs[...]
    send_tile = jnp.where((subs == 0) & (lanes == 4), rows_lse, send_tile)
    send_tile = jnp.where((subs == 0) & (lanes == 5), matched, send_tile)
    cs[...] = send_tile
    got = link.group(crx.at[pl.ds(0, 15)])
    for n in range(1, 16):
        t, peer = me.v_peer(n)
        got.copy(cs, crx.at[me.v], peer)
    crx[me.v] = send_tile
    got.wait_recv()
    total = crx[0]
    for n in range(1, 16):
        total = total + crx[n]
    cst[...] = total
    got = link.group(crx2.at[pl.ds(0, 7)])
    for n in range(1, 8):
        t, peer = me.s_peer(n)
        got.copy(cst, crx2.at[s], peer)
    crx2[s] = total
    got.wait_recv()
    total = crx2[0]
    for n in range(1, 8):
        total = total + crx2[n]
    cs_all = jnp.concatenate([total[j : j + 1, :] for j in range(8)], axis=1)
    ok = (lanes & 7) < 4
    cols_lse = jnp.sum(jnp.where(ok, jnp.log(jnp.where(ok, total, 1.0)), 0.0))
    loss = (total[0:1, 4:5] + cols_lse - 2.0 * total[0:1, 5:6]) / 1024.0
    ok = (col[0:1, :] & 7) < 4
    gl = e / row_sum + e / jnp.where(ok, cs_all, 1.0) - 2.0 * target
    gl = jnp.where(valid, gl, 0.0) * (1.0 / 1024.0)
    g_scale = jnp.sum(gl * logits)
    parts = split(gl, 2)
    gui = []
    for x in range(4):
        rhs = proj_cols(x, 32)
        gui.append(nn(parts[0], rhs) + nn(parts[1], rhs))
    gui = big * jnp.concatenate(gui, axis=1)
    ge = ri * gui - ri * ri * ri * embedded * jnp.sum(embedded * gui, axis=-1, keepdims=True)
    ge = ge.astype(BF)
    gp_pad = jnp.concatenate(
        [
            sum(nt(ge[:, 128 * x : 128 * x + 128], proj_cols(x, 0)) for x in range(4))
        ], axis=1
    )
    gp = []
    for n in range(2):
        gp.append(sum(nt(p, e3[...]) for p in split(gp_pad[:, 512 * n : 512 * n + 512], 3)))
    emb[...] = jnp.concatenate(gp, axis=1)
    both = jnp.concatenate([parts[0], parts[1]], axis=0)
    ub = jnp.concatenate([unit, unit], axis=0)
    for x in range(4):
        gproj = tn(padded, ge[:, 128 * x : 128 * x + 128]).astype(BF)
        gtext = (big * tn(both, ub[:, 128 * x : 128 * x + 128])).astype(BF)
        n = 0
        for y in range(4):
            for core in range(2):
                for z in range(4):
                    WP.store(gproj[32 * n : 32 * n + 32, :], core, 0, x=x, y=y, z=z)
                    WP.store(gtext[32 * n : 32 * n + 32, :], core, 32, x=x, y=y, z=z)
                    n += 1

    def keep(n, c):
        def finish(total):
            tot[n, :, 128 * c : 128 * c + 128] = total

        return finish

    def keep_p(total):
        ptot[...] = total

    def rx_part(ref, c, n):
        return ref.at[pl.ds(n * c, n)]

    todo.add("p", scatter_steps(me, link, WP, rxpc, rxp, keep_p))
    tick("p", "p")

    def own_rows(n):
        for j in range(8):
            ust[n - 1, j] = tot[n, 6 * j : 6 * j + 6, :]
        group = link.group(orx.at[n - 1, pl.ds(0, 7)])
        for m in range(1, 8):
            t, peer = me.s_peer(m)
            group.copy(ust.at[n - 1, t], orx.at[n - 1, s], peer)
        orx[n - 1, s] = ust[n - 1, s]
        return group

    def own_down():
        group = link.group(tot.at[3, pl.ds(0, 24)])
        group.copy(
            tot.at[0, ds(24 * (1 - odd), 24, 8)],
            tot.at[3, ds(24 * odd, 24, 8)],
            me.dev(x=me.x + 1 - 2 * odd),
        )
        tot[3, ds(24 * odd, 24, 8), :] = tot[0, ds(24 * odd, 24, 8), :]
        return group

    def own_proj():
        for j in range(4):
            pst[j, 0:8] = ptot[8 * j : 8 * j + 8, :]
            pst[j, 8:16] = ptot[32 + 8 * j : 40 + 8 * j, :]
        group = link.group(prx2.at[pl.ds(0, 3)])
        for n in range(1, 4):
            t = (me.x + n) % 4
            group.copy(pst.at[t], prx2.at[me.x], me.dev(x=t))
        prx2[me.x] = pst[me.x]
        return group

    g, b = gain(2)
    side_q = query() / ROOT
    for i in range(4):
        rows = pl.ds(IMG * i, IMG)
        gpi = emb[i : i + 1, :]
        m, r, e, sh = (cols[i, :, n : n + 1] for n in range(4))
        one, two = gpi * g, side_q * g
        xc = res[rows, :] - m
        w = r * jnp.sum(xc * one, axis=-1, keepdims=True)
        c = w + jnp.sum(b * gpi, axis=-1, keepdims=True)
        dl = sh * (c - jnp.sum(sh * c, axis=0, keepdims=True))
        pull = r * r * (sh * w + dl * (e / ROOT)) * (1.0 / D)
        one_c = one - jnp.mean(one, axis=-1, keepdims=True)
        two_c = two - jnp.mean(two, axis=-1, keepdims=True)
        out = (r * sh) * one_c + (r * dl) * two_c - pull * xc
        res[rows, :] = out
        gb[rows, :] = out.astype(BF)
        row = jnp.sum((r * dl) * xc, axis=0, keepdims=True)
        sum_dl = jnp.sum(dl, axis=0, keepdims=True)
        gvec[4, 0:1, :] += gpi * s1[i : i + 1, :] + side_q * row
        gvec[5, 0:1, :] += gpi * jnp.sum(sh, axis=0, keepdims=True) + side_q * sum_dl
        gvec[6, 0:1, :] += (row * g + b * sum_dl) / ROOT
    for y in range(4):
        ga = nt(gb[...], tall(WD, y))
        for l in range(6):
            at = pl.ds(R * (6 * y + l), R)
            gel[at, :] = (ga[:, 128 * l : 128 * l + 128] * gel[at, :].astype(F32)).astype(BF)
        tall_store(WD, y, tn(flat(act, y), gb[...]).astype(BF))
        tick(*(("p", "p"), (), ("p",), ("p",))[y])
    for c in range(3):
        todo.add("d", scatter_steps(me, link, WD[c], rx_part(rxc, c, 3072), rx_part(rxd, c, 3024), keep(0, c), give=credit.at[c]))
    tick("d", "d")
    for ch in range(4):
        gu = flat(gel, ch)
        part = nt(gu, wide(WU, ch))
        if ch == 0:
            acc[...] = part
        else:
            acc[...] += part
        wide_store(WU, ch, tn(nrm[...], gu).astype(BF))
        tick(*(("d",), (), ("d", "p"), ("d",))[ch])
        if ch == 2:
            got_proj = own_proj()
    for c in range(3):
        todo.add("u", scatter_steps(me, link, WU[c], rx_part(rxc, c, 3072), rx_part(rxu, c, 3024), keep(1, c), give=credit.at[3 + c], need=credit.at[c]))
    tick("u", "u")

    def fold_in(n, gg, gs):
        gvec[n] += gg
        gvec[n + 1] += gs

    g, _ = gain(1)
    for i in range(4):
        rows = pl.ds(IMG * i, IMG)
        y, xh = acc[rows, :], xh2[rows, :].astype(F32)
        out = res[rows, :] + whiten_back(y * g, xh, r2[rows, :])
        res[rows, :] = out
        gb[rows, :] = out.astype(BF)
        fold_in(2, fold(y * xh), fold(y))
    wide_store(GA, 3, tn(att[0:R, :], gb[...]).astype(BF))
    att[0:R, :] = nt(gb[...], wide(WA, 3)).astype(BF)
    norm_one()
    tick("u")
    low = lax.broadcasted_iota(jnp.int32, (256, 128), 0) < IMG
    side = lax.broadcasted_iota(jnp.int32, (256, 128), 1) < 64
    own = [jnp.where(low & side, 1.0, 0.0).astype(BF), jnp.where(low & ~side, 1.0, 0.0).astype(BF)]

    def attend_back(img):
        rows, wide_rows = pl.ds(IMG * img, IMG), pl.ds(IMG * img, 256)

        def pair(pr):
            c = ds(128 * pr, 128)
            q2, k2, v2, do = q[wide_rows, c], k[rows, c], v[rows, c], att[wide_rows, c]
            kt = k2.T
            dqt = []
            dk = jnp.zeros((IMG, 128), F32)
            dv = jnp.zeros((IMG, 128), F32)
            for h in range(2):
                doh, qh = do * own[h], q2 * heads[h]
                p = pb[img % 2, 2 * pr + h]
                dv = dv + nn(p, doh)
                pf = p.astype(F32)
                dp = nt(v2, doh)
                t = pf * dp
                dst = (t - pf * jnp.sum(t, axis=0, keepdims=True)).astype(BF)
                dk = dk + nn(dst, qh)
                dqt.append(nn(kt[64 * h : 64 * h + 64, :], dst))
            dq = (jnp.concatenate(dqt, axis=0) * 0.125).astype(BF).T
            q[rows, c] = dq[0:IMG, :]
            k[rows, c] = dk.astype(BF)
            v[rows, c] = dv.astype(BF)

        for pr in range(6):
            pair(pr)

    loads = {}
    for img in (2, 3, 0, 1):
        if img in loads:
            loads[img].wait()
        attend_back(img)
        if img >= 2:
            c = pltpu.make_async_copy(spill.at[img - 2], pb.at[img - 2], lsem.at[img])
            c.start()
            loads[img - 2] = c
        tick(*((), ("u", "d"), ("d", "u"), ("u",))[img])
    got_down = own_down()
    for ch, src in enumerate((q, k, v)):
        wide_store(GA, ch, tn(nrm[...], src[0:R, :]).astype(BF))
    for c in range(3):
        todo.add("a", scatter_steps(me, link, GA[c], rx_part(rxc, c, 3072), rx_part(rxa, c, 3024), keep(2, c), need=credit.at[3 + c]))
    tick("a", "a", "u")
    got_up = own_rows(1)
    for ch, src in enumerate((q, k, v)):
        part = nt(src[0:R, :], wide(WA, ch))
        if ch == 0:
            acc[...] = part
        else:
            acc[...] += part
        if ch == 1:
            tick("a")
    g, _ = gain(0)
    outs = []
    for i in range(4):
        rows = pl.ds(IMG * i, IMG)
        xh, r = whiten(tok[rows, :].astype(F32))
        y = acc[rows, :]
        out = res[rows, :] + whiten_back(y * g, xh, r)
        fold_in(0, fold(y * xh), fold(y))
        acc[196 * i : 196 * i + 196, :] = out[0:196, :]
        if i % 2 == 1:
            rows = pl.ds(392 * (i // 2), 392)
            outs.append(pltpu.make_async_copy(acc.at[rows], o_tok.at[rows], lsem.at[4 + i // 2]))
            outs[-1].start()
    tick("a")

    for n in range(7):
        vec[n : n + 1, :] = jnp.sum(gvec[n], axis=0, keepdims=True)
    vec[7:8, :] = jnp.zeros((1, D), F32)
    for n in range(16):
        t, off = 48 * n // 128, 48 * n % 128
        part = vec[:, 128 * t : 128 * t + 128]
        part = pltpu.roll(part, (128 - off) % 128, 1) if off else part
        if off > 80:
            more = pltpu.roll(vec[:, 128 * t + 128 : 128 * t + 256], 128 - off, 1)
            part = jnp.where(lanes < 128 - off, part, more)
        gst2[n] = jnp.where(subs == 7, g_scale, part)
    cv = link.group(grx.at[pl.ds(0, 15)])
    for n in range(1, 16):
        t, peer = me.v_peer(n)
        cv.copy(gst2.at[t], grx.at[me.v], peer)
    grx[me.v] = gst2[me.v]

    tick("a", "a")
    cv.wait_recv()
    total = grx[0]
    for n in range(1, 16):
        total = total + grx[n]
    vst[...] = total
    got_vec = link.group(grx2.at[pl.ds(0, 7)])
    for n in range(1, 8):
        t, peer = me.s_peer(n)
        got_vec.copy(vst, grx2.at[s], peer)
    grx2[s] = total
    todo.finish({"a"})
    last = own_rows(2)
    got_vec.wait_recv()
    total = grx2[0]
    for n in range(1, 8):
        total = total + grx2[n]
    total = pltpu.roll(total, (128 - 6 * s) % 128, 1)
    scal[...] = jnp.where((subs == 7) & (lanes == 1), loss, total)
    to_smem = pltpu.make_async_copy(scal, scal_s, lsem.at[6])
    to_smem.start()
    got_up.wait_recv()
    got_down.wait_recv()
    for j in range(8):
        o_up[:, 384 * j : 384 * j + 384] = orx[0, j]
    for j in range(2):
        o_down[:, 384 * j : 384 * j + 384] = tot[3, 24 * j : 24 * j + 24, :]
    got_proj.wait_recv()
    for j in range(4):
        o_proj[:, 128 * j : 128 * j + 128] = prx2[j, 0:6]
    gt = jnp.concatenate([prx2[j, 8:12] for j in range(4)], axis=1)
    txt = text[...]
    r = lax.rsqrt(jnp.sum(txt * txt, axis=-1, keepdims=True) + 1e-06)
    o_text[...] = r * gt - r * r * r * txt * jnp.sum(txt * gt, axis=-1, keepdims=True)
    to_smem.wait()
    for n, ref in enumerate((o0, o1, o2, o3, o4, o5, o6)):
        for e in range(6):
            ref[e] = scal_s[n, e]
    o_scale[0] = scal_s[7, 0]
    o_loss[0] = scal_s[7, 1]
    last.wait_recv()
    for j in range(8):
        if j < 6:
            o_qkv[:, 384 * j : 384 * j + 384] = orx[1, j]
        else:
            o_out[:, 384 * (j - 6) : 384 * (j - 6) + 384] = orx[1, j]
    for c in outs:
        c.wait()
    link.drain()


def hand_over(*refs):
    src, dst, buf, sem = refs[:16], refs[16:32], refs[32], refs[33]
    rows = [pl.ds(200 * n, 200 if n < 3 else 184) for n in range(4)]
    there = [pltpu.make_async_copy(src[1].at[r], buf.at[r], sem.at[n]) for n, r in enumerate(rows)]
    back = [pltpu.make_async_copy(buf.at[r], dst[1].at[r], sem.at[4 + n]) for n, r in enumerate(rows)]
    for c in there:
        c.start()
    for n, (a, b) in enumerate(zip(src, dst)):
        if n in (0, 15):
            b[0] = a[0]
        elif n >= 8:
            for e in range(6):
                b[e] = a[e]
        elif n != 1:
            b[...] = a[...]
    for a, b in zip(there, back):
        a.wait()
        b.start()
    for c in back:
        c.wait()


def shards(tokens, keep_mask, pairing, text_vectors, logit_scale, w_qkv, w_out, w_up, w_down, w_proj, *vectors):
    vm = pl.BlockSpec(memory_space=pltpu.VMEM)
    sm = pl.BlockSpec(memory_space=pltpu.SMEM)
    hbm = pl.BlockSpec(memory_space=pl.ANY)
    S = jax.ShapeDtypeStruct
    V = pltpu.VMEM
    outs = pl.pallas_call(
        kernel,
        out_shape=[
            S((1,), F32), S((784, D), F32), S((4, 512), F32), S((6, 2304), F32), S((6, 768), F32),
            S((6, 3072), F32), S((24, 768), F32), S((6, 512), F32), *[S((6,), F32)] * 7, S((1,), F32),
            S((2, 12, IMG, 256), BF),
        ],
        in_specs=[sm] * 9 + [hbm] + [vm] * 7,
        out_specs=[sm, hbm, vm, vm, vm, vm, vm, vm, *[sm] * 8, hbm],
        scratch_shapes=[
            V((18432, 128), BF), V((18432, 128), BF), V((18432, 128), BF), V((8192, 128), BF), V((R, D), BF),
            V((R + 48, D), BF), V((R, D), BF), V((R, D), BF), V((2, 12, IMG, 256), BF),
            V((R, D), BF), V((R, D), BF), V((R + 48, D), BF), V((R, D), BF),
            V((24 * R, 128), BF), V((24 * R, 128), BF), V((R, D), F32), V((R, D), F32), V((R, 1), F32),
            V((3 * 3072, 128), BF), V((3 * 3024, 128), BF), V((3 * 3024, 128), BF), V((3 * 3024, 128), BF),
            V((4096, 128), BF), V((4032, 128), BF),
            V((6, 3072), F32), V((8, 6, 384), F32), V((8, 6, 384), F32), V((2, 24, 384), F32),
            V((16, 512), F32), V((4, 16, 128), F32), V((8, 8, 128), F32), V((8, 128), F32),
            V((48, 384), F32), V((64, 128), F32), V((8, D), F32), V((7, 8, D), F32),
            V((8, 256), F32), V((256, 8), F32), V((4, IMG, 8), F32), V((4, IMG, 128), F32),
            V((8, D), F32), V((8, D), F32), V((384, 512), BF), V((8, D), F32),
            V((8, 128), F32), pltpu.SMEM((8, 128), F32),
            V((8, 128), F32), V((16, 8, 128), F32), V((8, 128), F32), V((8, 8, 128), F32),
            V((4, 48, 384), F32), V((64, 128), F32), V((2, 8, 6, 384), F32), V((2, 8, 6, 384), F32),
            V((4, 16, 128), F32), V((4, 16, 128), F32), V((16, 8, 128), F32), V((16, 8, 128), F32),
            V((16, 8, 128), F32), V((8, 8, 128), F32),
            pltpu.SemaphoreType.DMA((N_SEM,)), pltpu.SemaphoreType.DMA((N_SEM,)), pltpu.SemaphoreType.DMA((8,)),
            pltpu.SemaphoreType.REGULAR((6,)),
        ],
        compiler_params=pltpu.CompilerParams(
            collective_id=0, has_side_effects=True, vmem_limit_bytes=(64 << 20) - (256 << 10)
        ),
        cost_estimate=pl.CostEstimate(flops=40_000_000_000, bytes_accessed=20_000_000, transcendentals=0),
    )(pairing, logit_scale, *vectors, tokens, keep_mask, text_vectors, w_qkv, w_out, w_up, w_down, w_proj)
    outs = outs[:16]
    return pl.pallas_call(
        hand_over,
        out_shape=[S(o.shape, o.dtype) for o in outs],
        in_specs=[sm, hbm] + [vm] * 6 + [sm] * 8,
        out_specs=[sm, hbm] + [vm] * 6 + [sm] * 8,
        scratch_shapes=[V((784, D), F32), pltpu.SemaphoreType.DMA((8,))],
    )(*outs)


def solution(mesh):
    rows, vector, whole = P(("dp", "fsdp"), None), P(("dp", "fsdp")), P()
    in_specs = (rows, rows, whole, rows, whole, *[rows] * 5, *[vector] * 7)
    out_specs = (whole, rows, rows, *[rows] * 5, *[vector] * 7, whole)
    return jax.shard_map(shards, mesh=mesh, in_specs=in_specs, out_specs=out_specs, check_vma=False)
```

```python
from functools import partial
import math

import jax
import jax.numpy as jnp
from jax import lax
from jax.experimental import pallas as pl
from jax.experimental.pallas import tpu as pltpu
from jax.sharding import PartitionSpec as P

MESH = pl.DeviceIdType.MESH
BF = jnp.bfloat16
F32 = jnp.float32
IMG = 208
R = 4 * IMG
D = 768
ROOT = math.sqrt(768.0)


class Place:
    def __init__(self):
        dp = lax.axis_index("dp")
        fs = lax.axis_index("fsdp")
        self.y, self.core = dp // 2, dp % 2
        self.z, self.x = fs // 4, fs % 4
        self.s = (self.z % 2) * 4 + self.x
        self.v = dp * 2 + self.z // 2

    def dev(self, **moved):
        at = dict(x=self.x, y=self.y, z=self.z, core=self.core)
        at.update(moved)
        return (at["y"] * 2 + at["core"], at["z"] * 4 + at["x"])

    def hop(self, dim, step):
        return self.dev(**{dim: (getattr(self, dim) + step + 4) % 4})

    def sibling(self):
        return self.dev(core=1 - self.core)

    def s_peer(self, k):
        t = (self.s + k) % 8
        return t, self.dev(z=(self.z // 2) * 2 + t // 4, x=t % 4)

    def v_peer(self, k):
        t = (self.v + k) % 16
        return t, (t // 2, ((t % 2) * 2 + self.z % 2) * 4 + self.x)


class Group:
    def __init__(self, link, total):
        self.link, self.total = link, total
        self.k = link.n
        link.n += 1
        link.open.append(self)
        self.sems = dict(send_sem=link.send.at[self.k], recv_sem=link.recv.at[self.k])

    def copy(self, src, dst, dev):
        c = pltpu.make_async_remote_copy(
            src_ref=src, dst_ref=dst, device_id=dev, device_id_type=MESH, **self.sems
        )
        c.start()

    def whole(self):
        return pltpu.make_async_remote_copy(
            src_ref=self.total,
            dst_ref=self.total,
            device_id=self.link.any_device,
            device_id_type=MESH,
            **self.sems,
        )

    def wait_recv(self):
        self.whole().wait_recv()


class Link:
    def __init__(self, send, recv, any_device):
        self.send, self.recv, self.n = send, recv, 0
        self.any_device = any_device
        self.open = []

    def group(self, total):
        return Group(self, total)

    def drain(self):
        for g in self.open:
            g.whole().wait_send()
        self.open = []


ORDERS = (("x", "y", "z"), ("y", "z", "x"), ("z", "x", "y"))


def enter(me):
    sem = pltpu.get_barrier_semaphore()
    peers = []
    for n in range(1, 64):
        dx, dy, dz = n % 4, n // 4 % 4, n // 16
        if dx * dy * dz == 0:
            peers.append(me.dev(x=(me.x + dx) % 4, y=(me.y + dy) % 4, z=(me.z + dz) % 4))
    for n in range(8):
        peers.append(me.dev(y=(me.y + n % 4) % 4, z=(me.z + n // 4 * 2) % 4, core=1 - me.core))
    for p in peers:
        pl.semaphore_signal(sem, inc=1, device_id=p, device_id_type=MESH)
    pl.semaphore_wait(sem, len(peers))


def ds(start, size, unit=None):
    if isinstance(start, int):
        return pl.ds(start, size)
    return pl.ds(pl.multiple_of(start, unit or size), size)


class Pieces:
    def __init__(self, ref, base, order, rows):
        self.ref, self.base, self.order, self.rows = ref, base, order, rows

    def start(self, core, **at):
        d1, d2, d3 = (at[d] for d in self.order)
        return self.base + (((core * 4 + d3) * 4 + d2) * 4 + d1) * self.rows

    def piece(self, core, **at):
        return self.ref.at[ds(self.start(core, **at), self.rows, 16)]

    def load(self, core, lo=0, n=None, **at):
        return self.ref[pl.ds(self.start(core, **at) + lo, n or self.rows), :]

    def store(self, value, core, lo=0, **at):
        self.ref[pl.ds(self.start(core, **at) + lo, value.shape[0]), :] = value

    def block(self, core, stage, me, b):
        at = [getattr(me, d) for d in self.order]
        at[stage] = b
        for k in range(stage):
            at[k] = 0
        return self.start(core, **dict(zip(self.order, at))), self.rows * 4**stage


def rows_of(ref, block):
    return ref.at[ds(block[0], block[1], 16)]


def plane_peer(me, order, n):
    a, b = order[:2]
    i, j = (getattr(me, a) + n % 4) % 4, (getattr(me, b) + n // 4) % 4
    return {a: i, b: j}, me.dev(**{a: i, b: j})


def cut(block, which):
    start, size = block
    return (start + which * (size // 2), size // 2)


def gather_steps(me, link, buf, at_once):
    ref, d, rows = buf.ref, buf.order[2], buf.rows
    i, size = getattr(me, d), 16 * buf.rows
    lo, hi, far = (i + 3) % 4, (i + 1) % 4, (i + 2) % 4
    right, left = me.hop(d, 1), me.hop(d, -1)

    def bytes_of(pieces):
        return ref.at[pl.ds(buf.base, pieces * rows)]

    def send(group, block, dev):
        group.copy(rows_of(ref, block), rows_of(ref, block), dev)

    def block(b):
        return buf.block(me.core, 2, me, b)

    if at_once:
        own = buf.block(me.core, 0, me, getattr(me, buf.order[0]))
        others = link.group(bytes_of(15))
        for n in range(1, 16):
            send(others, own, plane_peer(me, buf.order, n)[1])
        yield
        others.wait_recv()
    for stage in () if at_once else (0, 1):
        axis = buf.order[stage]
        own = buf.block(me.core, stage, me, getattr(me, axis))
        others = link.group(bytes_of(3 * 4**stage))
        for n in (2, 1, 3):
            send(others, own, me.hop(axis, n))
        yield
        others.wait_recv()
    from_lo, from_hi = link.group(bytes_of(16)), link.group(bytes_of(16))
    send(from_lo, block(i), right)
    send(from_hi, block(i), left)
    sib = link.group(bytes_of(64))
    send(sib, block(i), me.sibling())
    yield
    from_lo.wait_recv()
    rest = link.group(bytes_of(16))
    send(rest, cut(block(lo), 0), right)
    from_hi.wait_recv()
    send(rest, cut(block(hi), 1), left)
    send(sib, block(lo), me.sibling())
    send(sib, block(hi), me.sibling())
    yield
    rest.wait_recv()
    send(sib, block(far), me.sibling())
    yield
    sib.wait_recv()


def add_rows(dst_ref, dst, *srcs):
    size = dst[1]
    rows = ds(dst[0], size, 16)
    if len(srcs) == 1:
        ref, start = srcs[0]
        dst_ref[rows, :] = dst_ref[rows, :] + ref[ds(start, size, 16), :]
        return
    total = dst_ref[rows, :].astype(F32)
    for ref, start in srcs:
        total = total + ref[ds(start, size, 16), :].astype(F32)
    dst_ref[rows, :] = total.astype(BF)


def scatter_steps(me, link, buf, rx_core, rx, finish, at_once, give=None, need=None):
    ref, rows, d = buf.ref, buf.rows, buf.order[2]
    i, size = getattr(me, d), 16 * buf.rows
    lo, hi, far = (i + 3) % 4, (i + 1) % 4, (i + 2) % 4
    right, left = me.hop(d, 1), me.hop(d, -1)

    def bytes_of(pieces):
        return ref.at[pl.ds(buf.base, pieces * rows)]

    def block(b, core=me.core):
        return buf.block(core, 2, me, b)

    def slot(n):
        return (n * size, size)

    if need is not None:
        pl.semaphore_wait(need, 1)
    def cross(group, b):
        group.copy(rows_of(ref, block(b, 1 - me.core)), rows_of(rx_core, (b * size, size)), me.sibling())

    first, rest = link.group(bytes_of(16)), link.group(bytes_of(48))
    cross(first, far)
    yield
    for b in (hi, lo, i):
        cross(rest, b)
    yield
    first.wait_recv()

    def settle(b):
        add_rows(ref, block(b), (rx_core, b * size))

    def send(group, src, dst, dev):
        group.copy(rows_of(ref, src), rows_of(rx, dst), dev)

    settle(far)
    merge = link.group(bytes_of(16))
    send(merge, cut(block(far), 0), cut(slot(0), 0), right)
    send(merge, cut(block(far), 1), cut(slot(0), 1), left)
    yield
    rest.wait_recv()
    settle(hi)
    ends = link.group(bytes_of(32))
    send(ends, cut(block(hi), 1), cut(slot(1), 1), right)
    settle(lo)
    send(ends, cut(block(lo), 0), cut(slot(2), 0), left)
    settle(i)
    if give is not None:
        pl.semaphore_signal(give, inc=1, device_id=me.sibling(), device_id_type=MESH)
    yield
    merge.wait_recv()
    add_rows(ref, cut(block(hi), 0), (rx, cut(slot(0), 0)[0]))
    send(ends, cut(block(hi), 0), cut(slot(1), 0), right)
    add_rows(ref, cut(block(lo), 1), (rx, cut(slot(0), 1)[0]))
    send(ends, cut(block(lo), 1), cut(slot(2), 1), left)
    yield
    ends.wait_recv()
    add_rows(ref, block(i), (rx, size), (rx, 2 * size))
    base = 3 * size
    if at_once:
        others = link.group(bytes_of(15))
        for n in range(1, 16):
            at, peer = plane_peer(me, buf.order, n)
            src = (buf.start(me.core, **{**at, d: i}), rows)
            send(others, src, (base + (n - 1) * rows, rows), peer)
        yield
        others.wait_recv()
        last = 15
    for stage in () if at_once else (1, 0):
        axis = buf.order[stage]
        j, part = getattr(me, axis), rows * 4**stage
        others = link.group(bytes_of(3 * 4**stage))
        for n in (2, 1, 3):
            src = buf.block(me.core, stage, me, (j + n) % 4)
            send(others, src, (base + (n - 1) * part, part), me.hop(axis, n))
        yield
        others.wait_recv()
        last = 3
        if stage == 1:
            add_rows(ref, buf.block(me.core, 1, me, j), *[(rx, base + n * part) for n in range(3)])
            base += 3 * part
    own = buf.block(me.core, 0, me, getattr(me, buf.order[0]))
    total = ref[ds(own[0], rows, 16), :].astype(F32)
    for n in range(last):
        total = total + rx[pl.ds(base + n * rows, rows), :].astype(F32)
    finish(total)


class Queue:
    def __init__(self):
        self.live = []

    def add(self, name, gen):
        self.live.append((name, gen))

    def step(self, names=None):
        keep = []
        for name, gen in self.live:
            if names is None or name in names:
                try:
                    next(gen)
                except StopIteration:
                    continue
            keep.append((name, gen))
        self.live = keep

    def finish(self, names=None):
        while any(names is None or n in names for n, _ in self.live):
            self.step(names)


def nn(a, b):
    return lax.dot_general(a, b, (((1,), (0,)), ((), ())), preferred_element_type=F32)


def nt(a, b):
    return lax.dot_general(a, b, (((1,), (1,)), ((), ())), preferred_element_type=F32)


def tn(a, b):
    return lax.dot_general(a, b, (((0,), (0,)), ((), ())), preferred_element_type=F32)


def whiten(x):
    centred = x - jnp.mean(x, axis=-1, keepdims=True)
    r = lax.rsqrt(jnp.mean(centred * centred, axis=-1, keepdims=True) + 1e-05)
    return centred * r, r


def whiten_back(y, xh, r):
    return r * (y - jnp.mean(y, axis=-1, keepdims=True) - xh * jnp.mean(y * xh, axis=-1, keepdims=True))


def fold(x):
    return jnp.sum(x.reshape(x.shape[0] // 8, 8, x.shape[1]), axis=0)


def split(x, parts):
    got = []
    for _ in range(parts):
        h = x.astype(BF)
        got.append(h)
        x = x - h.astype(F32)
    return got


def gelu_parts(u):
    a = jnp.abs(u)
    den = 1.0 + (0.3275911 * math.sqrt(0.5)) * a
    t = pltpu.reciprocal(den, approx=True)
    t = t * (2.0 - den * t)
    e = jnp.exp2((-0.5 * math.log2(math.e)) * (u * u))
    poly = t * (0.5 * 0.254829592 + t * (-0.5 * 0.284496736 + t * (0.5 * 1.421413741 + t * (-0.5 * 1.453152027 + t * (0.5 * 1.061405429)))))
    tail = poly * e
    phi = jnp.where(u < 0, tail, 1.0 - tail)
    return u * phi, phi + u * (e * (1.0 / math.sqrt(2.0 * math.pi)))


def blocks(n, body, unroll=1):
    lax.fori_loop(0, n, lambda k, c: (body(k), 0)[1], 0, unroll=unroll)


N_SEM = 136


def kernel(
    pairing, scale, v0, v1, v2, v3, v4, v5, v6,
    tokens, mask, text, w_qkv, w_out, w_up, w_down, w_proj,
    o_loss, o_tok, o_text, o_qkv, o_out, o_up, o_down, o_proj, o0, o1, o2, o3, o4, o5, o6, o_scale, spill,
    wa, wu, wd, wp, tok, q, k, v, pb, xh2, nrm, att, gb, act, gel, res, acc, r2,
    rxc, rxd, rxu, rxa, rxpc, rxp,
    aloc, arx, urx, drx, ploc, prx, vrx, vst, p48, p64, vec, gvec,
    mrow, mcol, cols, bias, pool, s1, e3, emb, scal, scal_s, cs, crx, cst, crx2,
    tot, ptot, orx, ust, pst, prx2, gst, grx, gst2, grx2,
    send, recv, lsem, credit,
):
    me = Place()
    link = Link(send, recv, me.sibling())
    todo = Queue()
    s = me.s
    lanes = lax.broadcasted_iota(jnp.int32, (8, 128), 1)
    subs = lax.broadcasted_iota(jnp.int32, (8, 128), 0)

    WA = [Pieces(wa, 6144 * c, ORDERS[c], 48) for c in range(3)]
    WU = [Pieces(wu, 6144 * c, ORDERS[c], 48) for c in range(3)]
    WD = [Pieces(wd, 6144 * c, ORDERS[c], 48) for c in range(3)]
    WP = Pieces(wp, 0, ORDERS[0], 64)
    GA = [Pieces(act, 6144 * c, ORDERS[c], 48) for c in range(3)]

    raw = pltpu.make_async_copy(tokens, gb.at[pl.ds(0, 784)], lsem.at[7])
    raw.start()
    aloc[:, 0:2304] = w_qkv[...]
    aloc[:, 2304:3072] = w_out[...]
    mine = jnp.zeros((8, 128), F32)
    for n, ref in enumerate((v0, v1, v2, v3, v4, v5, v6)):
        for e in range(6):
            mine = jnp.where((subs == n) & (lanes == e), ref[e], mine)
    vst[...] = mine.astype(BF).astype(F32)
    ploc[...] = jnp.zeros_like(ploc)
    ploc[0:6, :] = w_proj[...]
    txt = text[...]
    ploc[8:12, :] = txt * lax.rsqrt(jnp.sum(txt * txt, axis=-1, keepdims=True) + 1e-06)
    enter(me)
    firsts = {}

    def meet(name, src, rx):
        firsts[name] = link.group(rx.at[pl.ds(0, 7)])
        for n in range(1, 8):
            t, peer = me.s_peer(n)
            part = src if name == "v" else src.at[:, ds(384 * t, 384, 128)]
            firsts[name].copy(part, rx.at[s], peer)

    here = dict(x=me.x, y=me.y, z=me.z)

    def launch(name, bufs, n):
        for c, b in enumerate(bufs):
            if n == 48:
                b.piece(me.core, **here)[...] = p48[:, 128 * c : 128 * c + 128].astype(BF)
            else:
                b.piece(me.core, **here)[...] = p64[...].astype(BF)
            todo.add(name, gather_steps(me, link, b, name == "a"))

    meet("a", aloc, arx)
    meet("v", vst, vrx)
    arx[s] = aloc[:, ds(384 * s, 384, 128)]
    urx[s] = w_up[:, ds(384 * s, 384, 128)]
    odd = me.x % 2
    drx[odd] = w_down[:, ds(384 * odd, 384, 128)]
    prx[me.x] = ploc[:, ds(128 * me.x, 128)]
    vrx[s] = vst[...]
    firsts["a"].wait_recv()
    for j in range(8):
        p48[6 * j : 6 * j + 6, :] = arx[j]
    launch("a", WA, 48)
    todo.step({"a"})
    meet("u", w_up, urx)
    cp = link.group(prx.at[pl.ds(0, 3)])
    for n in range(1, 4):
        t = (me.x + n) % 4
        cp.copy(ploc.at[:, ds(128 * t, 128)], prx.at[me.x], me.dev(x=t))
    cd = link.group(drx.at[0])
    cd.copy(w_down.at[:, ds(384 * (1 - odd), 384, 128)], drx.at[odd], me.dev(x=me.x + 1 - 2 * odd))
    firsts["v"].wait_recv()
    total = vrx[0]
    for j in range(1, 8):
        total = total + pltpu.roll(vrx[j], 6 * j, 1)
    gst[me.v] = total
    cv = link.group(gst.at[pl.ds(0, 15)])
    for n in range(1, 16):
        t, peer = me.v_peer(n)
        cv.copy(gst.at[me.v], gst.at[me.v], peer)

    mrow[...] = jnp.zeros_like(mrow)
    mrow[0:4, 0:196] = mask[...].astype(F32)
    mcol[...] = mrow[...].T
    for i in range(4):
        col = jnp.where(mcol[0:IMG, i : i + 1] > 0, 0.0, -1e30)
        bias[i] = jnp.broadcast_to(col, (IMG, 128))
    for ref in (q, att):
        ref[R : R + 48, :] = jnp.zeros((48, D), BF)
    pool[...] = jnp.zeros_like(pool)
    gvec[...] = jnp.zeros_like(gvec)
    row = lax.broadcasted_iota(jnp.int32, (384, 512), 0)
    col = lax.broadcasted_iota(jnp.int32, (384, 512), 1)
    e3[...] = jnp.where(((col >> 3) * 6 + (col & 7) == row) & ((col & 7) < 6), 1.0, 0.0).astype(BF)
    todo.step({"a"})
    firsts["u"].wait_recv()
    for j in range(8):
        p48[6 * j : 6 * j + 6, :] = urx[j]
    launch("u", WU, 48)
    cp.wait_recv()
    for j in range(4):
        p64[8 * j : 8 * j + 8, :] = prx[j, 0:8]
        p64[32 + 8 * j : 40 + 8 * j, :] = prx[j, 8:16]
    launch("p", [WP], 64)
    cd.wait_recv()
    for j in range(2):
        p48[24 * j : 24 * j + 24, :] = drx[j]
    launch("d", WD, 48)
    todo.step({"u"})
    todo.step({"p"})
    todo.step({"d"})
    raw.wait()
    acc[0:784, :] = gb[0:784, :].astype(F32)
    acc[784:R, :] = jnp.zeros((R - 784, D), F32)
    for i in range(4):
        tok[IMG * i : IMG * i + IMG, :] = acc[196 * i : 196 * i + IMG, :].astype(BF)
    cv.wait_recv()
    vec[...] = jnp.zeros_like(vec)
    for n in range(16):
        t, off = 48 * n // 128, 48 * n % 128
        part = pltpu.roll(gst[n], off, 1) if off else gst[n]
        if off <= 80:
            vec[:, 128 * t : 128 * t + 128] += part
        else:
            vec[:, 128 * t : 128 * t + 128] += jnp.where(lanes >= off, part, 0.0)
            vec[:, 128 * t + 128 : 128 * t + 256] += jnp.where(lanes < off, part, 0.0)

    def gain(n):
        return vec[2 * n : 2 * n + 1, :], vec[2 * n + 1 : 2 * n + 2, :]

    def query():
        return vec[6:7, :]

    def tick(*names):
        for name in names:
            todo.step({name})

    def norm_one():
        g, b = gain(0)
        for i in range(4):
            rows = pl.ds(IMG * i, IMG)
            xh, _ = whiten(tok[rows, :].astype(F32))
            nrm[rows, :] = (xh * g + b).astype(BF)

    norm_one()

    def wide(bufs, ch):
        zlo, xp = ch // 2, ch % 2
        cols = []
        for l in range(6):
            at = [
                bufs[l % 3].load(core, x=2 * xp + l // 3, y=y, z=2 * h + zlo)
                for y in range(4) for core in range(2) for h in range(2)
            ]
            cols.append(jnp.concatenate(at, axis=0))
        return jnp.concatenate(cols, axis=1)

    def wide_store(bufs, ch, value):
        zlo, xp = ch // 2, ch % 2
        for l in range(6):
            n = 0
            for y in range(4):
                for core in range(2):
                    for h in range(2):
                        part = value[48 * n : 48 * n + 48, 128 * l : 128 * l + 128]
                        bufs[l % 3].store(part, core, x=2 * xp + l // 3, y=y, z=2 * h + zlo)
                        n += 1

    def tall(bufs, y):
        cols = []
        for l in range(6):
            at = [
                bufs[l % 3].load(core, x=2 * xh + l // 3, y=y, z=z)
                for core in range(2) for z in range(4) for xh in range(2)
            ]
            cols.append(jnp.concatenate(at, axis=0))
        return jnp.concatenate(cols, axis=1)

    def tall_store(bufs, y, value):
        for l in range(6):
            n = 0
            for core in range(2):
                for z in range(4):
                    for xh in range(2):
                        part = value[48 * n : 48 * n + 48, 128 * l : 128 * l + 128]
                        bufs[l % 3].store(part, core, x=2 * xh + l // 3, y=y, z=z)
                        n += 1

    def flat(ref, ch, rows=None):
        return jnp.concatenate([ref[R * (6 * ch + l) : R * (6 * ch + l) + R, :] for l in range(6)], axis=1)

    tick("a", "u", "p", "d", "a", "u")
    todo.finish({"a"})
    for ch, dst in enumerate((q, k, v)):
        out = nn(nrm[...], wide(WA, ch))
        if ch == 0:
            out = out * 0.125
        dst[0:R, :] = out.astype(BF)
    lane = lax.broadcasted_iota(jnp.int32, (1, 128), 1)
    heads = [jnp.where(lane < 64, 1.0, 0.0).astype(BF), jnp.where(lane < 64, 0.0, 1.0).astype(BF)]

    def attend(img):
        rows, wide_rows = pl.ds(IMG * img, IMG), pl.ds(IMG * img, 256)

        def pair(pr):
            c = ds(128 * pr, 128)
            q2, k2, v2 = q[wide_rows, c], k[rows, c], v[rows, c]
            vt = v2.T
            b2 = jnp.concatenate([bias[img], bias[img]], axis=1)
            got = []
            for h in range(2):
                st = nt(k2, q2 * heads[h]) + b2
                e = jnp.exp(st - jnp.max(st, axis=0, keepdims=True))
                p = (e * (1.0 / jnp.sum(e, axis=0, keepdims=True))).astype(BF)
                pb[img % 2, 2 * pr + h] = p
                got.append(nn(vt[64 * h : 64 * h + 64, :], p).astype(BF))
            o = jnp.concatenate(got, axis=0).T
            att[rows, c] = o[0:IMG, :]

        for pr in range(6):
            pair(pr)

    saves = []
    for img in range(4):
        if img >= 2:
            saves[img - 2].wait()
        attend(img)
        if img < 2:
            c = pltpu.make_async_copy(pb.at[img], spill.at[img], lsem.at[img])
            c.start()
            saves.append(c)
        if img % 2 == 0:
            tick("u", "p", "d")

    res[...] = tok[...].astype(F32) + nn(att[0:R, :], wide(WA, 3))

    g, b = gain(1)
    for i in range(4):
        rows = pl.ds(IMG * i, IMG)
        xh, r = whiten(res[rows, :])
        xh2[rows, :] = xh.astype(BF)
        r2[rows, :] = r
        nrm[rows, :] = (xh * g + b).astype(BF)
    todo.finish({"u"})
    for ch in range(4):
        a, d = gelu_parts(nn(nrm[...], wide(WU, ch)))
        for l in range(6):
            at = pl.ds(R * (6 * ch + l), R)
            act[at, :] = a[:, 128 * l : 128 * l + 128].astype(BF)
            gel[at, :] = d[:, 128 * l : 128 * l + 128].astype(BF)
        if ch == 0:
            tick("p", "d")
    todo.finish({"d"})
    for y in range(4):
        res[...] += nn(flat(act, y), tall(WD, y))

    g, b = gain(2)
    for i in range(4):
        x = res[IMG * i : IMG * i + IMG, :]
        m = jnp.mean(x, axis=-1, keepdims=True)
        xc = x - m
        r = lax.rsqrt(jnp.mean(xc * xc, axis=-1, keepdims=True) + 1e-05)
        e = r * jnp.sum(xc * (g * query()), axis=-1, keepdims=True)
        lg = (e + jnp.sum(b * query(), axis=-1, keepdims=True)) / ROOT
        lg = jnp.where(mcol[0:IMG, i : i + 1] > 0, lg, -1e30)
        ex = jnp.exp(lg - jnp.max(lg, axis=0, keepdims=True))
        sh = ex / jnp.sum(ex, axis=0, keepdims=True)
        row = jnp.sum((sh * r) * xc, axis=0, keepdims=True)
        s1[i : i + 1, :] = row
        pool[i : i + 1, :] = row * g + b * jnp.sum(sh, axis=0, keepdims=True)
        for n, c in enumerate((m, r, e, sh)):
            cols[i, :, n : n + 1] = c
    todo.finish()
    link.drain()

    def proj_cols(x, lo):
        at = [
            WP.load(core, lo, 32, x=x, y=y, z=z)
            for y in range(4) for core in range(2) for z in range(4)
        ]
        return jnp.concatenate(at, axis=0)

    pooled = pool[...].astype(BF)
    padded = jnp.concatenate(
        [nn(pooled[:, 384 * n : 384 * n + 384], e3[...]).astype(BF) for n in range(2)], axis=1
    )
    embedded = jnp.concatenate([nn(padded, proj_cols(x, 0)) for x in range(4)], axis=1)
    ri = lax.rsqrt(jnp.sum(embedded * embedded, axis=-1, keepdims=True) + 1e-06)
    unit = (embedded * ri).astype(BF)
    big = jnp.exp(jnp.full((1, 1), scale[0], F32))
    dots = nt(unit[:, 0:128], proj_cols(0, 32))
    for x in range(1, 4):
        dots = dots + nt(unit[:, 128 * x : 128 * x + 128], proj_cols(x, 32))
    logits = big * dots
    row = lax.broadcasted_iota(jnp.int32, (8, 1024), 0)
    col = lax.broadcasted_iota(jnp.int32, (8, 1024), 1)
    valid = (row < 4) & ((col & 7) < 4)
    target = jnp.zeros((8, 1024), F32)
    first = 4 * ((me.y * 2 + me.core) * 16 + me.z * 4 + me.x)
    for i in range(4):
        t = pairing[first + i]
        target = jnp.where((row == i) & (col == 8 * (t >> 2) + (t & 3)), 1.0, target)
    e = jnp.where(valid, jnp.exp(logits), 0.0)
    row_sum = jnp.where(row[:, 0:1] < 4, jnp.sum(e, axis=-1, keepdims=True), 1.0)
    col_sum = jnp.sum(e, axis=0, keepdims=True)
    for j in range(8):
        cs[j : j + 1, :] = col_sum[:, 128 * j : 128 * j + 128]
    rows_lse = jnp.sum(jnp.log(row_sum), axis=0, keepdims=True)
    matched = jnp.sum(jnp.sum(logits * target, axis=-1, keepdims=True), axis=0, keepdims=True)
    send_tile = cs[...]
    send_tile = jnp.where((subs == 0) & (lanes == 4), rows_lse, send_tile)
    send_tile = jnp.where((subs == 0) & (lanes == 5), matched, send_tile)
    cs[...] = send_tile
    got = link.group(crx.at[pl.ds(0, 15)])
    for n in range(1, 16):
        t, peer = me.v_peer(n)
        got.copy(cs, crx.at[me.v], peer)
    crx[me.v] = send_tile
    got.wait_recv()
    total = crx[0]
    for n in range(1, 16):
        total = total + crx[n]
    cst[...] = total
    got = link.group(crx2.at[pl.ds(0, 7)])
    for n in range(1, 8):
        t, peer = me.s_peer(n)
        got.copy(cst, crx2.at[s], peer)
    crx2[s] = total
    got.wait_recv()
    total = crx2[0]
    for n in range(1, 8):
        total = total + crx2[n]
    cs_all = jnp.concatenate([total[j : j + 1, :] for j in range(8)], axis=1)
    ok = (lanes & 7) < 4
    cols_lse = jnp.sum(jnp.where(ok, jnp.log(jnp.where(ok, total, 1.0)), 0.0))
    loss = (total[0:1, 4:5] + cols_lse - 2.0 * total[0:1, 5:6]) / 1024.0
    ok = (col[0:1, :] & 7) < 4
    gl = e / row_sum + e / jnp.where(ok, cs_all, 1.0) - 2.0 * target
    gl = jnp.where(valid, gl, 0.0) * (1.0 / 1024.0)
    g_scale = jnp.sum(gl * logits)
    parts = split(gl, 2)
    gui = []
    for x in range(4):
        rhs = proj_cols(x, 32)
        gui.append(nn(parts[0], rhs) + nn(parts[1], rhs))
    gui = big * jnp.concatenate(gui, axis=1)
    ge = ri * gui - ri * ri * ri * embedded * jnp.sum(embedded * gui, axis=-1, keepdims=True)
    ge = ge.astype(BF)
    gp_pad = jnp.concatenate(
        [
            sum(nt(ge[:, 128 * x : 128 * x + 128], proj_cols(x, 0)) for x in range(4))
        ], axis=1
    )
    gp = []
    for n in range(2):
        gp.append(sum(nt(p, e3[...]) for p in split(gp_pad[:, 512 * n : 512 * n + 512], 3)))
    emb[...] = jnp.concatenate(gp, axis=1)
    both = jnp.concatenate([parts[0], parts[1]], axis=0)
    ub = jnp.concatenate([unit, unit], axis=0)
    for x in range(4):
        gproj = tn(padded, ge[:, 128 * x : 128 * x + 128]).astype(BF)
        gtext = (big * tn(both, ub[:, 128 * x : 128 * x + 128])).astype(BF)
        n = 0
        for y in range(4):
            for core in range(2):
                for z in range(4):
                    WP.store(gproj[32 * n : 32 * n + 32, :], core, 0, x=x, y=y, z=z)
                    WP.store(gtext[32 * n : 32 * n + 32, :], core, 32, x=x, y=y, z=z)
                    n += 1

    def keep(n, c):
        def finish(total):
            tot[n, :, 128 * c : 128 * c + 128] = total

        return finish

    def keep_p(total):
        ptot[...] = total

    def rx_part(ref, c, n):
        return ref.at[pl.ds(n * c, n)]

    todo.add("p", scatter_steps(me, link, WP, rxpc, rxp, keep_p, False))
    tick("p", "p")

    def own_rows(n):
        for j in range(8):
            ust[n - 1, j] = tot[n, 6 * j : 6 * j + 6, :]
        group = link.group(orx.at[n - 1, pl.ds(0, 7)])
        for m in range(1, 8):
            t, peer = me.s_peer(m)
            group.copy(ust.at[n - 1, t], orx.at[n - 1, s], peer)
        orx[n - 1, s] = ust[n - 1, s]
        return group

    def own_down():
        group = link.group(tot.at[3, pl.ds(0, 24)])
        group.copy(
            tot.at[0, ds(24 * (1 - odd), 24, 8)],
            tot.at[3, ds(24 * odd, 24, 8)],
            me.dev(x=me.x + 1 - 2 * odd),
        )
        tot[3, ds(24 * odd, 24, 8), :] = tot[0, ds(24 * odd, 24, 8), :]
        return group

    def own_proj():
        for j in range(4):
            pst[j, 0:8] = ptot[8 * j : 8 * j + 8, :]
            pst[j, 8:16] = ptot[32 + 8 * j : 40 + 8 * j, :]
        group = link.group(prx2.at[pl.ds(0, 3)])
        for n in range(1, 4):
            t = (me.x + n) % 4
            group.copy(pst.at[t], prx2.at[me.x], me.dev(x=t))
        prx2[me.x] = pst[me.x]
        return group

    g, b = gain(2)
    side_q = query() / ROOT
    for i in range(4):
        rows = pl.ds(IMG * i, IMG)
        gpi = emb[i : i + 1, :]
        m, r, e, sh = (cols[i, :, n : n + 1] for n in range(4))
        one, two = gpi * g, side_q * g
        xc = res[rows, :] - m
        w = r * jnp.sum(xc * one, axis=-1, keepdims=True)
        c = w + jnp.sum(b * gpi, axis=-1, keepdims=True)
        dl = sh * (c - jnp.sum(sh * c, axis=0, keepdims=True))
        pull = r * r * (sh * w + dl * (e / ROOT)) * (1.0 / D)
        one_c = one - jnp.mean(one, axis=-1, keepdims=True)
        two_c = two - jnp.mean(two, axis=-1, keepdims=True)
        out = (r * sh) * one_c + (r * dl) * two_c - pull * xc
        res[rows, :] = out
        gb[rows, :] = out.astype(BF)
        row = jnp.sum((r * dl) * xc, axis=0, keepdims=True)
        sum_dl = jnp.sum(dl, axis=0, keepdims=True)
        gvec[4, 0:1, :] += gpi * s1[i : i + 1, :] + side_q * row
        gvec[5, 0:1, :] += gpi * jnp.sum(sh, axis=0, keepdims=True) + side_q * sum_dl
        gvec[6, 0:1, :] += (row * g + b * sum_dl) / ROOT
    for y in range(4):
        ga = nt(gb[...], tall(WD, y))
        for l in range(6):
            at = pl.ds(R * (6 * y + l), R)
            gel[at, :] = (ga[:, 128 * l : 128 * l + 128] * gel[at, :].astype(F32)).astype(BF)
        tall_store(WD, y, tn(flat(act, y), gb[...]).astype(BF))
        tick(*(("p",), (), ("p", "p"), ())[y])
    for c in range(3):
        todo.add("d", scatter_steps(me, link, WD[c], rx_part(rxc, c, 3072), rx_part(rxd, c, 3024), keep(0, c), False, give=credit.at[c]))
    tick("d", "d")
    for ch in range(4):
        gu = flat(gel, ch)
        part = nt(gu, wide(WU, ch))
        if ch == 0:
            acc[...] = part
        else:
            acc[...] += part
        wide_store(WU, ch, tn(nrm[...], gu).astype(BF))
        tick(*(("d", "p"), ("p",), ("d", "d"), ("p",))[ch])
        if ch == 3:
            got_proj = own_proj()
    for c in range(3):
        todo.add("u", scatter_steps(me, link, WU[c], rx_part(rxc, c, 3072), rx_part(rxu, c, 3024), keep(1, c), False, give=credit.at[3 + c], need=credit.at[c]))
    tick("u", "u")

    def fold_in(n, gg, gs):
        gvec[n] += gg
        gvec[n + 1] += gs

    g, _ = gain(1)
    for i in range(4):
        rows = pl.ds(IMG * i, IMG)
        y, xh = acc[rows, :], xh2[rows, :].astype(F32)
        out = res[rows, :] + whiten_back(y * g, xh, r2[rows, :])
        res[rows, :] = out
        gb[rows, :] = out.astype(BF)
        fold_in(2, fold(y * xh), fold(y))
    wide_store(GA, 3, tn(att[0:R, :], gb[...]).astype(BF))
    att[0:R, :] = nt(gb[...], wide(WA, 3)).astype(BF)
    norm_one()
    tick("u")
    low = lax.broadcasted_iota(jnp.int32, (256, 128), 0) < IMG
    side = lax.broadcasted_iota(jnp.int32, (256, 128), 1) < 64
    own = [jnp.where(low & side, 1.0, 0.0).astype(BF), jnp.where(low & ~side, 1.0, 0.0).astype(BF)]

    def attend_back(img):
        rows, wide_rows = pl.ds(IMG * img, IMG), pl.ds(IMG * img, 256)

        def pair(pr):
            c = ds(128 * pr, 128)
            q2, k2, v2, do = q[wide_rows, c], k[rows, c], v[rows, c], att[wide_rows, c]
            kt = k2.T
            dqt = []
            dk = jnp.zeros((IMG, 128), F32)
            dv = jnp.zeros((IMG, 128), F32)
            for h in range(2):
                doh, qh = do * own[h], q2 * heads[h]
                p = pb[img % 2, 2 * pr + h]
                dv = dv + nn(p, doh)
                pf = p.astype(F32)
                dp = nt(v2, doh)
                t = pf * dp
                dst = (t - pf * jnp.sum(t, axis=0, keepdims=True)).astype(BF)
                dk = dk + nn(dst, qh)
                dqt.append(nn(kt[64 * h : 64 * h + 64, :], dst))
            dq = (jnp.concatenate(dqt, axis=0) * 0.125).astype(BF).T
            q[rows, c] = dq[0:IMG, :]
            k[rows, c] = dk.astype(BF)
            v[rows, c] = dv.astype(BF)

        for pr in range(6):
            pair(pr)

    loads = {}
    for img in (2, 3, 0, 1):
        if img in loads:
            loads[img].wait()
        attend_back(img)
        if img >= 2:
            c = pltpu.make_async_copy(spill.at[img - 2], pb.at[img - 2], lsem.at[img])
            c.start()
            loads[img - 2] = c
        tick(*(("d",), ("u",), ("d",), ("u", "u"))[img])
    for ch, src in enumerate((q, k, v)):
        wide_store(GA, ch, tn(nrm[...], src[0:R, :]).astype(BF))
        if ch == 0:
            tick("d")
            got_down = own_down()
    for c in range(3):
        todo.add("a", scatter_steps(me, link, GA[c], rx_part(rxc, c, 3072), rx_part(rxa, c, 3024), keep(2, c), True, need=credit.at[3 + c]))
    tick("a", "a", "u")
    for ch, src in enumerate((q, k, v)):
        part = nt(src[0:R, :], wide(WA, ch))
        if ch == 0:
            acc[...] = part
        else:
            acc[...] += part
        if ch == 1:
            tick("a")
        if ch == 2:
            tick("u")
            got_up = own_rows(1)
    g, _ = gain(0)
    outs = []
    for i in range(4):
        rows = pl.ds(IMG * i, IMG)
        xh, r = whiten(tok[rows, :].astype(F32))
        y = acc[rows, :]
        out = res[rows, :] + whiten_back(y * g, xh, r)
        fold_in(0, fold(y * xh), fold(y))
        acc[196 * i : 196 * i + 196, :] = out[0:196, :]
        if i % 2 == 1:
            rows = pl.ds(392 * (i // 2), 392)
            outs.append(pltpu.make_async_copy(acc.at[rows], o_tok.at[rows], lsem.at[4 + i // 2]))
            outs[-1].start()
    tick("a")

    for n in range(7):
        vec[n : n + 1, :] = jnp.sum(gvec[n], axis=0, keepdims=True)
    vec[7:8, :] = jnp.zeros((1, D), F32)
    for n in range(16):
        t, off = 48 * n // 128, 48 * n % 128
        part = vec[:, 128 * t : 128 * t + 128]
        part = pltpu.roll(part, (128 - off) % 128, 1) if off else part
        if off > 80:
            more = pltpu.roll(vec[:, 128 * t + 128 : 128 * t + 256], 128 - off, 1)
            part = jnp.where(lanes < 128 - off, part, more)
        gst2[n] = jnp.where(subs == 7, g_scale, part)
    cv = link.group(grx.at[pl.ds(0, 15)])
    for n in range(1, 16):
        t, peer = me.v_peer(n)
        cv.copy(gst2.at[t], grx.at[me.v], peer)
    grx[me.v] = gst2[me.v]

    tick("a", "a")
    cv.wait_recv()
    total = grx[0]
    for n in range(1, 16):
        total = total + grx[n]
    vst[...] = total
    got_vec = link.group(grx2.at[pl.ds(0, 7)])
    for n in range(1, 8):
        t, peer = me.s_peer(n)
        got_vec.copy(vst, grx2.at[s], peer)
    grx2[s] = total
    todo.finish({"a"})
    last = own_rows(2)
    got_vec.wait_recv()
    total = grx2[0]
    for n in range(1, 8):
        total = total + grx2[n]
    total = pltpu.roll(total, (128 - 6 * s) % 128, 1)
    scal[...] = jnp.where((subs == 7) & (lanes == 1), loss, total)
    to_smem = pltpu.make_async_copy(scal, scal_s, lsem.at[6])
    to_smem.start()
    got_up.wait_recv()
    got_down.wait_recv()
    for j in range(8):
        o_up[:, 384 * j : 384 * j + 384] = orx[0, j]
    for j in range(2):
        o_down[:, 384 * j : 384 * j + 384] = tot[3, 24 * j : 24 * j + 24, :]
    got_proj.wait_recv()
    for j in range(4):
        o_proj[:, 128 * j : 128 * j + 128] = prx2[j, 0:6]
    gt = jnp.concatenate([prx2[j, 8:12] for j in range(4)], axis=1)
    txt = text[...]
    r = lax.rsqrt(jnp.sum(txt * txt, axis=-1, keepdims=True) + 1e-06)
    o_text[...] = r * gt - r * r * r * txt * jnp.sum(txt * gt, axis=-1, keepdims=True)
    to_smem.wait()
    for n, ref in enumerate((o0, o1, o2, o3, o4, o5, o6)):
        for e in range(6):
            ref[e] = scal_s[n, e]
    o_scale[0] = scal_s[7, 0]
    o_loss[0] = scal_s[7, 1]
    last.wait_recv()
    for j in range(8):
        if j < 6:
            o_qkv[:, 384 * j : 384 * j + 384] = orx[1, j]
        else:
            o_out[:, 384 * (j - 6) : 384 * (j - 6) + 384] = orx[1, j]
    for c in outs:
        c.wait()
    link.drain()


def hand_over(*refs):
    src, dst, buf, sem = refs[:16], refs[16:32], refs[32], refs[33]
    rows = [pl.ds(200 * n, 200 if n < 3 else 184) for n in range(4)]
    there = [pltpu.make_async_copy(src[1].at[r], buf.at[r], sem.at[n]) for n, r in enumerate(rows)]
    back = [pltpu.make_async_copy(buf.at[r], dst[1].at[r], sem.at[4 + n]) for n, r in enumerate(rows)]
    for c in there:
        c.start()
    for n, (a, b) in enumerate(zip(src, dst)):
        if n in (0, 15):
            b[0] = a[0]
        elif n >= 8:
            for e in range(6):
                b[e] = a[e]
        elif n != 1:
            b[...] = a[...]
    for a, b in zip(there, back):
        a.wait()
        b.start()
    for c in back:
        c.wait()


def shards(tokens, keep_mask, pairing, text_vectors, logit_scale, w_qkv, w_out, w_up, w_down, w_proj, *vectors):
    vm = pl.BlockSpec(memory_space=pltpu.VMEM)
    sm = pl.BlockSpec(memory_space=pltpu.SMEM)
    hbm = pl.BlockSpec(memory_space=pl.ANY)
    S = jax.ShapeDtypeStruct
    V = pltpu.VMEM
    outs = pl.pallas_call(
        kernel,
        out_shape=[
            S((1,), F32), S((784, D), F32), S((4, 512), F32), S((6, 2304), F32), S((6, 768), F32),
            S((6, 3072), F32), S((24, 768), F32), S((6, 512), F32), *[S((6,), F32)] * 7, S((1,), F32),
            S((2, 12, IMG, 256), BF),
        ],
        in_specs=[sm] * 9 + [hbm] + [vm] * 7,
        out_specs=[sm, hbm, vm, vm, vm, vm, vm, vm, *[sm] * 8, hbm],
        scratch_shapes=[
            V((18432, 128), BF), V((18432, 128), BF), V((18432, 128), BF), V((8192, 128), BF), V((R, D), BF),
            V((R + 48, D), BF), V((R, D), BF), V((R, D), BF), V((2, 12, IMG, 256), BF),
            V((R, D), BF), V((R, D), BF), V((R + 48, D), BF), V((R, D), BF),
            V((24 * R, 128), BF), V((24 * R, 128), BF), V((R, D), F32), V((R, D), F32), V((R, 1), F32),
            V((3 * 3072, 128), BF), V((3 * 3024, 128), BF), V((3 * 3024, 128), BF), V((3 * 3024, 128), BF),
            V((4096, 128), BF), V((4032, 128), BF),
            V((6, 3072), F32), V((8, 6, 384), F32), V((8, 6, 384), F32), V((2, 24, 384), F32),
            V((16, 512), F32), V((4, 16, 128), F32), V((8, 8, 128), F32), V((8, 128), F32),
            V((48, 384), F32), V((64, 128), F32), V((8, D), F32), V((7, 8, D), F32),
            V((8, 256), F32), V((256, 8), F32), V((4, IMG, 8), F32), V((4, IMG, 128), F32),
            V((8, D), F32), V((8, D), F32), V((384, 512), BF), V((8, D), F32),
            V((8, 128), F32), pltpu.SMEM((8, 128), F32),
            V((8, 128), F32), V((16, 8, 128), F32), V((8, 128), F32), V((8, 8, 128), F32),
            V((4, 48, 384), F32), V((64, 128), F32), V((2, 8, 6, 384), F32), V((2, 8, 6, 384), F32),
            V((4, 16, 128), F32), V((4, 16, 128), F32), V((16, 8, 128), F32), V((16, 8, 128), F32),
            V((16, 8, 128), F32), V((8, 8, 128), F32),
            pltpu.SemaphoreType.DMA((N_SEM,)), pltpu.SemaphoreType.DMA((N_SEM,)), pltpu.SemaphoreType.DMA((8,)),
            pltpu.SemaphoreType.REGULAR((6,)),
        ],
        compiler_params=pltpu.CompilerParams(
            collective_id=0, has_side_effects=True, vmem_limit_bytes=(64 << 20) - (256 << 10)
        ),
        cost_estimate=pl.CostEstimate(flops=40_000_000_000, bytes_accessed=20_000_000, transcendentals=0),
    )(pairing, logit_scale, *vectors, tokens, keep_mask, text_vectors, w_qkv, w_out, w_up, w_down, w_proj)
    outs = outs[:16]
    return pl.pallas_call(
        hand_over,
        out_shape=[S(o.shape, o.dtype) for o in outs],
        in_specs=[sm, hbm] + [vm] * 6 + [sm] * 8,
        out_specs=[sm, hbm] + [vm] * 6 + [sm] * 8,
        scratch_shapes=[V((784, D), F32), pltpu.SemaphoreType.DMA((8,))],
    )(*outs)


def solution(mesh):
    rows, vector, whole = P(("dp", "fsdp"), None), P(("dp", "fsdp")), P()
    in_specs = (rows, rows, whole, rows, whole, *[rows] * 5, *[vector] * 7)
    out_specs = (whole, rows, rows, *[rows] * 5, *[vector] * 7, whole)
    return jax.shard_map(shards, mesh=mesh, in_specs=in_specs, out_specs=out_specs, check_vma=False)
```

```python
from functools import partial
import math

import jax
import jax.numpy as jnp
from jax import lax
from jax.experimental import pallas as pl
from jax.experimental.pallas import tpu as pltpu
from jax.sharding import PartitionSpec as P

MESH = pl.DeviceIdType.MESH
BF = jnp.bfloat16
F32 = jnp.float32
IMG = 208
R = 4 * IMG
D = 768
ROOT = math.sqrt(768.0)


class Place:
    def __init__(self):
        dp = lax.axis_index("dp")
        fs = lax.axis_index("fsdp")
        self.y, self.core = dp // 2, dp % 2
        self.z, self.x = fs // 4, fs % 4
        self.s = (self.z % 2) * 4 + self.x
        self.v = dp * 2 + self.z // 2

    def dev(self, **moved):
        at = dict(x=self.x, y=self.y, z=self.z, core=self.core)
        at.update(moved)
        return (at["y"] * 2 + at["core"], at["z"] * 4 + at["x"])

    def hop(self, dim, step):
        return self.dev(**{dim: (getattr(self, dim) + step + 4) % 4})

    def sibling(self):
        return self.dev(core=1 - self.core)

    def s_peer(self, k):
        t = (self.s + k) % 8
        return t, self.dev(z=(self.z // 2) * 2 + t // 4, x=t % 4)

    def v_peer(self, k):
        t = (self.v + k) % 16
        return t, (t // 2, ((t % 2) * 2 + self.z % 2) * 4 + self.x)


class Group:
    def __init__(self, link, total):
        self.link, self.total = link, total
        self.k = link.n
        link.n += 1
        link.open.append(self)
        self.sems = dict(send_sem=link.send.at[self.k], recv_sem=link.recv.at[self.k])

    def copy(self, src, dst, dev):
        c = pltpu.make_async_remote_copy(
            src_ref=src, dst_ref=dst, device_id=dev, device_id_type=MESH, **self.sems
        )
        c.start()

    def whole(self):
        return pltpu.make_async_remote_copy(
            src_ref=self.total,
            dst_ref=self.total,
            device_id=self.link.any_device,
            device_id_type=MESH,
            **self.sems,
        )

    def wait_recv(self):
        self.whole().wait_recv()


class Link:
    def __init__(self, send, recv, any_device):
        self.send, self.recv, self.n = send, recv, 0
        self.any_device = any_device
        self.open = []

    def group(self, total):
        return Group(self, total)

    def drain(self):
        for g in self.open:
            g.whole().wait_send()
        self.open = []


ORDERS = (("x", "y", "z"), ("y", "z", "x"), ("z", "x", "y"))


def enter(me):
    sem = pltpu.get_barrier_semaphore()
    peers = []
    for n in range(1, 64):
        dx, dy, dz = n % 4, n // 4 % 4, n // 16
        if dx * dy * dz == 0:
            peers.append(me.dev(x=(me.x + dx) % 4, y=(me.y + dy) % 4, z=(me.z + dz) % 4))
    for n in range(8):
        peers.append(me.dev(y=(me.y + n % 4) % 4, z=(me.z + n // 4 * 2) % 4, core=1 - me.core))
    for p in peers:
        pl.semaphore_signal(sem, inc=1, device_id=p, device_id_type=MESH)
    pl.semaphore_wait(sem, len(peers))


def ds(start, size, unit=None):
    if isinstance(start, int):
        return pl.ds(start, size)
    return pl.ds(pl.multiple_of(start, unit or size), size)


class Pieces:
    def __init__(self, ref, base, order, rows):
        self.ref, self.base, self.order, self.rows = ref, base, order, rows

    def start(self, core, **at):
        d1, d2, d3 = (at[d] for d in self.order)
        return self.base + (((core * 4 + d3) * 4 + d2) * 4 + d1) * self.rows

    def piece(self, core, **at):
        return self.ref.at[ds(self.start(core, **at), self.rows, 16)]

    def load(self, core, lo=0, n=None, **at):
        return self.ref[pl.ds(self.start(core, **at) + lo, n or self.rows), :]

    def store(self, value, core, lo=0, **at):
        self.ref[pl.ds(self.start(core, **at) + lo, value.shape[0]), :] = value

    def block(self, core, stage, me, b):
        at = [getattr(me, d) for d in self.order]
        at[stage] = b
        for k in range(stage):
            at[k] = 0
        return self.start(core, **dict(zip(self.order, at))), self.rows * 4**stage


def rows_of(ref, block):
    return ref.at[ds(block[0], block[1], 16)]


def plane_peer(me, order, n):
    a, b = order[:2]
    i, j = (getattr(me, a) + n % 4) % 4, (getattr(me, b) + n // 4) % 4
    return {a: i, b: j}, me.dev(**{a: i, b: j})


def cut(block, which):
    start, size = block
    return (start + which * (size // 2), size // 2)


def gather_steps(me, link, buf, at_once):
    ref, d, rows = buf.ref, buf.order[2], buf.rows
    i, size = getattr(me, d), 16 * buf.rows
    lo, hi, far = (i + 3) % 4, (i + 1) % 4, (i + 2) % 4
    right, left = me.hop(d, 1), me.hop(d, -1)

    def bytes_of(pieces):
        return ref.at[pl.ds(buf.base, pieces * rows)]

    def send(group, block, dev):
        group.copy(rows_of(ref, block), rows_of(ref, block), dev)

    def block(b):
        return buf.block(me.core, 2, me, b)

    if at_once:
        own = buf.block(me.core, 0, me, getattr(me, buf.order[0]))
        others = link.group(bytes_of(15))
        for n in range(1, 16):
            send(others, own, plane_peer(me, buf.order, n)[1])
        yield
        others.wait_recv()
    for stage in () if at_once else (0, 1):
        axis = buf.order[stage]
        own = buf.block(me.core, stage, me, getattr(me, axis))
        others = link.group(bytes_of(3 * 4**stage))
        for n in (2, 1, 3):
            send(others, own, me.hop(axis, n))
        yield
        others.wait_recv()
    from_lo, from_hi = link.group(bytes_of(16)), link.group(bytes_of(16))
    send(from_lo, block(i), right)
    send(from_hi, block(i), left)
    sib = link.group(bytes_of(64))
    send(sib, block(i), me.sibling())
    yield
    from_lo.wait_recv()
    rest = link.group(bytes_of(16))
    send(rest, cut(block(lo), 0), right)
    from_hi.wait_recv()
    send(rest, cut(block(hi), 1), left)
    send(sib, block(lo), me.sibling())
    send(sib, block(hi), me.sibling())
    yield
    rest.wait_recv()
    send(sib, block(far), me.sibling())
    yield
    sib.wait_recv()


def add_rows(dst_ref, dst, *srcs):
    size = dst[1]
    rows = ds(dst[0], size, 16)
    if len(srcs) == 1:
        ref, start = srcs[0]
        dst_ref[rows, :] = dst_ref[rows, :] + ref[ds(start, size, 16), :]
        return
    total = dst_ref[rows, :].astype(F32)
    for ref, start in srcs:
        total = total + ref[ds(start, size, 16), :].astype(F32)
    dst_ref[rows, :] = total.astype(BF)


def scatter_steps(me, link, buf, rx_core, rx, finish, at_once, give=None, need=None):
    ref, rows, d = buf.ref, buf.rows, buf.order[2]
    i, size = getattr(me, d), 16 * buf.rows
    lo, hi, far = (i + 3) % 4, (i + 1) % 4, (i + 2) % 4
    right, left = me.hop(d, 1), me.hop(d, -1)

    def bytes_of(pieces):
        return ref.at[pl.ds(buf.base, pieces * rows)]

    def block(b, core=me.core):
        return buf.block(core, 2, me, b)

    def slot(n):
        return (n * size, size)

    if need is not None:
        pl.semaphore_wait(need, 1)
    def cross(group, b):
        group.copy(rows_of(ref, block(b, 1 - me.core)), rows_of(rx_core, (b * size, size)), me.sibling())

    first, rest = link.group(bytes_of(16)), link.group(bytes_of(48))
    cross(first, far)
    yield
    for b in (hi, lo, i):
        cross(rest, b)
    yield
    first.wait_recv()

    def settle(b):
        add_rows(ref, block(b), (rx_core, b * size))

    def send(group, src, dst, dev):
        group.copy(rows_of(ref, src), rows_of(rx, dst), dev)

    settle(far)
    merge = link.group(bytes_of(16))
    send(merge, cut(block(far), 0), cut(slot(0), 0), right)
    send(merge, cut(block(far), 1), cut(slot(0), 1), left)
    yield
    rest.wait_recv()
    settle(hi)
    ends = link.group(bytes_of(32))
    send(ends, cut(block(hi), 1), cut(slot(1), 1), right)
    settle(lo)
    send(ends, cut(block(lo), 0), cut(slot(2), 0), left)
    settle(i)
    if give is not None:
        pl.semaphore_signal(give, inc=1, device_id=me.sibling(), device_id_type=MESH)
    yield
    merge.wait_recv()
    add_rows(ref, cut(block(hi), 0), (rx, cut(slot(0), 0)[0]))
    send(ends, cut(block(hi), 0), cut(slot(1), 0), right)
    add_rows(ref, cut(block(lo), 1), (rx, cut(slot(0), 1)[0]))
    send(ends, cut(block(lo), 1), cut(slot(2), 1), left)
    yield
    ends.wait_recv()
    add_rows(ref, block(i), (rx, size), (rx, 2 * size))
    base = 3 * size
    if at_once:
        others = link.group(bytes_of(15))
        for n in range(1, 16):
            at, peer = plane_peer(me, buf.order, n)
            src = (buf.start(me.core, **{**at, d: i}), rows)
            send(others, src, (base + (n - 1) * rows, rows), peer)
        yield
        others.wait_recv()
        last = 15
    for stage in () if at_once else (1, 0):
        axis = buf.order[stage]
        j, part = getattr(me, axis), rows * 4**stage
        others = link.group(bytes_of(3 * 4**stage))
        for n in (2, 1, 3):
            src = buf.block(me.core, stage, me, (j + n) % 4)
            send(others, src, (base + (n - 1) * part, part), me.hop(axis, n))
        yield
        others.wait_recv()
        last = 3
        if stage == 1:
            add_rows(ref, buf.block(me.core, 1, me, j), *[(rx, base + n * part) for n in range(3)])
            base += 3 * part
    own = buf.block(me.core, 0, me, getattr(me, buf.order[0]))
    total = ref[ds(own[0], rows, 16), :].astype(F32)
    for n in range(last):
        total = total + rx[pl.ds(base + n * rows, rows), :].astype(F32)
    finish(total)


class Queue:
    def __init__(self):
        self.live = []

    def add(self, name, gen):
        self.live.append((name, gen))

    def step(self, names=None):
        keep = []
        for name, gen in self.live:
            if names is None or name in names:
                try:
                    next(gen)
                except StopIteration:
                    continue
            keep.append((name, gen))
        self.live = keep

    def finish(self, names=None):
        while any(names is None or n in names for n, _ in self.live):
            self.step(names)


def nn(a, b):
    return lax.dot_general(a, b, (((1,), (0,)), ((), ())), preferred_element_type=F32)


def nt(a, b):
    return lax.dot_general(a, b, (((1,), (1,)), ((), ())), preferred_element_type=F32)


def tn(a, b):
    return lax.dot_general(a, b, (((0,), (0,)), ((), ())), preferred_element_type=F32)


def whiten(x):
    centred = x - jnp.mean(x, axis=-1, keepdims=True)
    r = lax.rsqrt(jnp.mean(centred * centred, axis=-1, keepdims=True) + 1e-05)
    return centred * r, r


def whiten_back(y, xh, r):
    return r * (y - jnp.mean(y, axis=-1, keepdims=True) - xh * jnp.mean(y * xh, axis=-1, keepdims=True))


def fold(x):
    return jnp.sum(x.reshape(x.shape[0] // 8, 8, x.shape[1]), axis=0)


def split(x, parts):
    got = []
    for _ in range(parts):
        h = x.astype(BF)
        got.append(h)
        x = x - h.astype(F32)
    return got


def gelu_parts(u):
    a = jnp.abs(u)
    den = 1.0 + (0.3275911 * math.sqrt(0.5)) * a
    t = pltpu.reciprocal(den, approx=True)
    t = t * (2.0 - den * t)
    e = jnp.exp2((-0.5 * math.log2(math.e)) * (u * u))
    poly = t * (0.5 * 0.254829592 + t * (-0.5 * 0.284496736 + t * (0.5 * 1.421413741 + t * (-0.5 * 1.453152027 + t * (0.5 * 1.061405429)))))
    tail = poly * e
    phi = jnp.where(u < 0, tail, 1.0 - tail)
    return u * phi, phi + u * (e * (1.0 / math.sqrt(2.0 * math.pi)))


def blocks(n, body, unroll=1):
    lax.fori_loop(0, n, lambda k, c: (body(k), 0)[1], 0, unroll=unroll)


N_SEM = 128


def kernel(
    pairing, scale, v0, v1, v2, v3, v4, v5, v6,
    tokens, mask, text, w_qkv, w_out, w_up, w_down, w_proj,
    o_tok, o_text, o_qkv, o_out, o_up, o_down, o_proj, o_small, spill,
    wa, wu, wd, wp, tok, q, k, v, pb, xh2, nrm, att, gb, act, gel, res, acc, r2,
    rxc, rxd, rxu, rxa, rxpc, rxp,
    aloc, arx, urx, drx, ploc, prx, vrx, vst, p48, p64, vec, gvec,
    mrow, mcol, cols, bias, pool, s1, e3, emb, cs, crx, cst, crx2,
    tot, ptot, orx, ust, pst, prx2, gst, grx, gst2, grx2,
    send, recv, lsem, credit,
):
    me = Place()
    link = Link(send, recv, me.sibling())
    todo = Queue()
    s = me.s
    lanes = lax.broadcasted_iota(jnp.int32, (8, 128), 1)
    subs = lax.broadcasted_iota(jnp.int32, (8, 128), 0)

    WA = [Pieces(wa, 6144 * c, ORDERS[c], 48) for c in range(3)]
    WU = [Pieces(wu, 6144 * c, ORDERS[c], 48) for c in range(3)]
    WD = [Pieces(wd, 6144 * c, ORDERS[c], 48) for c in range(3)]
    WP = Pieces(wp, 0, ORDERS[0], 64)
    GA = [Pieces(act, 6144 * c, ORDERS[c], 48) for c in range(3)]

    raw = pltpu.make_async_copy(tokens, gb.at[pl.ds(0, 784)], lsem.at[7])
    raw.start()
    aloc[:, 0:2304] = w_qkv[...]
    aloc[:, 2304:3072] = w_out[...]
    mine = jnp.zeros((8, 128), F32)
    for n, ref in enumerate((v0, v1, v2, v3, v4, v5, v6)):
        for e in range(6):
            mine = jnp.where((subs == n) & (lanes == e), ref[e], mine)
    vst[...] = mine.astype(BF).astype(F32)
    ploc[...] = jnp.zeros_like(ploc)
    ploc[0:6, :] = w_proj[...]
    txt = text[...]
    ploc[8:12, :] = txt * lax.rsqrt(jnp.sum(txt * txt, axis=-1, keepdims=True) + 1e-06)
    enter(me)
    firsts = {}

    def meet(name, src, rx):
        firsts[name] = link.group(rx.at[pl.ds(0, 7)])
        for n in range(1, 8):
            t, peer = me.s_peer(n)
            part = src if name == "v" else src.at[:, ds(384 * t, 384, 128)]
            firsts[name].copy(part, rx.at[s], peer)

    here = dict(x=me.x, y=me.y, z=me.z)

    def launch(name, bufs, n):
        for c, b in enumerate(bufs):
            if n == 48:
                b.piece(me.core, **here)[...] = p48[:, 128 * c : 128 * c + 128].astype(BF)
            else:
                b.piece(me.core, **here)[...] = p64[...].astype(BF)
            todo.add(name, gather_steps(me, link, b, name == "a"))

    meet("a", aloc, arx)
    meet("v", vst, vrx)
    arx[s] = aloc[:, ds(384 * s, 384, 128)]
    urx[s] = w_up[:, ds(384 * s, 384, 128)]
    odd = me.x % 2
    drx[odd] = w_down[:, ds(384 * odd, 384, 128)]
    prx[me.x] = ploc[:, ds(128 * me.x, 128)]
    vrx[s] = vst[...]
    firsts["a"].wait_recv()
    for j in range(8):
        p48[6 * j : 6 * j + 6, :] = arx[j]
    launch("a", WA, 48)
    todo.step({"a"})
    meet("u", w_up, urx)
    cp = link.group(prx.at[pl.ds(0, 3)])
    for n in range(1, 4):
        t = (me.x + n) % 4
        cp.copy(ploc.at[:, ds(128 * t, 128)], prx.at[me.x], me.dev(x=t))
    cd = link.group(drx.at[0])
    cd.copy(w_down.at[:, ds(384 * (1 - odd), 384, 128)], drx.at[odd], me.dev(x=me.x + 1 - 2 * odd))
    firsts["v"].wait_recv()
    total = vrx[0]
    for j in range(1, 8):
        total = total + pltpu.roll(vrx[j], 6 * j, 1)
    gst[me.v] = total
    cv = link.group(gst.at[pl.ds(0, 15)])
    for n in range(1, 16):
        t, peer = me.v_peer(n)
        cv.copy(gst.at[me.v], gst.at[me.v], peer)

    mrow[...] = jnp.zeros_like(mrow)
    mrow[0:4, 0:196] = mask[...].astype(F32)
    mcol[...] = mrow[...].T
    for i in range(4):
        col = jnp.where(mcol[0:IMG, i : i + 1] > 0, 0.0, -1e30)
        bias[i] = jnp.broadcast_to(col, (IMG, 128))
    for ref in (q, att):
        ref[R : R + 48, :] = jnp.zeros((48, D), BF)
    pool[...] = jnp.zeros_like(pool)
    gvec[...] = jnp.zeros_like(gvec)
    row = lax.broadcasted_iota(jnp.int32, (384, 512), 0)
    col = lax.broadcasted_iota(jnp.int32, (384, 512), 1)
    e3[...] = jnp.where(((col >> 3) * 6 + (col & 7) == row) & ((col & 7) < 6), 1.0, 0.0).astype(BF)
    todo.step({"a"})
    firsts["u"].wait_recv()
    for j in range(8):
        p48[6 * j : 6 * j + 6, :] = urx[j]
    launch("u", WU, 48)
    cp.wait_recv()
    for j in range(4):
        p64[8 * j : 8 * j + 8, :] = prx[j, 0:8]
        p64[32 + 8 * j : 40 + 8 * j, :] = prx[j, 8:16]
    launch("p", [WP], 64)
    cd.wait_recv()
    for j in range(2):
        p48[24 * j : 24 * j + 24, :] = drx[j]
    launch("d", WD, 48)
    todo.step({"u"})
    todo.step({"p"})
    todo.step({"d"})
    raw.wait()
    acc[0:784, :] = gb[0:784, :].astype(F32)
    acc[784:R, :] = jnp.zeros((R - 784, D), F32)
    for i in range(4):
        tok[IMG * i : IMG * i + IMG, :] = acc[196 * i : 196 * i + IMG, :].astype(BF)
    cv.wait_recv()
    vec[...] = jnp.zeros_like(vec)
    for n in range(16):
        t, off = 48 * n // 128, 48 * n % 128
        part = pltpu.roll(gst[n], off, 1) if off else gst[n]
        if off <= 80:
            vec[:, 128 * t : 128 * t + 128] += part
        else:
            vec[:, 128 * t : 128 * t + 128] += jnp.where(lanes >= off, part, 0.0)
            vec[:, 128 * t + 128 : 128 * t + 256] += jnp.where(lanes < off, part, 0.0)

    def gain(n):
        return vec[2 * n : 2 * n + 1, :], vec[2 * n + 1 : 2 * n + 2, :]

    def query():
        return vec[6:7, :]

    def tick(*names):
        for name in names:
            todo.step({name})

    def norm_one():
        g, b = gain(0)
        for i in range(4):
            rows = pl.ds(IMG * i, IMG)
            xh, _ = whiten(tok[rows, :].astype(F32))
            nrm[rows, :] = (xh * g + b).astype(BF)

    norm_one()

    def wide(bufs, ch):
        zlo, xp = ch // 2, ch % 2
        cols = []
        for l in range(6):
            at = [
                bufs[l % 3].load(core, x=2 * xp + l // 3, y=y, z=2 * h + zlo)
                for y in range(4) for core in range(2) for h in range(2)
            ]
            cols.append(jnp.concatenate(at, axis=0))
        return jnp.concatenate(cols, axis=1)

    def wide_store(bufs, ch, value):
        zlo, xp = ch // 2, ch % 2
        for l in range(6):
            n = 0
            for y in range(4):
                for core in range(2):
                    for h in range(2):
                        part = value[48 * n : 48 * n + 48, 128 * l : 128 * l + 128]
                        bufs[l % 3].store(part, core, x=2 * xp + l // 3, y=y, z=2 * h + zlo)
                        n += 1

    def tall(bufs, y):
        cols = []
        for l in range(6):
            at = [
                bufs[l % 3].load(core, x=2 * xh + l // 3, y=y, z=z)
                for core in range(2) for z in range(4) for xh in range(2)
            ]
            cols.append(jnp.concatenate(at, axis=0))
        return jnp.concatenate(cols, axis=1)

    def tall_store(bufs, y, value):
        for l in range(6):
            n = 0
            for core in range(2):
                for z in range(4):
                    for xh in range(2):
                        part = value[48 * n : 48 * n + 48, 128 * l : 128 * l + 128]
                        bufs[l % 3].store(part, core, x=2 * xh + l // 3, y=y, z=z)
                        n += 1

    def flat(ref, ch, rows=None):
        return jnp.concatenate([ref[R * (6 * ch + l) : R * (6 * ch + l) + R, :] for l in range(6)], axis=1)

    tick("a", "u", "p", "d", "a", "u")
    todo.finish({"a"})
    for ch, dst in enumerate((q, k, v)):
        out = nn(nrm[...], wide(WA, ch))
        if ch == 0:
            out = out * 0.125
        dst[0:R, :] = out.astype(BF)
    lane = lax.broadcasted_iota(jnp.int32, (1, 128), 1)
    heads = [jnp.where(lane < 64, 1.0, 0.0).astype(BF), jnp.where(lane < 64, 0.0, 1.0).astype(BF)]

    def attend(img):
        rows, wide_rows = pl.ds(IMG * img, IMG), pl.ds(IMG * img, 256)

        def pair(pr):
            c = ds(128 * pr, 128)
            q2, k2, v2 = q[wide_rows, c], k[rows, c], v[rows, c]
            vt = v2.T
            b2 = jnp.concatenate([bias[img], bias[img]], axis=1)
            got = []
            for h in range(2):
                st = nt(k2, q2 * heads[h]) + b2
                e = jnp.exp(st - jnp.max(st, axis=0, keepdims=True))
                p = (e * (1.0 / jnp.sum(e, axis=0, keepdims=True))).astype(BF)
                pb[img % 2, 2 * pr + h] = p
                got.append(nn(vt[64 * h : 64 * h + 64, :], p).astype(BF))
            o = jnp.concatenate(got, axis=0).T
            att[rows, c] = o[0:IMG, :]

        for pr in range(6):
            pair(pr)

    saves = []
    for img in range(4):
        if img >= 2:
            saves[img - 2].wait()
        attend(img)
        if img < 2:
            c = pltpu.make_async_copy(pb.at[img], spill.at[img], lsem.at[img])
            c.start()
            saves.append(c)
        if img % 2 == 0:
            tick("u", "p", "d")

    res[...] = tok[...].astype(F32) + nn(att[0:R, :], wide(WA, 3))

    g, b = gain(1)
    for i in range(4):
        rows = pl.ds(IMG * i, IMG)
        xh, r = whiten(res[rows, :])
        xh2[rows, :] = xh.astype(BF)
        r2[rows, :] = r
        nrm[rows, :] = (xh * g + b).astype(BF)
    todo.finish({"u"})
    for ch in range(4):
        a, d = gelu_parts(nn(nrm[...], wide(WU, ch)))
        for l in range(6):
            at = pl.ds(R * (6 * ch + l), R)
            act[at, :] = a[:, 128 * l : 128 * l + 128].astype(BF)
            gel[at, :] = d[:, 128 * l : 128 * l + 128].astype(BF)
        if ch == 0:
            tick("p", "d")
    todo.finish({"d"})
    for y in range(4):
        res[...] += nn(flat(act, y), tall(WD, y))

    g, b = gain(2)
    for i in range(4):
        x = res[IMG * i : IMG * i + IMG, :]
        m = jnp.mean(x, axis=-1, keepdims=True)
        xc = x - m
        r = lax.rsqrt(jnp.mean(xc * xc, axis=-1, keepdims=True) + 1e-05)
        e = r * jnp.sum(xc * (g * query()), axis=-1, keepdims=True)
        lg = (e + jnp.sum(b * query(), axis=-1, keepdims=True)) / ROOT
        lg = jnp.where(mcol[0:IMG, i : i + 1] > 0, lg, -1e30)
        ex = jnp.exp(lg - jnp.max(lg, axis=0, keepdims=True))
        sh = ex / jnp.sum(ex, axis=0, keepdims=True)
        row = jnp.sum((sh * r) * xc, axis=0, keepdims=True)
        s1[i : i + 1, :] = row
        pool[i : i + 1, :] = row * g + b * jnp.sum(sh, axis=0, keepdims=True)
        for n, c in enumerate((m, r, e, sh)):
            cols[i, :, n : n + 1] = c
    todo.finish()
    link.drain()

    def proj_cols(x, lo):
        at = [
            WP.load(core, lo, 32, x=x, y=y, z=z)
            for y in range(4) for core in range(2) for z in range(4)
        ]
        return jnp.concatenate(at, axis=0)

    pooled = pool[...].astype(BF)
    padded = jnp.concatenate(
        [nn(pooled[:, 384 * n : 384 * n + 384], e3[...]).astype(BF) for n in range(2)], axis=1
    )
    embedded = jnp.concatenate([nn(padded, proj_cols(x, 0)) for x in range(4)], axis=1)
    ri = lax.rsqrt(jnp.sum(embedded * embedded, axis=-1, keepdims=True) + 1e-06)
    unit = (embedded * ri).astype(BF)
    big = jnp.exp(jnp.full((1, 1), scale[0], F32))
    dots = nt(unit[:, 0:128], proj_cols(0, 32))
    for x in range(1, 4):
        dots = dots + nt(unit[:, 128 * x : 128 * x + 128], proj_cols(x, 32))
    logits = big * dots
    row = lax.broadcasted_iota(jnp.int32, (8, 1024), 0)
    col = lax.broadcasted_iota(jnp.int32, (8, 1024), 1)
    valid = (row < 4) & ((col & 7) < 4)
    target = jnp.zeros((8, 1024), F32)
    first = 4 * ((me.y * 2 + me.core) * 16 + me.z * 4 + me.x)
    for i in range(4):
        t = pairing[first + i]
        target = jnp.where((row == i) & (col == 8 * (t >> 2) + (t & 3)), 1.0, target)
    e = jnp.where(valid, jnp.exp(logits), 0.0)
    row_sum = jnp.where(row[:, 0:1] < 4, jnp.sum(e, axis=-1, keepdims=True), 1.0)
    col_sum = jnp.sum(e, axis=0, keepdims=True)
    for j in range(8):
        cs[j : j + 1, :] = col_sum[:, 128 * j : 128 * j + 128]
    rows_lse = jnp.sum(jnp.log(row_sum), axis=0, keepdims=True)
    matched = jnp.sum(jnp.sum(logits * target, axis=-1, keepdims=True), axis=0, keepdims=True)
    send_tile = cs[...]
    send_tile = jnp.where((subs == 0) & (lanes == 4), rows_lse, send_tile)
    send_tile = jnp.where((subs == 0) & (lanes == 5), matched, send_tile)
    cs[...] = send_tile
    got = link.group(crx.at[pl.ds(0, 15)])
    for n in range(1, 16):
        t, peer = me.v_peer(n)
        got.copy(cs, crx.at[me.v], peer)
    crx[me.v] = send_tile
    got.wait_recv()
    total = crx[0]
    for n in range(1, 16):
        total = total + crx[n]
    cst[...] = total
    got = link.group(crx2.at[pl.ds(0, 7)])
    for n in range(1, 8):
        t, peer = me.s_peer(n)
        got.copy(cst, crx2.at[s], peer)
    crx2[s] = total
    got.wait_recv()
    total = crx2[0]
    for n in range(1, 8):
        total = total + crx2[n]
    cs_all = jnp.concatenate([total[j : j + 1, :] for j in range(8)], axis=1)
    ok = (lanes & 7) < 4
    cols_lse = jnp.sum(jnp.where(ok, jnp.log(jnp.where(ok, total, 1.0)), 0.0))
    loss = (total[0:1, 4:5] + cols_lse - 2.0 * total[0:1, 5:6]) / 1024.0
    ok = (col[0:1, :] & 7) < 4
    gl = e / row_sum + e / jnp.where(ok, cs_all, 1.0) - 2.0 * target
    gl = jnp.where(valid, gl, 0.0) * (1.0 / 1024.0)
    g_scale = jnp.sum(gl * logits)
    parts = split(gl, 2)
    gui = []
    for x in range(4):
        rhs = proj_cols(x, 32)
        gui.append(nn(parts[0], rhs) + nn(parts[1], rhs))
    gui = big * jnp.concatenate(gui, axis=1)
    ge = ri * gui - ri * ri * ri * embedded * jnp.sum(embedded * gui, axis=-1, keepdims=True)
    ge = ge.astype(BF)
    gp_pad = jnp.concatenate(
        [
            sum(nt(ge[:, 128 * x : 128 * x + 128], proj_cols(x, 0)) for x in range(4))
        ], axis=1
    )
    gp = []
    for n in range(2):
        gp.append(sum(nt(p, e3[...]) for p in split(gp_pad[:, 512 * n : 512 * n + 512], 3)))
    emb[...] = jnp.concatenate(gp, axis=1)
    both = jnp.concatenate([parts[0], parts[1]], axis=0)
    ub = jnp.concatenate([unit, unit], axis=0)
    for x in range(4):
        gproj = tn(padded, ge[:, 128 * x : 128 * x + 128]).astype(BF)
        gtext = (big * tn(both, ub[:, 128 * x : 128 * x + 128])).astype(BF)
        n = 0
        for y in range(4):
            for core in range(2):
                for z in range(4):
                    WP.store(gproj[32 * n : 32 * n + 32, :], core, 0, x=x, y=y, z=z)
                    WP.store(gtext[32 * n : 32 * n + 32, :], core, 32, x=x, y=y, z=z)
                    n += 1

    def keep(n, c):
        def finish(total):
            tot[n, :, 128 * c : 128 * c + 128] = total

        return finish

    def keep_p(total):
        ptot[...] = total

    def rx_part(ref, c, n):
        return ref.at[pl.ds(n * c, n)]

    todo.add("p", scatter_steps(me, link, WP, rxpc, rxp, keep_p, False))
    tick("p", "p")

    def own_rows(n):
        for j in range(8):
            ust[n - 1, j] = tot[n, 6 * j : 6 * j + 6, :]
        group = link.group(orx.at[n - 1, pl.ds(0, 7)])
        for m in range(1, 8):
            t, peer = me.s_peer(m)
            group.copy(ust.at[n - 1, t], orx.at[n - 1, s], peer)
        orx[n - 1, s] = ust[n - 1, s]
        return group

    def own_down():
        group = link.group(tot.at[3, pl.ds(0, 24)])
        group.copy(
            tot.at[0, ds(24 * (1 - odd), 24, 8)],
            tot.at[3, ds(24 * odd, 24, 8)],
            me.dev(x=me.x + 1 - 2 * odd),
        )
        tot[3, ds(24 * odd, 24, 8), :] = tot[0, ds(24 * odd, 24, 8), :]
        return group

    def own_proj():
        for j in range(4):
            pst[j, 0:8] = ptot[8 * j : 8 * j + 8, :]
            pst[j, 8:16] = ptot[32 + 8 * j : 40 + 8 * j, :]
        group = link.group(prx2.at[pl.ds(0, 3)])
        for n in range(1, 4):
            t = (me.x + n) % 4
            group.copy(pst.at[t], prx2.at[me.x], me.dev(x=t))
        prx2[me.x] = pst[me.x]
        return group

    g, b = gain(2)
    side_q = query() / ROOT
    for i in range(4):
        rows = pl.ds(IMG * i, IMG)
        gpi = emb[i : i + 1, :]
        m, r, e, sh = (cols[i, :, n : n + 1] for n in range(4))
        one, two = gpi * g, side_q * g
        xc = res[rows, :] - m
        w = r * jnp.sum(xc * one, axis=-1, keepdims=True)
        c = w + jnp.sum(b * gpi, axis=-1, keepdims=True)
        dl = sh * (c - jnp.sum(sh * c, axis=0, keepdims=True))
        pull = r * r * (sh * w + dl * (e / ROOT)) * (1.0 / D)
        one_c = one - jnp.mean(one, axis=-1, keepdims=True)
        two_c = two - jnp.mean(two, axis=-1, keepdims=True)
        out = (r * sh) * one_c + (r * dl) * two_c - pull * xc
        res[rows, :] = out
        gb[rows, :] = out.astype(BF)
        row = jnp.sum((r * dl) * xc, axis=0, keepdims=True)
        sum_dl = jnp.sum(dl, axis=0, keepdims=True)
        gvec[4, 0:1, :] += gpi * s1[i : i + 1, :] + side_q * row
        gvec[5, 0:1, :] += gpi * jnp.sum(sh, axis=0, keepdims=True) + side_q * sum_dl
        gvec[6, 0:1, :] += (row * g + b * sum_dl) / ROOT
    for y in range(4):
        ga = nt(gb[...], tall(WD, y))
        for l in range(6):
            at = pl.ds(R * (6 * y + l), R)
            gel[at, :] = (ga[:, 128 * l : 128 * l + 128] * gel[at, :].astype(F32)).astype(BF)
        tall_store(WD, y, tn(flat(act, y), gb[...]).astype(BF))
        tick(*(("p",), (), ("p", "p"), ())[y])
    for c in range(3):
        todo.add("d", scatter_steps(me, link, WD[c], rx_part(rxc, c, 3072), rx_part(rxd, c, 3024), keep(0, c), False, give=credit.at[c]))
    tick("d", "d")
    for ch in range(4):
        gu = flat(gel, ch)
        part = nt(gu, wide(WU, ch))
        if ch == 0:
            acc[...] = part
        else:
            acc[...] += part
        wide_store(WU, ch, tn(nrm[...], gu).astype(BF))
        tick(*(("d", "p"), ("p",), ("d", "d"), ("p",))[ch])
        if ch == 3:
            got_proj = own_proj()
    for c in range(3):
        todo.add("u", scatter_steps(me, link, WU[c], rx_part(rxc, c, 3072), rx_part(rxu, c, 3024), keep(1, c), False, give=credit.at[3 + c], need=credit.at[c]))
    tick("u", "u")

    def fold_in(n, gg, gs):
        gvec[n] += gg
        gvec[n + 1] += gs

    g, _ = gain(1)
    for i in range(4):
        rows = pl.ds(IMG * i, IMG)
        y, xh = acc[rows, :], xh2[rows, :].astype(F32)
        out = res[rows, :] + whiten_back(y * g, xh, r2[rows, :])
        res[rows, :] = out
        gb[rows, :] = out.astype(BF)
        fold_in(2, fold(y * xh), fold(y))
    wide_store(GA, 3, tn(att[0:R, :], gb[...]).astype(BF))
    att[0:R, :] = nt(gb[...], wide(WA, 3)).astype(BF)
    norm_one()
    tick("u")
    low = lax.broadcasted_iota(jnp.int32, (256, 128), 0) < IMG
    side = lax.broadcasted_iota(jnp.int32, (256, 128), 1) < 64
    own = [jnp.where(low & side, 1.0, 0.0).astype(BF), jnp.where(low & ~side, 1.0, 0.0).astype(BF)]

    def attend_back(img):
        rows, wide_rows = pl.ds(IMG * img, IMG), pl.ds(IMG * img, 256)

        def pair(pr):
            c = ds(128 * pr, 128)
            q2, k2, v2, do = q[wide_rows, c], k[rows, c], v[rows, c], att[wide_rows, c]
            kt = k2.T
            dqt = []
            dk = jnp.zeros((IMG, 128), F32)
            dv = jnp.zeros((IMG, 128), F32)
            for h in range(2):
                doh, qh = do * own[h], q2 * heads[h]
                p = pb[img % 2, 2 * pr + h]
                dv = dv + nn(p, doh)
                pf = p.astype(F32)
                dp = nt(v2, doh)
                t = pf * dp
                dst = (t - pf * jnp.sum(t, axis=0, keepdims=True)).astype(BF)
                dk = dk + nn(dst, qh)
                dqt.append(nn(kt[64 * h : 64 * h + 64, :], dst))
            dq = (jnp.concatenate(dqt, axis=0) * 0.125).astype(BF).T
            q[rows, c] = dq[0:IMG, :]
            k[rows, c] = dk.astype(BF)
            v[rows, c] = dv.astype(BF)

        for pr in range(6):
            pair(pr)

    loads = {}
    for img in (2, 3, 0, 1):
        if img in loads:
            loads[img].wait()
        attend_back(img)
        if img >= 2:
            c = pltpu.make_async_copy(spill.at[img - 2], pb.at[img - 2], lsem.at[img])
            c.start()
            loads[img - 2] = c
        tick(*(("d",), ("u",), ("d",), ("u", "u"))[img])
    for ch, src in enumerate((q, k, v)):
        wide_store(GA, ch, tn(nrm[...], src[0:R, :]).astype(BF))
        if ch == 0:
            tick("d")
            got_down = own_down()
    for c in range(3):
        todo.add("a", scatter_steps(me, link, GA[c], rx_part(rxc, c, 3072), rx_part(rxa, c, 3024), keep(2, c), True, need=credit.at[3 + c]))
    tick("a", "a", "u")
    for ch, src in enumerate((q, k, v)):
        part = nt(src[0:R, :], wide(WA, ch))
        if ch == 0:
            acc[...] = part
        else:
            acc[...] += part
        if ch == 1:
            tick("a")
        if ch == 2:
            tick("u")
            got_up = own_rows(1)
    g, _ = gain(0)
    outs = []
    for i in range(4):
        rows = pl.ds(IMG * i, IMG)
        xh, r = whiten(tok[rows, :].astype(F32))
        y = acc[rows, :]
        out = res[rows, :] + whiten_back(y * g, xh, r)
        fold_in(0, fold(y * xh), fold(y))
        acc[196 * i : 196 * i + 196, :] = out[0:196, :]
        if i % 2 == 1:
            rows = pl.ds(392 * (i // 2), 392)
            outs.append(pltpu.make_async_copy(acc.at[rows], o_tok.at[rows], lsem.at[4 + i // 2]))
            outs[-1].start()
    tick("a")

    for n in range(7):
        vec[n : n + 1, :] = jnp.sum(gvec[n], axis=0, keepdims=True)
    vec[7:8, :] = jnp.zeros((1, D), F32)
    for n in range(16):
        t, off = 48 * n // 128, 48 * n % 128
        part = vec[:, 128 * t : 128 * t + 128]
        part = pltpu.roll(part, (128 - off) % 128, 1) if off else part
        if off > 80:
            more = pltpu.roll(vec[:, 128 * t + 128 : 128 * t + 256], 128 - off, 1)
            part = jnp.where(lanes < 128 - off, part, more)
        gst2[n] = jnp.where(subs == 7, g_scale, part)
    cv = link.group(grx.at[pl.ds(0, 15)])
    for n in range(1, 16):
        t, peer = me.v_peer(n)
        cv.copy(gst2.at[t], grx.at[me.v], peer)
    grx[me.v] = gst2[me.v]

    tick("a", "a")
    cv.wait_recv()
    total = grx[0]
    for n in range(1, 16):
        total = total + grx[n]
    vst[...] = total
    got_vec = link.group(grx2.at[pl.ds(0, 7)])
    for n in range(1, 8):
        t, peer = me.s_peer(n)
        got_vec.copy(vst, grx2.at[s], peer)
    grx2[s] = total
    todo.finish({"a"})
    last = own_rows(2)
    got_vec.wait_recv()
    total = grx2[0]
    for n in range(1, 8):
        total = total + grx2[n]
    total = pltpu.roll(total, (128 - 6 * s) % 128, 1)
    o_small[...] = jnp.where((subs == 7) & (lanes == 1), loss, total)
    got_up.wait_recv()
    got_down.wait_recv()
    for j in range(8):
        o_up[:, 384 * j : 384 * j + 384] = orx[0, j]
    for j in range(2):
        o_down[:, 384 * j : 384 * j + 384] = tot[3, 24 * j : 24 * j + 24, :]
    got_proj.wait_recv()
    for j in range(4):
        o_proj[:, 128 * j : 128 * j + 128] = prx2[j, 0:6]
    gt = jnp.concatenate([prx2[j, 8:12] for j in range(4)], axis=1)
    txt = text[...]
    r = lax.rsqrt(jnp.sum(txt * txt, axis=-1, keepdims=True) + 1e-06)
    o_text[...] = r * gt - r * r * r * txt * jnp.sum(txt * gt, axis=-1, keepdims=True)
    last.wait_recv()
    for j in range(8):
        if j < 6:
            o_qkv[:, 384 * j : 384 * j + 384] = orx[1, j]
        else:
            o_out[:, 384 * (j - 6) : 384 * (j - 6) + 384] = orx[1, j]
    for c in outs:
        c.wait()
    link.drain()


def hand_over(*refs):
    src, small, dst, tiny, bufs, sem = refs[:7], refs[7], refs[8:15], refs[15:24], refs[24:31], refs[31]
    parts = [(src[0].at[r], bufs[0].at[r], dst[0].at[r]) for r in (pl.ds(104 * n, 104 if n < 7 else 56) for n in range(8))]
    parts += list(zip(src[1:], bufs[1:], dst[1:]))
    there = [pltpu.make_async_copy(a, b, sem.at[0, n]) for n, (a, b, _) in enumerate(parts)]
    back = [pltpu.make_async_copy(b, c, sem.at[1, n]) for n, (_, b, c) in enumerate(parts)]
    for c in there:
        c.start()
    for n, ref in enumerate(tiny):
        for e in range(ref.shape[0]):
            ref[e] = small[n, e] if n < 7 else small[7, n - 7]
    for a, b in zip(there, back):
        a.wait()
        b.start()
    for c in back:
        c.wait()


def shards(tokens, keep_mask, pairing, text_vectors, logit_scale, w_qkv, w_out, w_up, w_down, w_proj, *vectors):
    vm = pl.BlockSpec(memory_space=pltpu.VMEM)
    sm = pl.BlockSpec(memory_space=pltpu.SMEM)
    hbm = pl.BlockSpec(memory_space=pl.ANY)
    S = jax.ShapeDtypeStruct
    V = pltpu.VMEM
    outs = pl.pallas_call(
        kernel,
        out_shape=[
            S((784, D), F32), S((4, 512), F32), S((6, 2304), F32), S((6, 768), F32), S((6, 3072), F32),
            S((24, 768), F32), S((6, 512), F32), S((8, 128), F32),
            S((2, 12, IMG, 256), BF),
        ],
        in_specs=[sm] * 9 + [hbm] + [vm] * 7,
        out_specs=[hbm, vm, vm, vm, vm, vm, vm, vm, hbm],
        scratch_shapes=[
            V((18432, 128), BF), V((18432, 128), BF), V((18432, 128), BF), V((8192, 128), BF), V((R, D), BF),
            V((R + 48, D), BF), V((R, D), BF), V((R, D), BF), V((2, 12, IMG, 256), BF),
            V((R, D), BF), V((R, D), BF), V((R + 48, D), BF), V((R, D), BF),
            V((24 * R, 128), BF), V((24 * R, 128), BF), V((R, D), F32), V((R, D), F32), V((R, 1), F32),
            V((3 * 3072, 128), BF), V((3 * 3024, 128), BF), V((3 * 3024, 128), BF), V((3 * 3024, 128), BF),
            V((4096, 128), BF), V((4032, 128), BF),
            V((6, 3072), F32), V((8, 6, 384), F32), V((8, 6, 384), F32), V((2, 24, 384), F32),
            V((16, 512), F32), V((4, 16, 128), F32), V((8, 8, 128), F32), V((8, 128), F32),
            V((48, 384), F32), V((64, 128), F32), V((8, D), F32), V((7, 8, D), F32),
            V((8, 256), F32), V((256, 8), F32), V((4, IMG, 8), F32), V((4, IMG, 128), F32),
            V((8, D), F32), V((8, D), F32), V((384, 512), BF), V((8, D), F32),
            V((8, 128), F32), V((16, 8, 128), F32), V((8, 128), F32), V((8, 8, 128), F32),
            V((4, 48, 384), F32), V((64, 128), F32), V((2, 8, 6, 384), F32), V((2, 8, 6, 384), F32),
            V((4, 16, 128), F32), V((4, 16, 128), F32), V((16, 8, 128), F32), V((16, 8, 128), F32),
            V((16, 8, 128), F32), V((8, 8, 128), F32),
            pltpu.SemaphoreType.DMA((N_SEM,)), pltpu.SemaphoreType.DMA((N_SEM,)), pltpu.SemaphoreType.DMA((8,)),
            pltpu.SemaphoreType.REGULAR((6,)),
        ],
        compiler_params=pltpu.CompilerParams(
            collective_id=0, has_side_effects=True, vmem_limit_bytes=(64 << 20) - (256 << 10)
        ),
        cost_estimate=pl.CostEstimate(flops=40_000_000_000, bytes_accessed=20_000_000, transcendentals=0),
    )(pairing, logit_scale, *vectors, tokens, keep_mask, text_vectors, w_qkv, w_out, w_up, w_down, w_proj)
    outs = outs[:8]
    tiny = [S((6,), F32)] * 7 + [S((1,), F32)] * 2
    got = pl.pallas_call(
        hand_over,
        out_shape=[S(o.shape, F32) for o in outs[:7]] + tiny,
        in_specs=[hbm] * 7 + [sm],
        out_specs=[hbm] * 7 + [sm] * 9,
        scratch_shapes=[V(o.shape, F32) for o in outs[:7]] + [pltpu.SemaphoreType.DMA((2, 14))],
    )(*outs)
    return (got[15], *got[:14], got[14])


def solution(mesh):
    rows, vector, whole = P(("dp", "fsdp"), None), P(("dp", "fsdp")), P()
    in_specs = (rows, rows, whole, rows, whole, *[rows] * 5, *[vector] * 7)
    out_specs = (whole, rows, rows, *[rows] * 5, *[vector] * 7, whole)
    return jax.shard_map(shards, mesh=mesh, in_specs=in_specs, out_specs=out_specs, check_vma=False)
```
